32 devices in a mesh: dp: 8 (over y, x, core), tensor: 4 (over z).
Axes of the slice: x: 2, y: 2, z: 4, core: 2. Of those that a mesh axis runs over, the one named last changes fastest.
Arguments:
- block_in: float32 [8192, 1536], P(('dp', 'tensor')), may hold values from -6 to 6
- out_grad: float32 [8192, 1536], P(('dp', 'tensor')), may hold values from -6 to 6
- positions: int32 [8192], P('dp'), may hold values from 0 to 4096, as said below
- qkv_weight: float32 [1536, 2560], P('dp', 'tensor'), may hold values from -0.15625 to 0.15625
- qkv_first: float32 [1536, 2560], P('dp', 'tensor'), may hold values from -96 to 96
- qkv_second: float32 [1536, 2560], P('dp', 'tensor'), may hold values from 18.432 to 73.728
- out_weight: float32 [1536, 1536], P('tensor', 'dp'), may hold values from -0.875 to 0.875
- out_first: float32 [1536, 1536], P('tensor', 'dp'), may hold values from -8 to 8
- out_second: float32 [1536, 1536], P('tensor', 'dp'), may hold values from 0.18432 to 0.73728
- gate_up: float32 [2, 1536, 6912], P(None, 'dp', 'tensor'), may hold values from -0.15625 to 0.15625
- gate_up_first: float32 [2, 1536, 6912], P(None, 'dp', 'tensor'), may hold values from -16 to 16
- gate_up_second: float32 [2, 1536, 6912], P(None, 'dp', 'tensor'), may hold values from 0.73728 to 2.94912
- down_weight: float32 [6912, 1536], P('tensor', 'dp'), may hold values from -0.078125 to 0.078125
- down_first: float32 [6912, 1536], P('tensor', 'dp'), may hold values from -32 to 32
- down_second: float32 [6912, 1536], P('tensor', 'dp'), may hold values from 2.94912 to 11.79648
- norm_gains: float32 [3200], P(('dp', 'tensor')), may hold values from 0.5 to 1.5
- norm_gains_first: float32 [3200], P(('dp', 'tensor')), may hold values from -128 to 128
- norm_gains_second: float32 [3200], P(('dp', 'tensor')), may hold values from 32.768 to 131.072
Outputs:
- block_out: float32 [8192, 1536], P(('dp', 'tensor'))
- in_grad: float32 [8192, 1536], P(('dp', 'tensor'))
- qkv_weight_new: float32 [1536, 2560], P('dp', 'tensor')
- qkv_first_new: float32 [1536, 2560], P('dp', 'tensor')
- qkv_second_new: float32 [1536, 2560], P('dp', 'tensor')
- out_weight_new: float32 [1536, 1536], P('tensor', 'dp')
- out_first_new: float32 [1536, 1536], P('tensor', 'dp')
- out_second_new: float32 [1536, 1536], P('tensor', 'dp')
- gate_up_new: float32 [2, 1536, 6912], P(None, 'dp', 'tensor')
- gate_up_first_new: float32 [2, 1536, 6912], P(None, 'dp', 'tensor')
- gate_up_second_new: float32 [2, 1536, 6912], P(None, 'dp', 'tensor')
- down_weight_new: float32 [6912, 1536], P('tensor', 'dp')
- down_first_new: float32 [6912, 1536], P('tensor', 'dp')
- down_second_new: float32 [6912, 1536], P('tensor', 'dp')
- norm_gains_new: float32 [3200], P(('dp', 'tensor'))
- norm_gains_first_new: float32 [3200], P(('dp', 'tensor'))
- norm_gains_second_new: float32 [3200], P(('dp', 'tensor'))
The draws below stay inside these ranges and needn't reach their ends.
Inputs may be any that keep to these rules, and one draw needn't show every extreme that they name: Within each sequence of 1024 tokens the positions rise by one inside a document and restart at 0 where a new document begins; the first document of a sequence may begin at a larger position.
All inputs are finite; a program needn't handle non-finite values.
Results may differ from the reference program's by a relative error of at most 0.023.
Values may be sent and summed in bfloat16 or wider, within the bound.
No kernel may reach another device: no remote copies, remote signals or barrier semaphores. Data moves between devices by JAX's collectives and lax.ppermute only.
A program may use at most 256 MiB of HBM per device.

```python
import math
import jax
import jax.numpy as jnp
from jax import lax

D = 1536
HQ = 24
KEY_VALUE_HEADS = 8
HEAD_DIMENSION = 64
FF = 6912
SEQ = 1024
STEP = 10
QUERY_GROUP = 3
QKVW = 2560
GAINS = 3200
TOKENS = 8192


def draw_positions(key, part):
    key = jax.random.fold_in(key, 11)
    key_first, key_second, key_offset, key_pick = jax.random.split(key, 4)
    seq_count = TOKENS // SEQ
    first_end = jax.random.randint(key_first, (seq_count, 1), 1, SEQ // 8 + 1)
    second_end = jax.random.randint(key_second, (seq_count, 1), SEQ - SEQ // 8, SEQ)
    offset = jax.random.randint(key_offset, (seq_count, 1), 0, 4 * SEQ - SEQ // 8 + 1)
    picked = jax.random.randint(key_pick, (), 0, seq_count)
    is_picked = (jnp.arange(seq_count, dtype=jnp.int32) == picked)[:, None]
    first_end = jnp.where(is_picked, SEQ // 8, first_end)
    offset = jnp.where(is_picked, 4 * SEQ - SEQ // 8 + 1, offset)
    places = jnp.arange(SEQ, dtype=jnp.int32)[None, :]
    result = jnp.where(places < first_end, places + offset, jnp.where(places < second_end, places - first_end, places - second_end))
    return result.reshape(-1).astype(jnp.int32)


def shard_levels(stream_key, extent, pieces, least, top_value):
    def one(dim, parts):
        heights = jax.random.uniform(jax.random.fold_in(jax.random.fold_in(stream_key, 6), dim), (parts,), jnp.float32, least / len(pieces), top_value / len(pieces))
        return jnp.repeat(jnp.exp(heights), extent[dim] // parts).reshape((-1,) + (1,) * (len(extent) - dim - 1))

    factor_of = one(*pieces[0])
    for cut in pieces[1:]:
        factor_of = factor_of * one(*cut)
    return factor_of


def normal_values(rng, dims, spread, most, cuts=(), kind=jnp.bfloat16):
    factor_of = shard_levels(rng, dims, cuts, -0.22, 0.18) if cuts else 1.0
    values = jax.random.normal(rng, dims, jnp.float32) * spread * factor_of
    return jnp.minimum(jnp.maximum(values, -most), most).astype(kind)


def setup_inputs(seed: int = 0) -> dict:
    key_list = jax.random.split(jax.random.key(seed), 19)
    return {
        "block_in": normal_values(key_list[0], (TOKENS, D), 1.0, 6.0, ((0, 32),), jnp.float32),
        "out_grad": normal_values(key_list[1], (TOKENS, D), 1.0, 6.0, ((0, 32),), jnp.float32),
        "positions": draw_positions(jax.random.fold_in(key_list[18], 71), 0),
        "qkv_weight": normal_values(key_list[3], (D, QKVW), D ** -0.5, 0.15625, ((0, 8), (1, 4)), jnp.float32),
        "qkv_first": normal_values(key_list[4], (D, QKVW), (0.17 * TOKENS ** 0.5), 96.0, ((0, 8), (1, 4)), jnp.float32),
        "qkv_second": jnp.clip(jnp.exp(math.log(73.728) - 1.3862944 * jax.random.uniform(key_list[5], (D, QKVW), jnp.float32) ** shard_levels(key_list[5], (D, QKVW), ((0, 8), (1, 4)), -0.2, 0.2)), 18.432, 73.728),
        "out_weight": normal_values(key_list[6], (HQ * HEAD_DIMENSION, D), (HQ * HEAD_DIMENSION // 32) ** -0.5, 0.875, ((0, 4), (1, 8)), jnp.float32),
        "out_first": normal_values(key_list[7], (HQ * HEAD_DIMENSION, D), (0.0165 * TOKENS ** 0.5), 8.0, ((0, 4), (1, 8)), jnp.float32),
        "out_second": jnp.clip(jnp.exp(math.log(0.73728) - 1.3862944 * jax.random.uniform(key_list[8], (HQ * HEAD_DIMENSION, D), jnp.float32) ** shard_levels(key_list[8], (HQ * HEAD_DIMENSION, D), ((0, 4), (1, 8)), -0.2, 0.2)), 0.18432, 0.73728),
        "gate_up": normal_values(key_list[9], (2, D, FF), D ** -0.5, 0.15625, ((1, 8), (2, 4)), jnp.float32),
        "gate_up_first": normal_values(key_list[10], (2, D, FF), (0.033 * TOKENS ** 0.5), 16.0, ((1, 8), (2, 4)), jnp.float32),
        "gate_up_second": jnp.clip(jnp.exp(math.log(2.94912) - 1.3862944 * jax.random.uniform(key_list[11], (2, D, FF), jnp.float32) ** shard_levels(key_list[11], (2, D, FF), ((1, 8), (2, 4)), -0.2, 0.2)), 0.73728, 2.94912),
        "down_weight": normal_values(key_list[12], (FF, D), FF ** -0.5, 0.078125, ((0, 4), (1, 8)), jnp.float32),
        "down_first": normal_values(key_list[13], (FF, D), (0.066 * TOKENS ** 0.5), 32.0, ((0, 4), (1, 8)), jnp.float32),
        "down_second": jnp.clip(jnp.exp(math.log(11.79648) - 1.3862944 * jax.random.uniform(key_list[14], (FF, D), jnp.float32) ** shard_levels(key_list[14], (FF, D), ((0, 4), (1, 8)), -0.2, 0.2)), 2.94912, 11.79648),
        "norm_gains": jnp.clip(1.0 + 0.1 * jax.random.normal(key_list[15], (GAINS,), jnp.float32), 0.5, 1.5),
        "norm_gains_first": normal_values(key_list[16], (GAINS,), (0.22 * TOKENS ** 0.5), 128.0, ((0, 32),), jnp.float32),
        "norm_gains_second": jnp.clip(jnp.exp(math.log(131.072) - 1.3862944 * jax.random.uniform(key_list[17], (GAINS,), jnp.float32) ** shard_levels(key_list[17], (GAINS,), ((0, 32),), -0.2, 0.2)), 32.768, 131.072),
    }


eps_norm = 1e-05
rope_base = 1000000.0
beta_one = 0.9
beta_two = 0.999
adam_eps = 1e-08
decay_matrix = 0.1
rate_matrix = 0.03
rate_output = 0.15
rate_gains = 0.8
highest = lax.Precision.HIGHEST

@jax.custom_vjp
def low(v):
    return lax.optimization_barrier(v.astype(jnp.bfloat16)).astype(jnp.float32)

@jax.custom_vjp
def low_back(v):
    return v

def low_keep(v):
    return (low(v), None)

def low_pass(kept, grad):
    return (grad,)

def back_keep(v):
    return (v, None)

def back_low(kept, grad):
    return (low(grad),)
low.defvjp(low_keep, low_pass)
low_back.defvjp(back_keep, back_low)

def matmul(left, right):
    return jnp.dot(left, right, precision=highest, preferred_element_type=jnp.float32)

def norm_rows(row_block, gain_vec):
    inverse = lax.rsqrt(lax.optimization_barrier(jnp.mean(row_block * row_block, axis=-1, keepdims=True)) + eps_norm)
    return row_block * inverse * gain_vec

def rope_angles(positions, head_size):
    inverse_freq = rope_base ** (-(jnp.arange(head_size // 2, dtype=jnp.float32) * 2.0) / head_size)
    return positions.astype(jnp.float32)[:, None] * inverse_freq[None, :]

def rotate(vectors, angles):
    half_size = vectors.shape[-1] // 2
    first_half = vectors[..., :half_size]
    second_half = vectors[..., half_size:]
    cos_part = jnp.cos(angles)
    sin_part = jnp.sin(angles)
    return jnp.concatenate([first_half * cos_part - second_half * sin_part, second_half * cos_part + first_half * sin_part], axis=-1)

def document_ids(positions):
    previous = jnp.concatenate([positions[:1] - 2, positions[:-1]])
    starts = (positions != previous + 1).astype(jnp.int32)
    return jnp.cumsum(starts).astype(jnp.int32)

def prepare(projected, gain_q, gain_k, angles):
    length = projected.shape[0]
    grouped_heads = projected.reshape(length, -1, QUERY_GROUP + 2, HEAD_DIMENSION)
    query_rows = grouped_heads[:, :, :QUERY_GROUP, :]
    key_heads = grouped_heads[:, :, QUERY_GROUP, :]
    value_heads = grouped_heads[:, :, QUERY_GROUP + 1, :]
    query_rows = rotate(norm_rows(query_rows, gain_q), angles[:, None, None, :])
    key_heads = rotate(norm_rows(key_heads, gain_k), angles[:, None, :])
    return (query_rows, key_heads, value_heads)

def attention(query_rows, key_heads, value_heads, doc_ids):
    length = query_rows.shape[0]
    block_length = min(512, length)
    count_of_blocks = length // block_length
    score_scale = HEAD_DIMENSION ** (-0.5)
    grouped_heads = query_rows.reshape(count_of_blocks, block_length, KEY_VALUE_HEADS, QUERY_GROUP, HEAD_DIMENSION)
    first_rows = jnp.arange(count_of_blocks, dtype=jnp.int32) * block_length
    key_pos = jnp.arange(length, dtype=jnp.int32)

    def one_block(inputs):
        query_blk, first_row = inputs
        row_pos = first_row + jnp.arange(block_length, dtype=jnp.int32)
        row_docs = lax.dynamic_slice_in_dim(doc_ids, first_row, block_length)
        allowed = (row_docs[:, None] == doc_ids[None, :]) & (key_pos[None, :] <= row_pos[:, None])
        scores = low_back(jnp.einsum('bkgd,skd->kgbs', query_blk, key_heads, precision=highest) * score_scale)
        scores = jnp.where(allowed[None, None], scores, -1e+30)
        row_max = lax.optimization_barrier(jnp.max(scores, axis=-1, keepdims=True))
        weights = jnp.exp(scores - row_max)
        probs_low = low(weights / lax.optimization_barrier(jnp.sum(weights, axis=-1, keepdims=True)))
        return jnp.einsum('kgbs,skd->bkgd', probs_low, value_heads, precision=highest)
    outputs = lax.map(jax.checkpoint(one_block), (grouped_heads, first_rows))
    return outputs.reshape(length, HQ * HEAD_DIMENSION)

def layer(rows_in, qkv_w, out_w, gate_up_w, down_w, gains_w, positions):
    model_width = rows_in.shape[1]
    gain_attn = gains_w[:model_width]
    gain_q = gains_w[model_width:model_width + HEAD_DIMENSION]
    gain_k = gains_w[model_width + HEAD_DIMENSION:model_width + 2 * HEAD_DIMENSION]
    gain_ffn = gains_w[model_width + 2 * HEAD_DIMENSION:]
    normed = low(norm_rows(rows_in, gain_attn))
    projected = low_back(matmul(normed, low(qkv_w)))
    angles = rope_angles(positions, HEAD_DIMENSION)
    query_rows, key_heads, value_heads = prepare(projected, gain_q, gain_k, angles)
    attended = attention(low(query_rows), low(key_heads), low(value_heads), document_ids(positions))
    attended = low(low_back(attended))
    middle = rows_in + low_back(matmul(attended, low(out_w)))
    normed_two = low(norm_rows(middle, gain_ffn))
    gate_out = low_back(matmul(normed_two, low(gate_up_w[0])))
    up_out = low_back(matmul(normed_two, low(gate_up_w[1])))
    hidden = low(jax.nn.silu(gate_out) * up_out)
    return middle + low_back(matmul(hidden, low(down_w)))

def adam_step(weight, first_old, second_old, gradient, step_rate, decay_rate):
    first_new = beta_one * first_old + (1.0 - beta_one) * gradient
    second_new = beta_two * second_old + (1.0 - beta_two) * gradient * gradient
    fix_one = 1.0 - beta_one ** STEP
    fix_two = 1.0 - beta_two ** STEP
    update = first_new / fix_one / (jnp.sqrt(second_new / fix_two) + adam_eps)
    return (weight - step_rate * (update + decay_rate * weight), first_new, second_new)

def reference(block_in, out_grad, positions, qkv_weight, qkv_first, qkv_second, out_weight, out_first, out_second, gate_up, gate_up_first, gate_up_second, down_weight, down_first, down_second, norm_gains, norm_gains_first, norm_gains_second):
    seq_count = block_in.shape[0] // SEQ
    seq_rows = block_in.reshape(seq_count, SEQ, D)
    seq_grads = out_grad.reshape(seq_count, SEQ, D)
    seq_pos = positions.reshape(seq_count, SEQ)
    params = (qkv_weight, out_weight, gate_up, down_weight, norm_gains)
    zero_grads = jax.tree.map(jnp.zeros_like, params)

    def seq_step(running, inputs):
        rows_now, grad_now, pos_now = inputs

        def apply_layer(rows_arg, qkv_arg, out_arg, gate_arg, down_arg, gains_arg):
            return layer(rows_arg, qkv_arg, out_arg, gate_arg, down_arg, gains_arg, pos_now)
        result, pull_back = jax.vjp(apply_layer, rows_now, *params)
        grad_list = pull_back(grad_now)
        running = jax.tree.map(jnp.add, running, tuple(grad_list[1:]))
        return (running, (result, grad_list[0]))
    totals, (results, in_grads) = lax.scan(seq_step, zero_grads, (seq_rows, seq_grads, seq_pos))
    grad_qkv, grad_out, grad_gate_up, grad_down, grad_gains = totals
    qkv_new = adam_step(qkv_weight, qkv_first, qkv_second, grad_qkv, rate_matrix, decay_matrix)
    out_new = adam_step(out_weight, out_first, out_second, grad_out, rate_output, decay_matrix)
    gate_up_new = adam_step(gate_up, gate_up_first, gate_up_second, grad_gate_up, rate_matrix, decay_matrix)
    down_new = adam_step(down_weight, down_first, down_second, grad_down, rate_matrix, decay_matrix)
    gains_new = adam_step(norm_gains, norm_gains_first, norm_gains_second, grad_gains, rate_gains, 0.0)
    return (results.reshape(-1, D), in_grads.reshape(-1, D), qkv_new[0], qkv_new[1], qkv_new[2], out_new[0], out_new[1], out_new[2], gate_up_new[0], gate_up_new[1], gate_up_new[2], down_new[0], down_new[1], down_new[2], gains_new[0], gains_new[1], gains_new[2])
```

```python
import functools

import jax
import jax.numpy as jnp
from jax import lax
from jax.experimental import pallas as pl
from jax.experimental.pallas import tpu as pltpu
from jax.sharding import PartitionSpec as P

HEAD_DIMENSION = 64
STEP = 10
QUERY_GROUP = 3
AXES = ("dp", "tensor")

eps_norm = 1e-05
rope_base = 1000000.0
beta_one = 0.9
beta_two = 0.999
adam_eps = 1e-08
decay_matrix = 0.1
rate_matrix = 0.03
rate_output = 0.15
rate_gains = 0.8
bf16 = jnp.bfloat16
f32 = jnp.float32
VMEM_LIMIT = 48 * 1024 * 1024
SMALL = pl.CostEstimate(flops=1000, bytes_accessed=1000, transcendentals=0)


def dot(left, right, left_dim, right_dim):
    return lax.dot_general(
        left, right, (((left_dim,), (right_dim,)), ((), ())), preferred_element_type=f32
    )


def norm_rows(row_block, gain_vec):
    inverse = lax.rsqrt(jnp.mean(row_block * row_block, axis=-1, keepdims=True) + eps_norm)
    return row_block * inverse * gain_vec


def rope_tables(positions, head_size):
    inverse_freq = rope_base ** (-(jnp.arange(head_size // 2, dtype=f32) * 2.0) / head_size)
    angles = positions.astype(f32)[:, None] * inverse_freq[None, :]
    cos_part, sin_part = jnp.cos(angles), jnp.sin(angles)
    return (
        jnp.concatenate([cos_part, cos_part], axis=1),
        jnp.concatenate([-sin_part, sin_part], axis=1),
    )


def adam_step(weight, first_old, second_old, gradient, step_rate, decay_rate):
    first_new = beta_one * first_old + (1.0 - beta_one) * gradient
    second_new = beta_two * second_old + (1.0 - beta_two) * gradient * gradient
    fix_one = 1.0 - beta_one**STEP
    fix_two = 1.0 - beta_two**STEP
    update = first_new / fix_one / (jnp.sqrt(second_new / fix_two) + adam_eps)
    return (weight - step_rate * (update + decay_rate * weight), first_new, second_new)


def swap_halves(value):
    half = value.shape[1] // 2
    return jnp.concatenate([value[:, half:], value[:, :half]], axis=1)


def as_row(column):
    return jnp.broadcast_to(column, (column.shape[0], 128)).T[:1, :]


def place_parts(place_ref, part_refs, whole_ref, scale):
    rows = part_refs[0].shape[0]
    for j, part_ref in enumerate(part_refs):
        at_row = pl.multiple_of((j ^ place_ref[0]) * rows, rows)
        value = part_ref[...]
        if scale is not None:
            value = (value.astype(f32) * scale).astype(bf16)
        whole_ref[pl.ds(at_row, rows), :] = value


def attention_forward_kernel(
    place_ref,
    part_0,
    part_1,
    part_2,
    part_3,
    gain_ref,
    head_gain_ref,
    weight_ref,
    cos_ref,
    sin_ref,
    start_ref,
    normed_ref,
    projected_ref,
    q_ref,
    k_ref,
    v_ref,
    out_ref,
    lse_ref,
):
    size = HEAD_DIMENSION
    heads, length, _ = q_ref.shape
    group = QUERY_GROUP
    kv = heads // group
    block = min(256, length)
    place_parts(place_ref, (part_0, part_1, part_2, part_3), normed_ref, gain_ref[...])
    for i in range(length // block):
        here = pl.ds(i * block, block)
        projected = dot(normed_ref[here, :], weight_ref[:, : projected_ref.shape[1]], 1, 0)
        projected_ref[here, :] = projected
        cos_part, sin_part = cos_ref[here, :], sin_ref[here, :]
        for j in range(kv):
            for g in range(group + 2):
                column = (j * (group + 2) + g) * size
                raw = projected[:, column : column + size]
                if g == group + 1:
                    v_ref[j, here, :] = raw.astype(bf16)
                    continue
                inverse = lax.rsqrt(jnp.mean(raw * raw, axis=1, keepdims=True) + eps_norm)
                gain = head_gain_ref[:1, :] if g < group else head_gain_ref[1:, :]
                normed = raw * inverse * gain
                turned = (normed * cos_part + swap_halves(normed) * sin_part).astype(bf16)
                if g < group:
                    q_ref[j * group + g, here, :] = turned * jnp.asarray(size**-0.5, bf16)
                else:
                    k_ref[j, here, :] = turned
    row_at = lax.broadcasted_iota(jnp.int32, (block, block), 0)
    col_at = lax.broadcasted_iota(jnp.int32, (block, block), 1)
    causal = jnp.concatenate([col_at <= row_at] * group, axis=0)
    col_all = lax.broadcasted_iota(jnp.int32, (group * block, block), 1)
    ones = jnp.ones((block, size), bf16)
    for j in range(kv):
        for i in range(length // block):
            here = pl.ds(i * block, block)
            queries = jnp.concatenate(
                [q_ref[j * group + g, here, :] for g in range(group)], axis=0
            )
            start = jnp.concatenate([start_ref[here, :]] * group, axis=0)
            total = jnp.zeros((group * block, 2 * size), f32)
            for b in range(i + 1):
                there = pl.ds(b * block, block)
                scores = dot(queries, k_ref[j, there, :], 1, 1)
                allowed = col_all >= start - b * block
                if b == i:
                    allowed = allowed & causal
                weights = jnp.where(allowed, jnp.exp(scores), 0.0).astype(bf16)
                values = jnp.concatenate([v_ref[j, there, :], ones], axis=1)
                total = total + dot(weights, values, 1, 0)
            row_sum = total[:, size : size + 1]
            output = (total[:, :size] / row_sum).astype(bf16)
            log_sum = jnp.log(row_sum)
            for g in range(group):
                h = j * group + g
                part = slice(g * block, (g + 1) * block)
                out_ref[here, h * size : (h + 1) * size] = output[part]
                lse_ref[h, :, here] = as_row(log_sum[part])


def attention_forward(place, parts, gain_attn, head_gains, weight, tables, start):
    rows, width = parts[0].shape
    length = 4 * rows
    size = HEAD_DIMENSION
    kv = weight.shape[1] // ((2 * QUERY_GROUP + 2) * size)
    heads = kv * QUERY_GROUP
    vmem = pl.BlockSpec(memory_space=pltpu.VMEM)
    return pl.pallas_call(
        attention_forward_kernel,
        in_specs=[pl.BlockSpec(memory_space=pltpu.SMEM)] + [vmem] * 10,
        out_specs=(vmem,) * 7,
        out_shape=(
            jax.ShapeDtypeStruct((length, width), bf16),
            jax.ShapeDtypeStruct((length, (heads + 2 * kv) * size), f32),
            jax.ShapeDtypeStruct((heads, length, size), bf16),
            jax.ShapeDtypeStruct((kv, length, size), bf16),
            jax.ShapeDtypeStruct((kv, length, size), bf16),
            jax.ShapeDtypeStruct((length, heads * size), bf16),
            jax.ShapeDtypeStruct((heads, 1, length), f32),
        ),
        compiler_params=pltpu.CompilerParams(vmem_limit_bytes=VMEM_LIMIT),
        cost_estimate=SMALL,
    )(place, *parts, gain_attn, head_gains, weight, *tables, start)


def attention_turn_kernel(
    place_ref, part_0, part_1, part_2, part_3, weight_ref, out_ref, grads_ref, dot_ref, dw_ref, whole_ref
):
    size = HEAD_DIMENSION
    place_parts(place_ref, (part_0, part_1, part_2, part_3), whole_ref, None)
    heads, length, _ = grads_ref.shape
    block = min(256, length)
    for i in range(length // block):
        here = pl.ds(i * block, block)
        grads = dot(whole_ref[here, :], weight_ref[...], 1, 0).astype(bf16)
        products = grads.astype(f32) * out_ref[here, :].astype(f32)
        for h in range(heads):
            columns = slice(h * size, (h + 1) * size)
            grads_ref[h, here, :] = grads[:, columns]
            dot_ref[h, :, here] = as_row(jnp.sum(products[:, columns], axis=1, keepdims=True))
    dw_ref[...] = dot(whole_ref[...], out_ref[...], 0, 0).astype(bf16)


def attention_turn(place, parts, weight, attended):
    rows, width = parts[0].shape
    length, columns = attended.shape
    heads = columns // HEAD_DIMENSION
    vmem = pl.BlockSpec(memory_space=pltpu.VMEM)
    return pl.pallas_call(
        attention_turn_kernel,
        in_specs=[pl.BlockSpec(memory_space=pltpu.SMEM)] + [vmem] * 6,
        out_specs=(vmem,) * 3,
        out_shape=(
            jax.ShapeDtypeStruct((heads, length, HEAD_DIMENSION), bf16),
            jax.ShapeDtypeStruct((heads, 1, length), f32),
            jax.ShapeDtypeStruct((width, columns), bf16),
        ),
        scratch_shapes=[pltpu.VMEM((length, width), bf16)],
        compiler_params=pltpu.CompilerParams(vmem_limit_bytes=VMEM_LIMIT),
        cost_estimate=SMALL,
    )(place, *parts, weight, attended)


def attention_backward_kernel(
    q_ref,
    k_ref,
    v_ref,
    g_ref,
    lse_ref,
    dot_ref,
    start_ref,
    projected_ref,
    head_gain_ref,
    cos_ref,
    sin_ref,
    weight_ref,
    normed_ref,
    gain_ref,
    back_ref,
    part_ref,
    head_sum_ref,
    gain_sum_ref,
    dq_ref,
    dk_ref,
    dv_ref,
):
    size = HEAD_DIMENSION
    heads, length, _ = q_ref.shape
    group = QUERY_GROUP
    kv = heads // group
    block = min(256, length)
    lanes = group * block
    key_at = lax.broadcasted_iota(jnp.int32, (block, block), 0)
    row_at = lax.broadcasted_iota(jnp.int32, (block, block), 1)
    causal = jnp.concatenate([key_at <= row_at] * group, axis=1)
    key_all = lax.broadcasted_iota(jnp.int32, (block, lanes), 0)
    dk_ref[...] = jnp.zeros_like(dk_ref)
    dv_ref[...] = jnp.zeros_like(dv_ref)
    head_sum_ref[...] = jnp.zeros_like(head_sum_ref)
    gain_sum_ref[...] = jnp.zeros_like(gain_sum_ref)
    for j in range(kv):
        for i in range(length // block):
            here = pl.ds(i * block, block)
            head = [j * group + g for g in range(group)]
            queries = jnp.concatenate([q_ref[h, here, :] for h in head], axis=0)
            grads = jnp.concatenate([g_ref[h, here, :] for h in head], axis=0)
            lse = jnp.concatenate([lse_ref[h, :, here] for h in head], axis=1)
            row_dot = jnp.concatenate([dot_ref[h, :, here] for h in head], axis=1)
            start = jnp.concatenate([start_ref[:, here]] * group, axis=1)
            dq = jnp.zeros((size, lanes), f32)
            for b in range(i + 1):
                there = pl.ds(b * block, block)
                keys = k_ref[j, there, :]
                scores = dot(keys, queries, 1, 1)
                allowed = key_all >= start - b * block
                if b == i:
                    allowed = allowed & causal
                probs = jnp.where(allowed, jnp.exp(scores - lse), 0.0)
                grad_probs = dot(v_ref[j, there, :], grads, 1, 1)
                grad_scores = (probs * (grad_probs - row_dot)).astype(bf16)
                dv_ref[j, there, :] += dot(probs.astype(bf16), grads, 1, 0)
                dk_ref[j, there, :] += dot(grad_scores, queries, 1, 0)
                dq = dq + dot(keys, grad_scores, 0, 0)
            for g in range(group):
                dq_ref[head[g], here, :] = dq[:, g * block : (g + 1) * block].T * size**-0.5
    for i in range(length // block):
        here = pl.ds(i * block, block)
        cos_part, sin_part = cos_ref[here, :], sin_ref[here, :]
        for j in range(kv):
            for g in range(group + 2):
                column = (j * (group + 2) + g) * size
                if g == group + 1:
                    back = dv_ref[j, here, :]
                else:
                    which = 0 if g < group else 1
                    grad = dq_ref[j * group + g, here, :] if g < group else dk_ref[j, here, :]
                    grad = grad * cos_part + swap_halves(grad * sin_part)
                    raw = projected_ref[here, column : column + size]
                    inverse = lax.rsqrt(jnp.mean(raw * raw, axis=1, keepdims=True) + eps_norm)
                    scaled = raw * inverse
                    head_sum_ref[which : which + 1, :] += jnp.sum(
                        grad * scaled, axis=0, keepdims=True
                    )
                    weighted = grad * head_gain_ref[which : which + 1, :]
                    back = inverse * (
                        weighted - scaled * jnp.mean(weighted * scaled, axis=1, keepdims=True)
                    )
                back_ref[here, column : column + size] = back.astype(bf16)
        term = dot(back_ref[here, :], weight_ref[:, : back_ref.shape[1]], 1, 1)
        gain_sum_ref[...] += jnp.sum(
            term * normed_ref[here, :].astype(f32), axis=0, keepdims=True
        )
        part_ref[here, :] = term.astype(bf16)
    gain_sum_ref[...] = gain_sum_ref[...] / gain_ref[...]


def attention_backward(
    queries, keys, values, grads, lse, row_dot, start, projected, head_gains, tables, weight, normed, gain
):
    heads, length, size = queries.shape
    kv = keys.shape[0]
    width = normed.shape[1]
    vmem = pl.BlockSpec(memory_space=pltpu.VMEM)
    return pl.pallas_call(
        attention_backward_kernel,
        in_specs=[vmem] * 14,
        out_specs=(vmem,) * 4,
        out_shape=(
            jax.ShapeDtypeStruct(projected.shape, bf16),
            jax.ShapeDtypeStruct((length, width), bf16),
            jax.ShapeDtypeStruct((2, size), f32),
            jax.ShapeDtypeStruct((1, width), f32),
        ),
        scratch_shapes=[
            pltpu.VMEM((heads, length, size), f32),
            pltpu.VMEM((kv, length, size), f32),
            pltpu.VMEM((kv, length, size), f32),
        ],
        compiler_params=pltpu.CompilerParams(vmem_limit_bytes=VMEM_LIMIT),
        cost_estimate=SMALL,
    )(
        queries, keys, values, grads, lse, row_dot, start, projected, head_gains, *tables, weight, normed, gain
    )


TILE = 256


def pack_units_kernel(both_ref, down_ref, out_ref):
    columns = both_ref.shape[2]
    rows = both_ref.shape[1]
    for i in range(out_ref.shape[1] // (3 * TILE)):
        first, last = i * TILE, min(columns, (i + 1) * TILE)
        parts = (both_ref[0, :, first:last], both_ref[1, :, first:last], down_ref[:, first:last])
        for k, part in enumerate(parts):
            if last - first < TILE:
                part = jnp.concatenate(
                    [part, jnp.zeros((rows, TILE - (last - first)), f32)], axis=1
                )
            at_column = (3 * i + k) * TILE
            out_ref[:, at_column : at_column + TILE] = part.astype(bf16)


def pack_units(gate_up, down):
    rows, columns = gate_up.shape[1:]
    steps = -(-columns // TILE)
    vmem = pl.BlockSpec(memory_space=pltpu.VMEM)
    return pl.pallas_call(
        pack_units_kernel,
        in_specs=[vmem, vmem],
        out_specs=vmem,
        out_shape=jax.ShapeDtypeStruct((rows, steps * 3 * TILE), bf16),
        compiler_params=pltpu.CompilerParams(vmem_limit_bytes=VMEM_LIMIT),
        cost_estimate=SMALL,
    )(gate_up, down)


def adam_kernel(weight_ref, first_ref, second_ref, sum_ref, *out_refs):
    gradient = sum_ref[...].astype(f32).reshape(weight_ref.shape)
    new = adam_step(
        weight_ref[...], first_ref[...], second_ref[...], gradient, rate_matrix, decay_matrix
    )
    for ref, value in zip(out_refs, new):
        ref[...] = value


def adam_units(weight, first, second, summed):
    parts, rows, columns = weight.shape
    state = pl.BlockSpec((1, rows, TILE), lambda p, i: (p, 0, i))
    return pl.pallas_call(
        adam_kernel,
        grid=(parts, -(-columns // TILE)),
        in_specs=[state] * 3 + [pl.BlockSpec((rows, TILE), lambda p, i: (0, parts * i + p))],
        out_specs=(state,) * 3,
        out_shape=(jax.ShapeDtypeStruct(weight.shape, f32),) * 3,
        compiler_params=pltpu.CompilerParams(vmem_limit_bytes=VMEM_LIMIT),
        cost_estimate=SMALL,
    )(weight, first, second, summed)


def units_forward_kernel(rows_ref, grad_ref, units_ref, *refs):
    rows_out, grads_out, hidden_ref, both_ref = refs[-4:]

    @pl.when(pl.program_id(0) == 0)
    def _():
        rows_out[...] = rows_ref[...]
        grads_out[...] = grad_ref[...]

    rows = rows_ref[...]
    gate_out = dot(rows, units_ref[:, :TILE], 1, 0)
    up_out = dot(rows, units_ref[:, TILE : 2 * TILE], 1, 0)
    grad_hidden = dot(grad_ref[...], units_ref[:, 2 * TILE :], 1, 0)
    gate_sig = jax.nn.sigmoid(gate_out)
    gate_act = gate_out * gate_sig
    hidden_ref[...] = (gate_act * up_out).astype(bf16)
    both_ref[:, :TILE] = (
        grad_hidden * up_out * (gate_sig + gate_act * (1.0 - gate_sig))
    ).astype(bf16)
    both_ref[:, TILE:] = (grad_hidden * gate_act).astype(bf16)


def units_forward(rows, grads, units, buffers, index):
    length, width = rows.shape
    steps = units.shape[1] // (3 * TILE)
    full = pl.BlockSpec((length, width), lambda i: (0, 0))
    kept = pl.BlockSpec((length, width), lambda i: (index, 0))
    held = () if buffers is None else buffers
    return pl.pallas_call(
        units_forward_kernel,
        grid=(steps,),
        in_specs=[full, full, pl.BlockSpec((width, 3 * TILE), lambda i: (0, i))]
        + [pl.BlockSpec(memory_space=pl.ANY)] * len(held),
        out_specs=(
            kept,
            kept,
            pl.BlockSpec((length, TILE), lambda i: (index, i)),
            pl.BlockSpec((length, 2 * TILE), lambda i: (index, i)),
        ),
        out_shape=(
            jax.ShapeDtypeStruct((4 * length, width), bf16),
            jax.ShapeDtypeStruct((4 * length, width), bf16),
            jax.ShapeDtypeStruct((4 * length, steps * TILE), bf16),
            jax.ShapeDtypeStruct((4 * length, steps * 2 * TILE), bf16),
        ),
        input_output_aliases={3 + k: k for k in range(len(held))},
        compiler_params=pltpu.CompilerParams(vmem_limit_bytes=VMEM_LIMIT),
        cost_estimate=SMALL,
    )(rows, grads, units, *held)


def units_back_kernel(both_ref, units_ref, out_ref):
    total = None
    for i in range(both_ref.shape[1] // (2 * TILE)):
        term = dot(
            both_ref[:, i * 2 * TILE : (i + 1) * 2 * TILE],
            units_ref[:, i * 3 * TILE : (i * 3 + 2) * TILE],
            1,
            1,
        )
        total = term if total is None else total + term
    out_ref[...] = total.astype(bf16)


def units_down_kernel(hidden_ref, units_ref, out_ref):
    total = None
    for i in range(hidden_ref.shape[1] // TILE):
        term = dot(
            hidden_ref[:, i * TILE : (i + 1) * TILE],
            units_ref[:, (i * 3 + 2) * TILE : (i * 3 + 3) * TILE],
            1,
            1,
        )
        total = term if total is None else total + term
    out_ref[...] = total.astype(bf16)


def units_to_width(kernel, values, units, first, count):
    width = units.shape[0]
    block, columns = values.shape[0] // 4, values.shape[1]
    length = block * count
    return pl.pallas_call(
        kernel,
        grid=(width // TILE,),
        in_specs=[
            pl.BlockSpec((length, columns), lambda i: (first // count, 0)),
            pl.BlockSpec((TILE, units.shape[1]), lambda i: (i, 0)),
        ],
        out_specs=pl.BlockSpec((length, TILE), lambda i: (0, i)),
        out_shape=jax.ShapeDtypeStruct((length, width), bf16),
        compiler_params=pltpu.CompilerParams(vmem_limit_bytes=VMEM_LIMIT),
        cost_estimate=SMALL,
    )(values, units)


def units_gradient_kernel(core_ref, left_ref, right_ref, kept_ref, given_ref, total_ref):
    total_ref[...] = dot(left_ref[...], right_ref[...], 0, 0)
    core = core_ref[0]
    pairs, rows, _ = kept_ref.shape
    for p in range(pairs):
        for c, ref in ((core, kept_ref), (1 - core, given_ref)):
            at_row = pl.multiple_of((2 * p + c) * rows, 16)
            ref[p] = total_ref[pl.ds(at_row, rows), :].astype(bf16)


def units_gradient_parts(left, right, core):
    length, width = left.shape
    columns = right.shape[1]
    count = lax.axis_size("dp")
    rows = width // count
    tile = 2 * TILE if columns % (2 * TILE) == 0 else TILE
    out = pl.BlockSpec((count // 2, rows, tile), lambda i, c: (0, 0, i))
    shape = jax.ShapeDtypeStruct((count // 2, rows, columns), bf16)
    return pl.pallas_call(
        units_gradient_kernel,
        grid_spec=pltpu.PrefetchScalarGridSpec(
            num_scalar_prefetch=1,
            grid=(columns // tile,),
            in_specs=[
                pl.BlockSpec((length, width), lambda i, c: (0, 0)),
                pl.BlockSpec((length, tile), lambda i, c: (0, i)),
            ],
            out_specs=(out, out),
            scratch_shapes=[pltpu.VMEM((width, tile), f32)],
        ),
        out_shape=(shape, shape),
        compiler_params=pltpu.CompilerParams(vmem_limit_bytes=VMEM_LIMIT),
        cost_estimate=SMALL,
    )(core[None], left, right)


def swap_core(value):
    count = lax.axis_size("dp")
    return lax.ppermute(value, "dp", [(i, i ^ 1) for i in range(count)])


def swap_near(value):
    return lax.ppermute(value, "tensor", [(0, 1), (1, 0), (2, 3), (3, 2)])


def swap_far(value):
    return lax.ppermute(value, "tensor", [(0, 2), (2, 0), (1, 3), (3, 1)])


def swap_middle(value):
    return lax.ppermute(value, "tensor", [(1, 2), (2, 1)])


def to_ends(value):
    return lax.ppermute(value, "tensor", [(1, 0), (2, 3)])


def from_ends(value):
    return lax.ppermute(value, "tensor", [(0, 1), (3, 2)])


def device_of(pair, core, z):
    return (2 * pair + core) * 4 + z


def owner_swap(value):
    perm = []
    for p in range(lax.axis_size("dp") // 2):
        for z in range(4):
            own = z // 2
            perm.append((device_of(p, own, z), device_of(p, own, z ^ 1)))
            perm.append((device_of(p, 1 - own, z), device_of(p, own, z ^ 2)))
    return lax.ppermute(value, AXES, perm)


def guest_swap(value):
    perm = []
    for p in range(lax.axis_size("dp") // 2):
        for z in range(4):
            guest = 1 - z // 2
            perm.append((device_of(p, guest, z), device_of(p, guest, z ^ 1)))
    return lax.ppermute(value, AXES, perm)


def heads_gather(value, first, second, own):
    mine = jnp.where(own, value, first)
    mine_next = jnp.where(own, first, second)
    return mine, mine_next, swap_core(mine), swap_core(mine_next)


def heads_scatter_begin(partial, core):
    rows, width = partial.shape[0] // 8, partial.shape[1]
    halves = partial.reshape(4, 2, rows, width)
    return at(halves, core, 1), swap_core(at(halves, core ^ 1, 1))


def heads_scatter_near(mine, other, z):
    def term(index):
        return at(mine, index, 0).astype(f32) + at(other, index, 0).astype(f32)

    away = swap_near(term(z ^ 3).astype(bf16))
    return term(z), term(z ^ 2), swap_near(term(z ^ 1).astype(bf16)), away


def heads_scatter_end(home, far, own, core):
    kept = jnp.where(own, home, far.astype(f32))
    given = swap_core(jnp.where(own, far, home.astype(bf16))).astype(f32)
    return jnp.concatenate(
        [jnp.where(core == 0, kept, given), jnp.where(core == 0, given, kept)], axis=0
    )


def gather_tensor(value, bit):
    other = lax.ppermute(value, "tensor", [(i, i ^ bit) for i in range(4)])
    upper = (lax.axis_index("tensor") & bit) != 0
    return jnp.concatenate(
        [jnp.where(upper, other, value), jnp.where(upper, value, other)], axis=0
    )


def gather_dp(value):
    bit = 1
    while bit < lax.axis_size("dp"):
        other = swap_dp(value, bit)
        upper = (lax.axis_index("dp") & bit) != 0
        value = jnp.concatenate(
            [jnp.where(upper, other, value), jnp.where(upper, value, other)], axis=0
        )
        bit *= 2
    return value


def sum_dp(value):
    bit = 1
    while bit < lax.axis_size("dp"):
        value = value + swap_dp(value, bit)
        bit *= 2
    return value


def sum_tensor(value):
    value = value + swap_near(value)
    return value + swap_far(value)


def pair_groups():
    count = lax.axis_size("dp")
    return [list(range(c, count, 2)) for c in range(2)]


def swap_dp(value, mask):
    count = lax.axis_size("dp")
    return lax.ppermute(value, "dp", [(i, i ^ mask) for i in range(count)])


def gather_pairs_begin(value):
    if lax.axis_size("dp") != 8:
        return (lax.all_gather(value, "dp", axis=0, tiled=True, axis_index_groups=pair_groups()),)
    return value, swap_dp(value, 2), swap_dp(value, 4)


def gather_pairs_end(parts):
    if len(parts) == 1:
        return parts[0]
    value, by_two, by_four = parts
    pair = lax.axis_index("dp") >> 1
    rows = value.shape[0]
    half = rows // 2
    low, high = swap_dp(by_four[:half], 2), swap_dp(by_two[half:], 4)
    whole = jnp.zeros((4 * rows,) + value.shape[1:], value.dtype)
    for part, index, offset in (
        (value, pair, 0),
        (by_two, pair ^ 1, 0),
        (by_four, pair ^ 2, 0),
        (low, pair ^ 3, 0),
        (high, pair ^ 3, half),
    ):
        whole = lax.dynamic_update_slice_in_dim(whole, part, index * rows + offset, 0)
    return whole


def at(value, index, axis):
    return lax.dynamic_index_in_dim(value, index, axis, keepdims=False)


def add_low(left, right):
    return (left.astype(f32) + right.astype(f32)).astype(bf16)


def scatter_pairs_begin(value):
    if lax.axis_size("dp") != 8:
        return (
            lax.psum_scatter(
                value, "dp", scatter_dimension=0, tiled=True, axis_index_groups=pair_groups()
            ),
        )
    pair = lax.axis_index("dp") >> 1
    one, two = pair & 1, pair >> 1
    rows = value.shape[0] // 8
    parts = value.reshape((2, 2, 2, rows) + value.shape[1:])
    first, second = parts[:, :, 0], parts[:, :, 1]
    by_two = swap_dp(at(first, one ^ 1, 1), 2)
    by_four = swap_dp(at(second, two ^ 1, 0), 4)
    return at(first, one, 1), by_two, at(second, two, 0), by_four


def scatter_pairs_end(parts):
    if len(parts) == 1:
        return parts[0]
    pair = lax.axis_index("dp") >> 1
    one, two = pair & 1, pair >> 1
    first = add_low(parts[0], parts[1])
    second = add_low(parts[2], parts[3])
    by_four = swap_dp(at(first, two ^ 1, 0), 4)
    by_two = swap_dp(at(second, one ^ 1, 0), 2)
    first = add_low(at(first, two, 0), by_four)
    second = add_low(at(second, one, 0), by_two)
    return jnp.concatenate([first, second], axis=0)


def heads_pair(shard, far, own, core):
    kept = jnp.where(own, shard, far)
    other = swap_core(jnp.where(own, far, shard))
    return jnp.concatenate(
        [jnp.where(core == 0, kept, other), jnp.where(core == 0, other, kept)], axis=0
    )


def heads_home(pair, own, core):
    rows = pair.shape[0] // 2
    kept = jnp.where(core == 0, pair[:rows], pair[rows:])
    other = swap_core(jnp.where(core == 0, pair[rows:], pair[:rows]))
    return jnp.where(own, kept, other), jnp.where(own, other, kept)


def units_gradient(summed):
    return lax.psum_scatter(
        summed.reshape(-1, summed.shape[-1]),
        "dp",
        scatter_dimension=0,
        tiled=True,
        axis_index_groups=pair_groups(),
    )


def together(*values):
    return lax.optimization_barrier(values)


def shards(
    block_in,
    out_grad,
    positions,
    qkv_weight,
    qkv_first,
    qkv_second,
    out_weight,
    out_first,
    out_second,
    gate_up,
    gate_up_first,
    gate_up_second,
    down_weight,
    down_first,
    down_second,
    norm_gains,
    norm_gains_first,
    norm_gains_second,
):
    model_width = block_in.shape[1]
    z = lax.axis_index("tensor")
    core = lax.axis_index("dp") & 1
    own = core == z // 2
    place = jnp.where(own, z, z ^ 2)[None]

    units_columns = gate_up.shape[2]
    gains_near = gather_tensor(norm_gains[None], 1)
    heads_own = jnp.concatenate([qkv_weight.astype(bf16), out_weight.astype(bf16).T], axis=1)
    heads_far = swap_far(heads_own)
    inverse_in = lax.rsqrt(jnp.mean(block_in * block_in, axis=-1, keepdims=True) + eps_norm)
    scaled_in = block_in * inverse_in
    head_positions = jnp.where(own, positions, swap_core(positions))
    scaled_b, heads_own, heads_far, head_positions, units_shard, grad_own, gains_near = together(
        scaled_in.astype(bf16),
        heads_own,
        heads_far,
        head_positions,
        pack_units(gate_up, down_weight.T),
        out_grad.astype(bf16),
        gains_near,
    )

    scaled_first = owner_swap(scaled_b)
    heads_parts = gather_pairs_begin(heads_pair(heads_own, heads_far, own, core))
    gains_near = gather_tensor(gains_near, 2)
    tables = rope_tables(head_positions, HEAD_DIMENSION)
    length = head_positions.shape[0]
    start = jnp.maximum(jnp.arange(length, dtype=jnp.int32) - head_positions, 0)
    scaled_first, heads_parts, gains_near, units_shard, tables, start, grad_own = together(
        scaled_first, heads_parts, gains_near, units_shard, tables, start, grad_own
    )

    scaled_second = guest_swap(scaled_first)
    w_heads = gather_pairs_end(heads_parts)
    units = lax.all_gather(units_shard, "dp", axis=0, tiled=True)
    grad_middle_part = swap_middle(grad_own)
    gains_all = gather_dp(gains_near.reshape(1, -1)).reshape(1, -1)
    gain_attn = gains_all[:, :model_width]
    head_gains = gains_all[0, model_width : model_width + 2 * HEAD_DIMENSION].reshape(2, -1)
    gain_ffn = gains_all[:, model_width + 2 * HEAD_DIMENSION :]
    scaled_parts = heads_gather(scaled_b, scaled_first, scaled_second, own)
    w_heads, scaled_parts, gain_attn, head_gains, gain_ffn, grad_own = together(
        w_heads, scaled_parts, gain_attn, head_gains, gain_ffn, grad_own
    )

    qkv_columns = qkv_weight.shape[1]
    grad_far = swap_far(grad_own)
    grad_near = swap_near(grad_own)
    normed_all, projected, queries_b, keys_b, values_b, attended, lse = attention_forward(
        place, scaled_parts, gain_attn, head_gains, w_heads, tables, start[:, None]
    )
    w_qkv, w_out = w_heads[:, :qkv_columns], w_heads[:, qkv_columns:]
    branch = dot(attended, w_out, 1, 1).astype(bf16)
    branch, grad_far, grad_near, grad_middle_part = together(
        branch, grad_far, grad_near, grad_middle_part
    )
    branch_mine, branch_other = together(*heads_scatter_begin(branch, core))
    home, term_far, near, away = heads_scatter_near(branch_mine, branch_other, z)
    away, term_far, grad_far = together(away, term_far, grad_far)
    far = swap_far((term_far + away.astype(f32)).astype(bf16))
    grad_ends = to_ends(grad_far)
    middle = block_in + heads_scatter_end(home + near.astype(f32), far, own, core)

    inverse_mid = lax.rsqrt(jnp.mean(middle * middle, axis=-1, keepdims=True) + eps_norm)
    scaled_mid = middle * inverse_mid
    rows_own = (scaled_mid * gain_ffn).astype(bf16)
    rows_far = swap_far(rows_own)
    rows_near = swap_near(rows_own)
    inner = (z == 1) | (z == 2)
    buffers = units_forward(rows_own, grad_own, units, None, 0)
    rows_far, rows_near, rows_own, buffers = together(rows_far, rows_near, rows_own, buffers)
    rows_ends = to_ends(rows_far)
    rows_middle = swap_middle(rows_own)
    buffers = units_forward(rows_near, grad_near, units, buffers, 1)
    buffers = units_forward(rows_far, grad_far, units, buffers, 2)
    rows_ends, rows_middle, grad_ends, buffers = together(
        rows_ends, rows_middle, grad_ends, buffers
    )
    rows_last = jnp.where(inner, rows_middle, rows_ends)
    grad_last = jnp.where(inner, grad_middle_part, grad_ends)
    rows_all, grad_all, hidden_b, dboth = units_forward(rows_last, grad_last, units, buffers, 3)

    back_last = units_to_width(units_back_kernel, dboth, units, 3, 1)
    back_last, dboth = together(back_last, dboth)
    from_last = from_ends(back_last)
    from_middle = swap_middle(back_last)
    back_rest = units_to_width(units_back_kernel, dboth, units, 0, 3)
    rows = block_in.shape[0]
    back_rest, from_last, rows_all, grad_all, hidden_b, dboth = together(
        back_rest, from_last, rows_all, grad_all, hidden_b, dboth
    )
    back_own, back_near, back_far = (back_rest[k * rows : (k + 1) * rows] for k in range(3))
    from_near = swap_near(back_near)
    from_far = swap_far(add_low(back_far, from_last))
    down_kept, down_given = units_gradient_parts(grad_all, hidden_b, core)
    both_kept, both_given = units_gradient_parts(rows_all, dboth, core)
    from_far, from_near, from_middle, down_kept, down_given, both_kept, both_given = together(
        from_far, from_near, from_middle, down_kept, down_given, both_kept, both_given
    )
    grad_normed_two = (
        back_own.astype(f32)
        + from_near.astype(f32)
        + from_middle.astype(f32)
        + from_far.astype(f32)
    )

    grad_gain_ffn = jnp.sum(grad_normed_two * scaled_mid, axis=0)
    weighted = grad_normed_two * gain_ffn
    grad_middle = out_grad + inverse_mid * (
        weighted - scaled_mid * jnp.mean(weighted * scaled_mid, axis=-1, keepdims=True)
    )
    grad_mid_b, grad_gain_ffn = together(grad_middle.astype(bf16), grad_gain_ffn)
    grad_mid_first = owner_swap(grad_mid_b)
    down_other = swap_core(down_given)
    both_other = swap_core(both_given)
    down_part = units_to_width(units_down_kernel, hidden_b, units, 0, 4)
    grad_mid_first, down_part, down_other, both_other = together(
        grad_mid_first, down_part, down_other, both_other
    )
    grad_mid_second = guest_swap(grad_mid_first)
    down_own, down_near, down_far, down_last = (
        down_part[k * rows : (k + 1) * rows] for k in range(4)
    )
    branch_ends = from_ends(down_last)
    down_sum = add_low(down_kept, down_other)
    both_sum = add_low(both_kept, both_other)
    grad_mid_second, down_sum, both_sum = together(grad_mid_second, down_sum, both_sum)
    sum_down = units_gradient(down_sum)
    sum_both = units_gradient(both_sum)
    grad_mid_parts = heads_gather(grad_mid_b, grad_mid_first, grad_mid_second, own)
    grad_mid_parts, branch_ends = together(grad_mid_parts, branch_ends)

    branch_far = swap_far(add_low(down_far, branch_ends))
    branch_near = swap_near(down_near)
    branch_middle = swap_middle(down_last)
    grad_attended, row_dot, grad_out_w = attention_turn(place, grad_mid_parts, w_out, attended)
    grad_attended, row_dot, grad_out_w = together(grad_attended, row_dot, grad_out_w)
    out_parts = scatter_pairs_begin(grad_out_w)
    grad_projected, grad_normed_b, head_sums, gain_sums = attention_backward(
        queries_b,
        keys_b,
        values_b,
        grad_attended,
        lse,
        row_dot,
        start[None, :],
        projected,
        head_gains,
        tables,
        w_heads,
        normed_all,
        gain_attn,
    )
    grad_projected, grad_normed_b, branch_far, branch_near, branch_middle, out_parts = together(
        grad_projected, grad_normed_b, branch_far, branch_near, branch_middle, out_parts
    )

    part_mine, part_other = heads_scatter_begin(grad_normed_b, core)
    grad_qkv = dot(normed_all, grad_projected, 0, 0).astype(bf16)
    part_mine, part_other, grad_qkv = together(part_mine, part_other, grad_qkv)
    home, term_far, near, away = heads_scatter_near(part_mine, part_other, z)
    qkv_parts = scatter_pairs_begin(grad_qkv)
    out_pair = scatter_pairs_end(out_parts)
    gain_total = jnp.concatenate([gain_sums[0], head_sums.reshape(-1), grad_gain_ffn])
    down_new = adam_units(
        down_weight.T[None], down_first.T[None], down_second.T[None], sum_down
    )
    away, term_far, qkv_parts, out_pair, gain_total, down_new = together(
        away, term_far, qkv_parts, out_pair, gain_total, down_new
    )
    far = swap_far((term_far + away.astype(f32)).astype(bf16))
    heads_home_own, heads_home_away = heads_home(
        jnp.concatenate([scatter_pairs_end(qkv_parts), out_pair], axis=1), own, core
    )
    gain_total = sum_dp(gain_total)
    gate_up_new = adam_units(gate_up, gate_up_first, gate_up_second, sum_both)
    far, home, near, heads_home_own, heads_home_away, gain_total, gate_up_new = together(
        far, home, near, heads_home_own, heads_home_away, gain_total, gate_up_new
    )
    heads_away = swap_far(heads_home_away)
    grad_normed = heads_scatter_end(home + near.astype(f32), far, own, core)
    gain_total = sum_tensor(gain_total)
    block_out = (
        middle
        + down_own.astype(f32)
        + branch_near.astype(f32)
        + branch_middle.astype(f32)
        + branch_far.astype(f32)
    )
    weighted = grad_normed * gain_attn
    in_grad = grad_middle + inverse_in * (
        weighted - scaled_in * jnp.mean(weighted * scaled_in, axis=-1, keepdims=True)
    )
    heads_away, block_out, in_grad = together(heads_away, block_out, in_grad)
    sum_heads = heads_home_own.astype(f32) + heads_away.astype(f32)
    down_new = tuple(value[0].T for value in down_new)
    sum_qkv = sum_heads[:, :qkv_columns]
    sum_out = sum_heads[:, qkv_columns:].T
    gain_count = norm_gains.shape[0]
    gain_at = (lax.axis_index("dp") * 4 + z) * gain_count
    gain_grads = lax.dynamic_slice_in_dim(gain_total, gain_at, gain_count)

    qkv_new = adam_step(qkv_weight, qkv_first, qkv_second, sum_qkv, rate_matrix, decay_matrix)
    out_new = adam_step(out_weight, out_first, out_second, sum_out, rate_output, decay_matrix)
    gains_new = adam_step(
        norm_gains, norm_gains_first, norm_gains_second, gain_grads, rate_gains, 0.0
    )
    return (block_out, in_grad, *qkv_new, *out_new, *gate_up_new, *down_new, *gains_new)


def solution(mesh):
    tokens = P(("dp", "tensor"), None)
    by_rows = (P("dp", "tensor"),) * 3
    by_columns = (P("tensor", "dp"),) * 3
    stacked = (P(None, "dp", "tensor"),) * 3
    gains = (P(("dp", "tensor")),) * 3
    states = by_rows + by_columns + stacked + by_columns + gains
    return jax.shard_map(
        shards,
        mesh=mesh,
        in_specs=(tokens, tokens, P("dp")) + states,
        out_specs=(tokens, tokens) + states,
        check_vma=False,
    )
```

```python
import functools

import jax
import jax.numpy as jnp
from jax import lax
from jax.experimental import pallas as pl
from jax.experimental.pallas import tpu as pltpu
from jax.sharding import PartitionSpec as P

HEAD_DIMENSION = 64
STEP = 10
QUERY_GROUP = 3
AXES = ("dp", "tensor")

eps_norm = 1e-05
rope_base = 1000000.0
beta_one = 0.9
beta_two = 0.999
adam_eps = 1e-08
decay_matrix = 0.1
rate_matrix = 0.03
rate_output = 0.15
rate_gains = 0.8
bf16 = jnp.bfloat16
f32 = jnp.float32
VMEM_LIMIT = 58 * 1024 * 1024
SMALL = pl.CostEstimate(flops=1000, bytes_accessed=1000, transcendentals=0)


def whole(value):
    zeros = (0,) * len(value.shape)
    return pl.BlockSpec(value.shape, lambda i: zeros, pipeline_mode=pl.Buffered(1))


def scalars(count):
    return [pl.BlockSpec(memory_space=pltpu.SMEM)] * count


def dot(left, right, left_dim, right_dim):
    return lax.dot_general(
        left, right, (((left_dim,), (right_dim,)), ((), ())), preferred_element_type=f32
    )


def norm_rows(row_block, gain_vec):
    inverse = lax.rsqrt(jnp.mean(row_block * row_block, axis=-1, keepdims=True) + eps_norm)
    return row_block * inverse * gain_vec


def rope_tables(positions, head_size):
    inverse_freq = rope_base ** (-(jnp.arange(head_size // 2, dtype=f32) * 2.0) / head_size)
    angles = positions.astype(f32)[:, None] * inverse_freq[None, :]
    cos_part, sin_part = jnp.cos(angles), jnp.sin(angles)
    return (
        jnp.concatenate([cos_part] * 4, axis=1),
        jnp.concatenate([-sin_part, sin_part] * 2, axis=1),
    )


def adam_step(weight, first_old, second_old, gradient, step_rate, decay_rate):
    first_new = beta_one * first_old + (1.0 - beta_one) * gradient
    second_new = beta_two * second_old + (1.0 - beta_two) * gradient * gradient
    fix_one = 1.0 - beta_one**STEP
    fix_two = 1.0 - beta_two**STEP
    update = first_new / fix_one / (jnp.sqrt(second_new / fix_two) + adam_eps)
    return (weight - step_rate * (update + decay_rate * weight), first_new, second_new)


PAIR = 2 * HEAD_DIMENSION


def lanes_of(value):
    return lax.broadcasted_iota(jnp.int32, value.shape, 1)


def swap_halves(value):
    half = HEAD_DIMENSION // 2
    low = lanes_of(value) % HEAD_DIMENSION < half
    return jnp.where(low, pltpu.roll(value, PAIR - half, 1), pltpu.roll(value, half, 1))


def two_parts(value):
    high = value.astype(bf16)
    return high, (value - high.astype(f32)).astype(bf16)


def head_means(value):
    shape = (PAIR, PAIR)
    one, two = (lax.broadcasted_iota(jnp.int32, shape, d) // HEAD_DIMENSION for d in (0, 1))
    weights = jnp.where(one == two, 1.0 / HEAD_DIMENSION, 0.0).astype(bf16)
    high, low = two_parts(value)
    return dot(high, weights, 1, 0) + dot(low, weights, 1, 0)


def is_value(index, value):
    at_head = [(2 * index + k) % (QUERY_GROUP + 2) == QUERY_GROUP + 1 for k in range(2)]
    if not any(at_head):
        return None
    return (lanes_of(value) < HEAD_DIMENSION) == at_head[0]


def unless(mask, value, other):
    return value if mask is None else jnp.where(mask, other, value)


def as_row(column):
    return jnp.broadcast_to(column, (column.shape[0], 128)).T[:1, :]


def place_parts(place_ref, part_refs, whole_ref, scale):
    rows = part_refs[0].shape[0]
    for j, part_ref in enumerate(part_refs):
        at_row = pl.multiple_of((j ^ place_ref[0]) * rows, rows)
        value = part_ref[...]
        if scale is not None:
            value = (value.astype(f32) * scale).astype(bf16)
        whole_ref[pl.ds(at_row, rows), :] = value


def split_halves(core_ref, value, stage_ref, mine_ref, other_ref, index):
    half = value.shape[0] // 2
    stage_ref[...] = value
    core = core_ref[0]
    mine_ref[index] = stage_ref[pl.ds(pl.multiple_of(core * half, half), half), :]
    other_ref[index] = stage_ref[pl.ds(pl.multiple_of((1 - core) * half, half), half), :]


def place_blocks(begins_ref, block_refs, whole_ref):
    for k, block_ref in enumerate(block_refs):
        begin = pl.multiple_of(begins_ref[k], 16)
        whole_ref[pl.ds(begin, block_ref.shape[0]), :] = block_ref[...]


def attention_forward_kernel(count, place_ref, begins_ref, *refs):
    part_refs, refs = refs[:4], refs[4:]
    block_refs, refs = refs[:count], refs[count:]
    (
        gain_ref,
        head_gain_ref,
        cos_ref,
        sin_ref,
        start_ref,
        weight_ref,
        normed_ref,
        projected_ref,
        q_ref,
        k_ref,
        v_ref,
        out_ref,
        lse_ref,
    ) = refs
    place_blocks(begins_ref, block_refs, weight_ref)
    size = HEAD_DIMENSION
    heads, length, _ = q_ref.shape
    group = QUERY_GROUP
    kv = heads // group
    block = min(256, length)
    place_parts(place_ref, part_refs, normed_ref, gain_ref[...])
    for i in range(length // block):
        here = pl.ds(i * block, block)
        projected = dot(normed_ref[here, :], weight_ref[...], 1, 0)
        projected_ref[here, :] = projected
        cos_part, sin_part = cos_ref[here, :], sin_ref[here, :]
        for t in range(projected.shape[1] // PAIR):
            raw = projected[:, t * PAIR : (t + 1) * PAIR]
            keep = is_value(t, raw)
            inverse = unless(keep, lax.rsqrt(head_means(raw * raw) + eps_norm), 1.0)
            normed = raw * inverse * head_gain_ref[:, t * PAIR : (t + 1) * PAIR]
            turned = normed * unless(keep, cos_part, 1.0) + swap_halves(normed) * unless(
                keep, sin_part, 0.0
            )
            turned = turned.astype(bf16)
            for k in range(2):
                j, g = divmod(2 * t + k, group + 2)
                piece = turned[:, k * size : (k + 1) * size]
                if g < group:
                    q_ref[j * group + g, here, :] = piece * jnp.asarray(size**-0.5, bf16)
                elif g == group:
                    k_ref[j, here, :] = piece
                else:
                    v_ref[j, here, :] = piece
    row_at = lax.broadcasted_iota(jnp.int32, (block, block), 0)
    col_at = lax.broadcasted_iota(jnp.int32, (block, block), 1)
    causal = jnp.concatenate([col_at <= row_at] * group, axis=0)
    col_all = lax.broadcasted_iota(jnp.int32, (group * block, block), 1)
    ones = jnp.ones((block, size), bf16)
    for j in range(kv):
        for i in range(length // block):
            here = pl.ds(i * block, block)
            queries = jnp.concatenate(
                [q_ref[j * group + g, here, :] for g in range(group)], axis=0
            )
            start = jnp.concatenate([start_ref[here, :]] * group, axis=0)
            total = jnp.zeros((group * block, 2 * size), f32)
            for b in range(i + 1):
                there = pl.ds(b * block, block)
                scores = dot(queries, k_ref[j, there, :], 1, 1)
                allowed = col_all >= start - b * block
                if b == i:
                    allowed = allowed & causal
                weights = jnp.where(allowed, jnp.exp(scores), 0.0).astype(bf16)
                values = jnp.concatenate([v_ref[j, there, :], ones], axis=1)
                total = total + dot(weights, values, 1, 0)
            row_sum = total[:, size : size + 1]
            output = (total[:, :size] / row_sum).astype(bf16)
            log_sum = jnp.log(row_sum)
            for g in range(group):
                h = j * group + g
                part = slice(g * block, (g + 1) * block)
                out_ref[here, h * size : (h + 1) * size] = output[part]
                lse_ref[h, :, here] = as_row(log_sum[part])


def attention_branch_kernel(count, core_ref, begins_ref, *refs):
    block_refs = refs[:count]
    attended_ref, weight_ref, mine_ref, other_ref, stage_ref = refs[count:]
    place_blocks(begins_ref, block_refs, weight_ref)
    shard = attended_ref.shape[0] // 4
    for i in range(4):
        value = dot(attended_ref[i * shard : (i + 1) * shard, :], weight_ref[...], 1, 1)
        split_halves(core_ref, value.astype(bf16), stage_ref, mine_ref, other_ref, i)


def attention_forward(place, parts, blocks, begins, gain_attn, head_gains, tables, start):
    rows, width = parts[0].shape
    length = 4 * rows
    size = HEAD_DIMENSION
    columns = blocks[0].shape[1]
    kv = columns // ((QUERY_GROUP + 2) * size)
    heads = kv * QUERY_GROUP
    operands = (*parts, *blocks, gain_attn, head_gains, *tables, start)
    results = (
        jax.ShapeDtypeStruct((width, columns), bf16),
        jax.ShapeDtypeStruct((length, width), bf16),
        jax.ShapeDtypeStruct((length, columns), f32),
        jax.ShapeDtypeStruct((heads, length, size), bf16),
        jax.ShapeDtypeStruct((kv, length, size), bf16),
        jax.ShapeDtypeStruct((kv, length, size), bf16),
        jax.ShapeDtypeStruct((length, heads * size), bf16),
        jax.ShapeDtypeStruct((heads, 1, length), f32),
    )
    return pl.pallas_call(
        functools.partial(attention_forward_kernel, len(blocks)),
        grid=(1,),
        in_specs=scalars(2) + [whole(value) for value in operands],
        out_specs=tuple(whole(value) for value in results),
        out_shape=results,
        compiler_params=pltpu.CompilerParams(vmem_limit_bytes=VMEM_LIMIT),
        cost_estimate=SMALL,
    )(place, begins, *operands)


def attention_branch(core, blocks, begins, attended):
    length, columns = attended.shape
    width = 4 * (blocks[0].shape[0]) if len(blocks) > 1 else blocks[0].shape[0]
    half = jax.ShapeDtypeStruct((4, length // 8, width), bf16)
    operands = (*blocks, attended)
    results = (jax.ShapeDtypeStruct((width, columns), bf16), half, half)
    return pl.pallas_call(
        functools.partial(attention_branch_kernel, len(blocks)),
        grid=(1,),
        in_specs=scalars(2) + [whole(value) for value in operands],
        out_specs=tuple(whole(value) for value in results),
        out_shape=results,
        scratch_shapes=[pltpu.VMEM((length // 4, width), bf16)],
        compiler_params=pltpu.CompilerParams(vmem_limit_bytes=VMEM_LIMIT),
        cost_estimate=SMALL,
    )(core, begins, *operands)


def attention_turn_kernel(
    place_ref, part_0, part_1, part_2, part_3, weight_ref, out_ref, grads_ref, dot_ref, dw_ref, whole_ref
):
    size = HEAD_DIMENSION
    place_parts(place_ref, (part_0, part_1, part_2, part_3), whole_ref, None)
    heads, length, _ = grads_ref.shape
    block = min(256, length)
    shape = (dot_ref.shape[0], heads * size)
    of_head = (
        lax.broadcasted_iota(jnp.int32, shape, 0)
        == lax.broadcasted_iota(jnp.int32, shape, 1) // size
    ).astype(bf16)
    for i in range(length // block):
        here = pl.ds(i * block, block)
        grads = dot(whole_ref[here, :], weight_ref[...], 1, 0).astype(bf16)
        high, low = two_parts(grads.astype(f32) * out_ref[here, :].astype(f32))
        dot_ref[:, here] = dot(of_head, high, 1, 1) + dot(of_head, low, 1, 1)
        for h in range(heads):
            grads_ref[h, here, :] = grads[:, h * size : (h + 1) * size]
    dw_ref[...] = dot(whole_ref[...], out_ref[...], 0, 0).astype(bf16)


def attention_turn(place, parts, weight, attended):
    rows, width = parts[0].shape
    length, columns = attended.shape
    heads = columns // HEAD_DIMENSION
    operands = (*parts, weight, attended)
    results = (
        jax.ShapeDtypeStruct((heads, length, HEAD_DIMENSION), bf16),
        jax.ShapeDtypeStruct((-(-heads // 8) * 8, length), f32),
        jax.ShapeDtypeStruct((width, columns), bf16),
    )
    return pl.pallas_call(
        attention_turn_kernel,
        grid=(1,),
        in_specs=scalars(1) + [whole(value) for value in operands],
        out_specs=tuple(whole(value) for value in results),
        out_shape=results,
        scratch_shapes=[pltpu.VMEM((length, width), bf16)],
        compiler_params=pltpu.CompilerParams(vmem_limit_bytes=VMEM_LIMIT),
        cost_estimate=SMALL,
    )(place, *operands)


def attention_backward_kernel(
    core_ref,
    q_ref,
    k_ref,
    v_ref,
    g_ref,
    lse_ref,
    dot_ref,
    start_ref,
    projected_ref,
    head_gain_ref,
    cos_ref,
    sin_ref,
    weight_ref,
    normed_ref,
    gain_ref,
    back_ref,
    mine_ref,
    other_ref,
    head_sum_ref,
    gain_sum_ref,
    grad_ref,
    dk_ref,
    dv_ref,
    stage_ref,
):
    size = HEAD_DIMENSION
    heads, length, _ = q_ref.shape
    group = QUERY_GROUP
    kv = heads // group
    block = min(256, length)
    lanes = group * block
    key_at = lax.broadcasted_iota(jnp.int32, (block, block), 0)
    row_at = lax.broadcasted_iota(jnp.int32, (block, block), 1)
    causal = jnp.concatenate([key_at <= row_at] * group, axis=1)
    key_all = lax.broadcasted_iota(jnp.int32, (block, lanes), 0)
    dk_ref[...] = jnp.zeros_like(dk_ref)
    dv_ref[...] = jnp.zeros_like(dv_ref)
    head_sum_ref[...] = jnp.zeros_like(head_sum_ref)
    gain_sum_ref[...] = jnp.zeros_like(gain_sum_ref)
    for j in range(kv):
        for i in range(length // block):
            here = pl.ds(i * block, block)
            head = [j * group + g for g in range(group)]
            queries = jnp.concatenate([q_ref[h, here, :] for h in head], axis=0)
            grads = jnp.concatenate([g_ref[h, here, :] for h in head], axis=0)
            lse = jnp.concatenate([lse_ref[h, :, here] for h in head], axis=1)
            row_dot = jnp.concatenate([dot_ref[h : h + 1, here] for h in head], axis=1)
            start = jnp.concatenate([start_ref[:, here]] * group, axis=1)
            dq = jnp.zeros((size, lanes), f32)
            for b in range(i + 1):
                there = pl.ds(b * block, block)
                keys = k_ref[j, there, :]
                scores = dot(keys, queries, 1, 1)
                allowed = key_all >= start - b * block
                if b == i:
                    allowed = allowed & causal
                probs = jnp.where(allowed, jnp.exp(scores - lse), 0.0)
                grad_probs = dot(v_ref[j, there, :], grads, 1, 1)
                grad_scores = (probs * (grad_probs - row_dot)).astype(bf16)
                dv_ref[j, there, :] += dot(probs.astype(bf16), grads, 1, 0)
                dk_ref[j, there, :] += dot(grad_scores, queries, 1, 0)
                dq = dq + dot(keys, grad_scores, 0, 0)
            for g in range(group):
                column = (j * (group + 2) + g) * size
                grad_ref[here, column : column + size] = (
                    dq[:, g * block : (g + 1) * block].T * size**-0.5
                )
        key_column = (j * (group + 2) + group) * size
        grad_ref[:, key_column : key_column + size] = dk_ref[j]
        grad_ref[:, key_column + size : key_column + 2 * size] = dv_ref[j]
    shard = length // 4
    for i in range(4):
        here = pl.ds(i * shard, shard)
        cos_part, sin_part = cos_ref[here, :], sin_ref[here, :]
        for t in range(back_ref.shape[1] // PAIR):
            columns = slice(t * PAIR, (t + 1) * PAIR)
            given = grad_ref[here, columns]
            keep = is_value(t, given)
            grad = given * unless(keep, cos_part, 1.0) + swap_halves(
                given * unless(keep, sin_part, 0.0)
            )
            raw = projected_ref[here, columns]
            inverse = lax.rsqrt(head_means(raw * raw) + eps_norm)
            scaled = raw * inverse
            head_sum_ref[:, columns] += jnp.sum(grad * scaled, axis=0, keepdims=True)
            weighted = grad * head_gain_ref[:, columns]
            back = inverse * (weighted - scaled * head_means(weighted * scaled))
            back_ref[here, columns] = unless(keep, back, given).astype(bf16)
        term = dot(back_ref[here, :], weight_ref[...], 1, 1)
        gain_sum_ref[...] += jnp.sum(
            term * normed_ref[here, :].astype(f32), axis=0, keepdims=True
        )
        split_halves(core_ref, term.astype(bf16), stage_ref, mine_ref, other_ref, i)
    gain_sum_ref[...] = gain_sum_ref[...] / gain_ref[...]


def attention_backward(core, queries, keys, values, grads, lse, row_dot, start, projected, *rest):
    heads, length, size = queries.shape
    kv = keys.shape[0]
    normed = rest[-2]
    width = normed.shape[1]
    half = jax.ShapeDtypeStruct((4, length // 8, width), bf16)
    operands = (queries, keys, values, grads, lse, row_dot, start, projected) + rest
    results = (
        jax.ShapeDtypeStruct(projected.shape, bf16),
        half,
        half,
        jax.ShapeDtypeStruct((1, projected.shape[1]), f32),
        jax.ShapeDtypeStruct((1, width), f32),
    )
    return pl.pallas_call(
        attention_backward_kernel,
        grid=(1,),
        in_specs=scalars(1) + [whole(value) for value in operands],
        out_specs=tuple(whole(value) for value in results),
        out_shape=results,
        scratch_shapes=[
            pltpu.VMEM(projected.shape, f32),
            pltpu.VMEM((kv, length, size), f32),
            pltpu.VMEM((kv, length, size), f32),
            pltpu.VMEM((length // 4, width), bf16),
        ],
        compiler_params=pltpu.CompilerParams(vmem_limit_bytes=VMEM_LIMIT),
        cost_estimate=SMALL,
    )(core, *operands)


TILE = 256


def pack_units_kernel(both_ref, down_ref, out_ref):
    columns = both_ref.shape[2]
    rows = both_ref.shape[1]
    for i in range(out_ref.shape[1] // (3 * TILE)):
        first, last = i * TILE, min(columns, (i + 1) * TILE)
        parts = (both_ref[0, :, first:last], both_ref[1, :, first:last], down_ref[:, first:last])
        for k, part in enumerate(parts):
            if last - first < TILE:
                part = jnp.concatenate(
                    [part, jnp.zeros((rows, TILE - (last - first)), f32)], axis=1
                )
            at_column = (3 * i + k) * TILE
            out_ref[:, at_column : at_column + TILE] = part.astype(bf16)


def pack_units(gate_up, down):
    rows, columns = gate_up.shape[1:]
    steps = -(-columns // TILE)
    vmem = pl.BlockSpec(memory_space=pltpu.VMEM)
    return pl.pallas_call(
        pack_units_kernel,
        in_specs=[vmem, vmem],
        out_specs=vmem,
        out_shape=jax.ShapeDtypeStruct((rows, steps * 3 * TILE), bf16),
        compiler_params=pltpu.CompilerParams(vmem_limit_bytes=VMEM_LIMIT),
        cost_estimate=SMALL,
    )(gate_up, down)


def adam_kernel(weight_ref, first_ref, second_ref, sum_ref, *out_refs):
    parts = weight_ref.shape[0]
    groups = sum_ref.shape[1] // (parts * TILE)
    for p in range(parts):
        for k in range(groups):
            columns = slice(k * TILE, (k + 1) * TILE)
            at_sum = (k * parts + p) * TILE
            new = adam_step(
                weight_ref[p, :, columns],
                first_ref[p, :, columns],
                second_ref[p, :, columns],
                sum_ref[:, at_sum : at_sum + TILE].astype(f32),
                rate_matrix,
                decay_matrix,
            )
            for ref, value in zip(out_refs, new):
                ref[p, :, columns] = value


def adam_units(weight, first, second, summed, begin):
    parts, rows, columns = weight.shape
    groups = 2
    state = pl.BlockSpec((parts, rows, groups * TILE), lambda i: (0, 0, i))
    wide = parts * groups * TILE
    return pl.pallas_call(
        adam_kernel,
        grid=(-(-columns // (groups * TILE)),),
        in_specs=[state] * 3 + [pl.BlockSpec((rows, wide), lambda i: (0, begin // wide + i))],
        out_specs=(state,) * 3,
        out_shape=(jax.ShapeDtypeStruct(weight.shape, f32),) * 3,
        compiler_params=pltpu.CompilerParams(vmem_limit_bytes=VMEM_LIMIT),
        cost_estimate=SMALL,
    )(weight, first, second, summed)


def units_forward_kernel(count, *refs):
    row_refs, grad_refs, units_ref = refs[:count], refs[count : 2 * count], refs[2 * count]
    rows_out, grads_out, hidden_ref, both_ref = refs[-4:]

    @pl.when(pl.program_id(0) == 0)
    def _():
        for k in range(count):
            part = pl.ds(k * row_refs[k].shape[0], row_refs[k].shape[0])
            rows_out[part, :] = row_refs[k][...]
            grads_out[part, :] = grad_refs[k][...]

    rows = rows_out[...]
    gate_out = dot(rows, units_ref[:, :TILE], 1, 0)
    up_out = dot(rows, units_ref[:, TILE : 2 * TILE], 1, 0)
    grad_hidden = dot(grads_out[...], units_ref[:, 2 * TILE :], 1, 0)
    gate_sig = jax.nn.sigmoid(gate_out)
    gate_act = gate_out * gate_sig
    hidden_ref[...] = (gate_act * up_out).astype(bf16)
    both_ref[:, :TILE] = (
        grad_hidden * up_out * (gate_sig + gate_act * (1.0 - gate_sig))
    ).astype(bf16)
    both_ref[:, TILE:] = (grad_hidden * gate_act).astype(bf16)


def units_forward(rows, grads, units, buffers, index):
    count, (length, width) = len(rows), rows[0].shape
    steps = units.shape[1] // (3 * TILE)
    full = pl.BlockSpec((length, width), lambda i: (0, 0))
    kept = pl.BlockSpec((count * length, width), lambda i: (index, 0))
    held = () if buffers is None else buffers
    return pl.pallas_call(
        functools.partial(units_forward_kernel, count),
        grid=(steps,),
        in_specs=[full] * (2 * count)
        + [pl.BlockSpec((width, 3 * TILE), lambda i: (0, i))]
        + [pl.BlockSpec(memory_space=pl.ANY)] * len(held),
        out_specs=(
            kept,
            kept,
            pl.BlockSpec((count * length, TILE), lambda i: (index, i)),
            pl.BlockSpec((count * length, 2 * TILE), lambda i: (index, i)),
        ),
        out_shape=(
            jax.ShapeDtypeStruct((4 * length, width), bf16),
            jax.ShapeDtypeStruct((4 * length, width), bf16),
            jax.ShapeDtypeStruct((4 * length, steps * TILE), bf16),
            jax.ShapeDtypeStruct((4 * length, steps * 2 * TILE), bf16),
        ),
        input_output_aliases={2 * count + 1 + k: k for k in range(len(held))},
        compiler_params=pltpu.CompilerParams(vmem_limit_bytes=VMEM_LIMIT),
        cost_estimate=SMALL,
    )(*rows, *grads, units, *held)


def units_back_kernel(both_ref, units_ref, out_ref):
    total = None
    for i in range(both_ref.shape[1] // (2 * TILE)):
        term = dot(
            both_ref[:, i * 2 * TILE : (i + 1) * 2 * TILE],
            units_ref[:, i * 3 * TILE : (i * 3 + 2) * TILE],
            1,
            1,
        )
        total = term if total is None else total + term
    out_ref[...] = total.astype(bf16)


def units_down_kernel(hidden_ref, units_ref, out_ref):
    total = None
    for i in range(hidden_ref.shape[1] // TILE):
        term = dot(
            hidden_ref[:, i * TILE : (i + 1) * TILE],
            units_ref[:, (i * 3 + 2) * TILE : (i * 3 + 3) * TILE],
            1,
            1,
        )
        total = term if total is None else total + term
    out_ref[...] = total.astype(bf16)


def units_to_width(kernel, values, units, first, count):
    width = units.shape[0]
    block, columns = values.shape[0] // 4, values.shape[1]
    length = block * count
    return pl.pallas_call(
        kernel,
        grid=(width // TILE,),
        in_specs=[
            pl.BlockSpec((length, columns), lambda i: (first // count, 0)),
            pl.BlockSpec((TILE, units.shape[1]), lambda i: (i, 0)),
        ],
        out_specs=pl.BlockSpec((length, TILE), lambda i: (0, i)),
        out_shape=jax.ShapeDtypeStruct((length, width), bf16),
        compiler_params=pltpu.CompilerParams(vmem_limit_bytes=VMEM_LIMIT),
        cost_estimate=SMALL,
    )(values, units)


def units_add_kernel(*refs):
    out_ref = refs[-1]
    begin = 0
    for kept_ref, other_ref in zip(refs[0:-1:2], refs[1:-1:2]):
        columns = kept_ref.shape[2]
        out_ref[0, :, begin : begin + columns] = (
            kept_ref[0].astype(f32) + other_ref[0].astype(f32)
        ).astype(bf16)
        begin += columns


def units_add(*values):
    pairs, rows, _ = values[0].shape
    columns = sum(value.shape[2] for value in values[::2])
    return pl.pallas_call(
        units_add_kernel,
        grid=(pairs,),
        in_specs=[
            pl.BlockSpec((1, rows, value.shape[2]), lambda i: (i, 0, 0)) for value in values
        ],
        out_specs=pl.BlockSpec((1, rows, columns), lambda i: (i, 0, 0)),
        out_shape=jax.ShapeDtypeStruct((pairs, rows, columns), bf16),
        compiler_params=pltpu.CompilerParams(vmem_limit_bytes=VMEM_LIMIT),
        cost_estimate=SMALL,
    )(*values)


def units_gradient_kernel(core_ref, left_ref, right_ref, kept_ref, given_ref, total_ref):
    total_ref[...] = dot(left_ref[...], right_ref[...], 0, 0)
    core = core_ref[0]
    pairs, rows, _ = kept_ref.shape
    for p in range(pairs):
        for c, ref in ((core, kept_ref), (1 - core, given_ref)):
            at_row = pl.multiple_of((2 * p + c) * rows, 16)
            ref[p] = total_ref[pl.ds(at_row, rows), :].astype(bf16)


def units_gradient_parts(left, right, core):
    length, width = left.shape
    columns = right.shape[1]
    count = lax.axis_size("dp")
    rows = width // count
    tile = 2 * TILE if columns % (2 * TILE) == 0 else TILE
    out = pl.BlockSpec((count // 2, rows, tile), lambda i, c: (0, 0, i))
    shape = jax.ShapeDtypeStruct((count // 2, rows, columns), bf16)
    return pl.pallas_call(
        units_gradient_kernel,
        grid_spec=pltpu.PrefetchScalarGridSpec(
            num_scalar_prefetch=1,
            grid=(columns // tile,),
            in_specs=[
                pl.BlockSpec((length, width), lambda i, c: (0, 0)),
                pl.BlockSpec((length, tile), lambda i, c: (0, i)),
            ],
            out_specs=(out, out),
            scratch_shapes=[pltpu.VMEM((width, tile), f32)],
        ),
        out_shape=(shape, shape),
        compiler_params=pltpu.CompilerParams(vmem_limit_bytes=VMEM_LIMIT),
        cost_estimate=SMALL,
    )(core[None], left, right)


def swap_core(value):
    count = lax.axis_size("dp")
    return lax.ppermute(value, "dp", [(i, i ^ 1) for i in range(count)])


def swap_near(value):
    return lax.ppermute(value, "tensor", [(0, 1), (1, 0), (2, 3), (3, 2)])


def swap_far(value):
    return lax.ppermute(value, "tensor", [(0, 2), (2, 0), (1, 3), (3, 1)])


def swap_middle(value):
    return lax.ppermute(value, "tensor", [(1, 2), (2, 1)])


def swap_opposite(value):
    return lax.ppermute(value, "tensor", [(i, 3 - i) for i in range(4)])


def to_ends(value):
    return lax.ppermute(value, "tensor", [(1, 0), (2, 3)])


def from_ends(value):
    return lax.ppermute(value, "tensor", [(0, 1), (3, 2)])


def device_of(pair, core, z):
    return (2 * pair + core) * 4 + z


def owner_swap(value):
    perm = []
    for p in range(lax.axis_size("dp") // 2):
        for z in range(4):
            own = z // 2
            perm.append((device_of(p, own, z), device_of(p, own, z ^ 1)))
            perm.append((device_of(p, 1 - own, z), device_of(p, own, z ^ 2)))
    return lax.ppermute(value, AXES, perm)


def guest_swap(value):
    perm = []
    for p in range(lax.axis_size("dp") // 2):
        for z in range(4):
            guest = 1 - z // 2
            perm.append((device_of(p, guest, z), device_of(p, guest, z ^ 1)))
    return lax.ppermute(value, AXES, perm)


def heads_scatter_near(mine, other, z):
    def term(index):
        return at(mine, index, 0).astype(f32) + at(other, index, 0).astype(f32)

    away = swap_near(term(z ^ 3).astype(bf16))
    return term(z), term(z ^ 2), swap_near(term(z ^ 1).astype(bf16)), away


def heads_scatter_end(home, far, own, core):
    kept = jnp.where(own, home, far.astype(f32))
    given = swap_core(jnp.where(own, far, home.astype(bf16))).astype(f32)
    return jnp.concatenate(
        [jnp.where(core == 0, kept, given), jnp.where(core == 0, given, kept)], axis=0
    )


def gather_dp(value):
    bit = 1
    while bit < lax.axis_size("dp"):
        other = swap_dp(value, bit)
        upper = (lax.axis_index("dp") & bit) != 0
        value = jnp.concatenate(
            [jnp.where(upper, other, value), jnp.where(upper, value, other)], axis=0
        )
        bit *= 2
    return value


def gather_tensor(value, bit):
    other = lax.ppermute(value, "tensor", [(i, i ^ bit) for i in range(4)])
    upper = (lax.axis_index("tensor") & bit) != 0
    return jnp.concatenate(
        [jnp.where(upper, other, value), jnp.where(upper, value, other)], axis=1
    )


def sum_dp(value, first, last):
    bit = first
    while bit < last:
        value = value + swap_dp(value, bit)
        bit *= 2
    return value


def pair_groups():
    count = lax.axis_size("dp")
    return [list(range(c, count, 2)) for c in range(2)]


def swap_dp(value, mask):
    count = lax.axis_size("dp")
    return lax.ppermute(value, "dp", [(i, i ^ mask) for i in range(count)])


def gather_pairs_begin(value):
    if lax.axis_size("dp") != 8:
        return (lax.all_gather(value, "dp", axis=0, tiled=True, axis_index_groups=pair_groups()),)
    return value, swap_dp(value, 2), swap_dp(value, 4)


def gather_pairs_end(parts):
    if len(parts) == 1:
        return parts, jnp.zeros((1,), jnp.int32)
    value, by_two, by_four = parts
    pair = lax.axis_index("dp") >> 1
    rows = value.shape[0]
    half = rows // 2
    low, high = swap_dp(by_four[:half], 2), swap_dp(by_two[half:], 4)
    begins = jnp.stack([pair, pair ^ 1, pair ^ 2, pair ^ 3, pair ^ 3]) * rows
    begins = begins + jnp.array([0, 0, 0, 0, half], jnp.int32)
    return (value, by_two, by_four, low, high), begins


def at(value, index, axis):
    return lax.dynamic_index_in_dim(value, index, axis, keepdims=False)


def add_low(left, right):
    return (left.astype(f32) + right.astype(f32)).astype(bf16)


def scatter_pairs_begin(value):
    if lax.axis_size("dp") != 8:
        return (
            lax.psum_scatter(
                value, "dp", scatter_dimension=0, tiled=True, axis_index_groups=pair_groups()
            ),
        )
    pair = lax.axis_index("dp") >> 1
    one, two = pair & 1, pair >> 1
    rows = value.shape[0] // 8
    parts = value.reshape((2, 2, 2, rows) + value.shape[1:])
    first, second = parts[:, :, 0], parts[:, :, 1]
    by_two = swap_dp(at(first, one ^ 1, 1), 2)
    by_four = swap_dp(at(second, two ^ 1, 0), 4)
    return at(first, one, 1), by_two, at(second, two, 0), by_four


def scatter_pairs_middle(parts):
    if len(parts) == 1:
        return parts
    return add_low(parts[0], parts[1]), add_low(parts[2], parts[3])


def scatter_pairs_end(parts):
    if len(parts) == 1:
        return parts[0]
    pair = lax.axis_index("dp") >> 1
    one, two = pair & 1, pair >> 1
    first, second = parts
    by_four = swap_dp(at(first, two ^ 1, 0), 4)
    by_two = swap_dp(at(second, one ^ 1, 0), 2)
    first = add_low(at(first, two, 0), by_four)
    second = add_low(at(second, one, 0), by_two)
    return jnp.concatenate([first, second], axis=0)


def heads_pair(shard, far, own, core):
    kept = jnp.where(own, shard, far)
    other = swap_core(jnp.where(own, far, shard))
    return jnp.concatenate(
        [jnp.where(core == 0, kept, other), jnp.where(core == 0, other, kept)], axis=0
    )


def heads_home(pair, own, core):
    rows = pair.shape[0] // 2
    kept = jnp.where(core == 0, pair[:rows], pair[rows:])
    other = swap_core(jnp.where(core == 0, pair[rows:], pair[:rows]))
    return jnp.where(own, kept, other), jnp.where(own, other, kept)


def units_gradient(summed):
    return lax.psum_scatter(
        summed.reshape(-1, summed.shape[-1]),
        "dp",
        scatter_dimension=0,
        tiled=True,
        axis_index_groups=pair_groups(),
    )


def together(*values):
    return lax.optimization_barrier(values)


def shards(
    block_in,
    out_grad,
    positions,
    qkv_weight,
    qkv_first,
    qkv_second,
    out_weight,
    out_first,
    out_second,
    gate_up,
    gate_up_first,
    gate_up_second,
    down_weight,
    down_first,
    down_second,
    norm_gains,
    norm_gains_first,
    norm_gains_second,
):
    model_width = block_in.shape[1]
    z = lax.axis_index("tensor")
    core = lax.axis_index("dp") & 1
    own = core == z // 2
    place = jnp.where(own, z, z ^ 2)[None]

    units_columns = gate_up.shape[2]
    qkv_own = qkv_weight.astype(bf16)
    qkv_own, gains_own, positions = together(qkv_own, norm_gains[None], positions)
    qkv_far = swap_far(qkv_own)
    out_own = out_weight.astype(bf16).T
    out_far = swap_far(out_own)
    gains_near = gather_tensor(gather_dp(gains_own)[:, None], 1)
    inverse_in = lax.rsqrt(jnp.mean(block_in * block_in, axis=-1, keepdims=True) + eps_norm)
    scaled_in = block_in * inverse_in
    head_positions = jnp.where(own, positions, swap_core(positions))
    (
        scaled_b,
        qkv_own,
        qkv_far,
        head_positions,
        units_shard,
        grad_own,
        out_own,
        out_far,
        gains_near,
    ) = together(
        scaled_in.astype(bf16),
        qkv_own,
        qkv_far,
        head_positions,
        pack_units(gate_up, down_weight.T),
        out_grad.astype(bf16),
        out_own,
        out_far,
        gains_near,
    )

    scaled_first = owner_swap(scaled_b)
    qkv_parts = gather_pairs_begin(heads_pair(qkv_own, qkv_far, own, core))
    out_parts = gather_pairs_begin(heads_pair(out_own, out_far, own, core))
    gains_all = gather_tensor(gains_near, 2).reshape(1, -1)
    tables = rope_tables(head_positions, HEAD_DIMENSION)
    length = head_positions.shape[0]
    start = jnp.maximum(jnp.arange(length, dtype=jnp.int32) - head_positions, 0)
    start_column = start[:, None]
    scaled_first, qkv_parts, gains_all, units_shard, tables, start_column, grad_own, out_parts = (
        together(
            scaled_first,
            qkv_parts,
            gains_all,
            units_shard,
            tables,
            start_column,
            grad_own,
            out_parts,
        )
    )
    gain_attn = gains_all[:, :model_width]
    gain_q = gains_all[0, model_width : model_width + HEAD_DIMENSION]
    gain_k = gains_all[0, model_width + HEAD_DIMENSION : model_width + 2 * HEAD_DIMENSION]
    kv_local = qkv_weight.shape[1] // ((QUERY_GROUP + 2) * HEAD_DIMENSION)
    head_gains = jnp.concatenate(
        ([gain_q] * QUERY_GROUP + [gain_k, jnp.ones_like(gain_k)]) * kv_local
    )[None]
    gain_ffn = gains_all[:, model_width + 2 * HEAD_DIMENSION :]

    scaled_second = guest_swap(scaled_first)
    scaled_mine = jnp.where(own, scaled_b, scaled_first)
    scaled_other = swap_core(scaled_mine)
    qkv_blocks, qkv_begins = gather_pairs_end(qkv_parts)
    out_blocks, out_begins = gather_pairs_end(out_parts)
    half = grad_own.shape[0] // 2
    grad_far = swap_far(grad_own[:half])
    (
        qkv_blocks,
        scaled_second,
        scaled_mine,
        scaled_other,
        units_shard,
        grad_own,
        grad_far,
        out_blocks,
    ) = together(
        qkv_blocks,
        scaled_second,
        scaled_mine,
        scaled_other,
        units_shard,
        grad_own,
        grad_far,
        out_blocks,
    )

    units = lax.all_gather(units_shard, "dp", axis=0, tiled=True)
    grad_far_rest = swap_far(grad_own[half:])
    grad_near = swap_near(grad_own)
    scaled_next = jnp.where(own, scaled_first, scaled_second)
    scaled_parts = (scaled_mine, scaled_next, scaled_other, swap_core(scaled_next))
    w_qkv, normed_all, projected, queries_b, keys_b, values_b, attended, lse = attention_forward(
        place, scaled_parts, qkv_blocks, qkv_begins, gain_attn, head_gains, tables, start_column
    )
    attended, grad_far, grad_far_rest, grad_near, grad_own = together(
        attended, grad_far, grad_far_rest, grad_near, grad_own
    )
    grad_middle_part = swap_middle(grad_own)
    grad_far = jnp.concatenate([grad_far, grad_far_rest], axis=0)
    w_out, branch_mine, branch_other = attention_branch(
        core[None], out_blocks, out_begins, attended
    )
    branch_mine, branch_other, grad_far = together(
        branch_mine, swap_core(branch_other), grad_far
    )
    home, term_far, near, away = heads_scatter_near(branch_mine, branch_other, z)
    away, term_far, grad_middle_part = together(away, term_far, grad_middle_part)
    far = swap_far((term_far + away.astype(f32)).astype(bf16))
    far, home, near = together(far, home, near)
    middle = block_in + heads_scatter_end(home + near.astype(f32), far, own, core)

    inverse_mid = lax.rsqrt(jnp.mean(middle * middle, axis=-1, keepdims=True) + eps_norm)
    scaled_mid = middle * inverse_mid
    rows_own = (scaled_mid * gain_ffn).astype(bf16)
    rows_far = swap_far(rows_own)
    rows_near = swap_near(rows_own)
    inner = (z == 1) | (z == 2)
    buffers = units_forward((rows_own,), (grad_own,), units, None, 2)
    rows_far, rows_near, rows_own, buffers = together(rows_far, rows_near, rows_own, buffers)
    grad_ends = to_ends(grad_far)
    rows_ends = to_ends(rows_far)
    rows_middle = swap_middle(rows_own)
    buffers = units_forward((rows_near, rows_far), (grad_near, grad_far), units, buffers, 0)
    rows_all, grad_all, hidden_b, dboth = buffers
    back_first = units_to_width(units_back_kernel, dboth, units, 0, 2)
    rows_ends, rows_middle, grad_ends, back_first, buffers = together(
        rows_ends, rows_middle, grad_ends, back_first, buffers
    )
    rows = block_in.shape[0]
    from_near = swap_near(back_first[:rows])
    from_far = swap_far(back_first[rows:])
    rows_last = jnp.where(inner, rows_middle, rows_ends)
    grad_last = jnp.where(inner, grad_middle_part, grad_ends)
    rows_all, grad_all, hidden_b, dboth = units_forward(
        (rows_last,), (grad_last,), units, buffers, 3
    )
    back_second = units_to_width(units_back_kernel, dboth, units, 2, 2)
    from_near, from_far, back_second, rows_all, grad_all, hidden_b, dboth = together(
        from_near, from_far, back_second, rows_all, grad_all, hidden_b, dboth
    )
    from_last = swap_opposite(back_second[rows:])
    back_own = back_second[:rows]
    down_kept, down_given = units_gradient_parts(grad_all, hidden_b, core)
    both_kept, both_given = units_gradient_parts(rows_all, dboth, core)
    from_last, down_kept, down_given, both_kept, both_given = together(
        from_last, down_kept, down_given, both_kept, both_given
    )
    grad_normed_two = (
        back_own.astype(f32)
        + from_near.astype(f32)
        + from_far.astype(f32)
        + from_last.astype(f32)
    )

    grad_gain_ffn = jnp.sum(grad_normed_two * scaled_mid, axis=0)
    weighted = grad_normed_two * gain_ffn
    grad_middle = out_grad + inverse_mid * (
        weighted - scaled_mid * jnp.mean(weighted * scaled_mid, axis=-1, keepdims=True)
    )
    grad_mid_b, grad_gain_ffn, hidden_b, down_kept, down_given, both_kept, both_given = together(
        grad_middle.astype(bf16),
        grad_gain_ffn,
        hidden_b,
        down_kept,
        down_given,
        both_kept,
        both_given,
    )
    grad_mid_first = owner_swap(grad_mid_b)
    units_sum = units_add(both_kept, swap_core(both_given), down_kept, swap_core(down_given))
    down_last = units_to_width(units_down_kernel, hidden_b, units, 3, 1)
    grad_mid_first, down_last, units_sum = together(grad_mid_first, down_last, units_sum)
    units_sum = units_gradient(units_sum)
    grad_mid_second = guest_swap(grad_mid_first)
    branch_ends = from_ends(down_last)
    branch_middle = swap_middle(down_last)
    grad_mid_mine = jnp.where(own, grad_mid_b, grad_mid_first)
    grad_mid_other = swap_core(grad_mid_mine)
    down_rest = units_to_width(units_down_kernel, hidden_b, units, 0, 3)
    down_near, down_far, down_own = (down_rest[k * rows : (k + 1) * rows] for k in range(3))
    (
        grad_mid_second,
        grad_mid_mine,
        grad_mid_other,
        branch_ends,
        branch_middle,
        down_near,
        down_far,
        down_own,
    ) = together(
        grad_mid_second,
        grad_mid_mine,
        grad_mid_other,
        branch_ends,
        branch_middle,
        down_near,
        down_far,
        down_own,
    )
    down_far = add_low(down_far, branch_ends)
    grad_mid_next = jnp.where(own, grad_mid_first, grad_mid_second)
    grad_mid_parts = (grad_mid_mine, grad_mid_next, grad_mid_other, swap_core(grad_mid_next))
    grad_mid_parts, down_far, down_near = together(grad_mid_parts, down_far, down_near)

    branch_far = swap_far(down_far)
    branch_near = swap_near(down_near)
    grad_attended, row_dot, grad_out_w = attention_turn(place, grad_mid_parts, w_out, attended)
    grad_attended, row_dot, grad_out_w = together(grad_attended, row_dot, grad_out_w)
    grad_projected, part_mine, part_other, head_sums, gain_sums = attention_backward(
        core[None],
        queries_b,
        keys_b,
        values_b,
        grad_attended,
        lse,
        row_dot,
        start[None, :],
        projected,
        head_gains,
        *tables,
        w_qkv,
        normed_all,
        gain_attn,
    )
    head_sums = head_sums.reshape(-1, QUERY_GROUP + 2, HEAD_DIMENSION)
    gain_total = jnp.concatenate(
        [
            gain_sums[0],
            jnp.sum(head_sums[:, :QUERY_GROUP], axis=(0, 1)),
            jnp.sum(head_sums[:, QUERY_GROUP], axis=0),
            grad_gain_ffn,
        ]
    )
    (
        grad_projected,
        part_mine,
        part_other,
        gain_total,
        branch_far,
        branch_near,
        grad_out_w,
    ) = together(
        grad_projected,
        part_mine,
        part_other,
        gain_total,
        branch_far,
        branch_near,
        grad_out_w,
    )

    part_other = swap_core(part_other)
    grad_qkv = dot(normed_all, grad_projected, 0, 0).astype(bf16)
    gain_total = sum_dp(gain_total, 1, 2)
    part_mine, part_other, grad_qkv, gain_total, grad_out_w, branch_far = together(
        part_mine, part_other, grad_qkv, gain_total, grad_out_w, branch_far
    )
    home, term_far, near, away = heads_scatter_near(part_mine, part_other, z)
    qkv_parts = scatter_pairs_begin(grad_qkv)
    out_parts = scatter_pairs_begin(grad_out_w)
    gain_total = gain_total + swap_far(gain_total)
    block_out = (
        middle
        + down_own.astype(f32)
        + branch_near.astype(f32)
        + branch_middle.astype(f32)
        + branch_far.astype(f32)
    )
    qkv_parts, out_parts = scatter_pairs_middle(qkv_parts), scatter_pairs_middle(out_parts)
    far_term = (term_far + away.astype(f32)).astype(bf16)
    far_term, qkv_parts, out_parts, gain_total, block_out = together(
        far_term, qkv_parts, out_parts, gain_total, block_out
    )
    far = swap_far(far_term)
    qkv_pair = scatter_pairs_end(qkv_parts)
    out_pair = scatter_pairs_end(out_parts)
    far, home, near, qkv_pair, out_pair, gain_total = together(
        far, home, near, qkv_pair, out_pair, gain_total
    )
    heads_home_own, heads_home_away = heads_home(
        jnp.concatenate([qkv_pair, out_pair], axis=1), own, core
    )
    grad_normed = heads_scatter_end(home + near.astype(f32), far, own, core)
    heads_home_own, heads_home_away, gain_total, grad_normed, units_sum = together(
        heads_home_own, heads_home_away, gain_total, grad_normed, units_sum
    )
    heads_away = swap_far(heads_home_away)
    gain_total = gain_total + swap_near(gain_total)
    gate_up_new = adam_units(gate_up, gate_up_first, gate_up_second, units_sum, 0)
    down_new = adam_units(
        down_weight.T[None],
        down_first.T[None],
        down_second.T[None],
        units_sum,
        2 * units_sum.shape[1] // 3,
    )
    gain_total = sum_dp(gain_total, 2, lax.axis_size("dp"))
    weighted = grad_normed * gain_attn
    in_grad = grad_middle + inverse_in * (
        weighted - scaled_in * jnp.mean(weighted * scaled_in, axis=-1, keepdims=True)
    )
    heads_away, in_grad, gate_up_new, down_new = together(
        heads_away, in_grad, gate_up_new, down_new
    )
    sum_heads = heads_home_own.astype(f32) + heads_away.astype(f32)
    down_new = tuple(value[0].T for value in down_new)
    qkv_columns = qkv_weight.shape[1]
    sum_qkv = sum_heads[:, :qkv_columns]
    sum_out = sum_heads[:, qkv_columns:].T
    gain_count = norm_gains.shape[0]
    gain_at = (lax.axis_index("dp") * 4 + z) * gain_count
    gain_grads = lax.dynamic_slice_in_dim(gain_total, gain_at, gain_count)

    qkv_new = adam_step(qkv_weight, qkv_first, qkv_second, sum_qkv, rate_matrix, decay_matrix)
    out_new = adam_step(out_weight, out_first, out_second, sum_out, rate_output, decay_matrix)
    gains_new = adam_step(
        norm_gains, norm_gains_first, norm_gains_second, gain_grads, rate_gains, 0.0
    )
    return (block_out, in_grad, *qkv_new, *out_new, *gate_up_new, *down_new, *gains_new)


def solution(mesh):
    tokens = P(("dp", "tensor"), None)
    by_rows = (P("dp", "tensor"),) * 3
    by_columns = (P("tensor", "dp"),) * 3
    stacked = (P(None, "dp", "tensor"),) * 3
    gains = (P(("dp", "tensor")),) * 3
    states = by_rows + by_columns + stacked + by_columns + gains
    return jax.shard_map(
        shards,
        mesh=mesh,
        in_specs=(tokens, tokens, P("dp")) + states,
        out_specs=(tokens, tokens) + states,
        check_vma=False,
    )
```

```python
import functools

import jax
import jax.numpy as jnp
from jax import lax
from jax.experimental import pallas as pl
from jax.experimental.pallas import tpu as pltpu
from jax.sharding import PartitionSpec as P

HEAD_DIMENSION = 64
STEP = 10
QUERY_GROUP = 3
AXES = ("dp", "tensor")

eps_norm = 1e-05
rope_base = 1000000.0
beta_one = 0.9
beta_two = 0.999
adam_eps = 1e-08
decay_matrix = 0.1
rate_matrix = 0.03
rate_output = 0.15
rate_gains = 0.8
bf16 = jnp.bfloat16
f32 = jnp.float32
VMEM_LIMIT = 58 * 1024 * 1024
SMALL = pl.CostEstimate(flops=1000, bytes_accessed=1000, transcendentals=0)


def whole(value):
    zeros = (0,) * len(value.shape)
    return pl.BlockSpec(value.shape, lambda i: zeros, pipeline_mode=pl.Buffered(1))


def scalars(count):
    return [pl.BlockSpec(memory_space=pltpu.SMEM)] * count


def dot(left, right, left_dim, right_dim):
    return lax.dot_general(
        left, right, (((left_dim,), (right_dim,)), ((), ())), preferred_element_type=f32
    )


def norm_rows(row_block, gain_vec):
    inverse = lax.rsqrt(jnp.mean(row_block * row_block, axis=-1, keepdims=True) + eps_norm)
    return row_block * inverse * gain_vec


def rope_tables(positions, head_size):
    inverse_freq = rope_base ** (-(jnp.arange(head_size // 2, dtype=f32) * 2.0) / head_size)
    angles = positions.astype(f32)[:, None] * inverse_freq[None, :]
    cos_part, sin_part = jnp.cos(angles), jnp.sin(angles)
    return (
        jnp.concatenate([cos_part] * 4, axis=1),
        jnp.concatenate([-sin_part, sin_part] * 2, axis=1),
    )


def adam_step(weight, first_old, second_old, gradient, step_rate, decay_rate):
    first_new = beta_one * first_old + (1.0 - beta_one) * gradient
    second_new = beta_two * second_old + (1.0 - beta_two) * gradient * gradient
    fix_one = 1.0 - beta_one**STEP
    fix_two = 1.0 - beta_two**STEP
    update = first_new / fix_one / (jnp.sqrt(second_new / fix_two) + adam_eps)
    return (weight - step_rate * (update + decay_rate * weight), first_new, second_new)


PAIR = 2 * HEAD_DIMENSION


def lanes_of(value):
    return lax.broadcasted_iota(jnp.int32, value.shape, 1)


def swap_halves(value):
    half = HEAD_DIMENSION // 2
    low = lanes_of(value) % HEAD_DIMENSION < half
    return jnp.where(low, pltpu.roll(value, PAIR - half, 1), pltpu.roll(value, half, 1))


def two_parts(value):
    high = value.astype(bf16)
    return high, (value - high.astype(f32)).astype(bf16)


def head_means(value):
    shape = (PAIR, PAIR)
    one, two = (lax.broadcasted_iota(jnp.int32, shape, d) // HEAD_DIMENSION for d in (0, 1))
    weights = jnp.where(one == two, 1.0 / HEAD_DIMENSION, 0.0).astype(bf16)
    high, low = two_parts(value)
    return dot(high, weights, 1, 0) + dot(low, weights, 1, 0)


def is_value(index, value):
    at_head = [(2 * index + k) % (QUERY_GROUP + 2) == QUERY_GROUP + 1 for k in range(2)]
    if not any(at_head):
        return None
    return (lanes_of(value) < HEAD_DIMENSION) == at_head[0]


def unless(mask, value, other):
    return value if mask is None else jnp.where(mask, other, value)


def as_row(column):
    return jnp.broadcast_to(column, (column.shape[0], 128)).T[:1, :]


def as_column(row):
    return jnp.broadcast_to(row, (128, row.shape[1])).T[:, :1]


def place_parts(place_ref, part_refs, whole_ref, scale):
    rows = part_refs[0].shape[0]
    for j, part_ref in enumerate(part_refs):
        at_row = pl.multiple_of((j ^ place_ref[0]) * rows, rows)
        value = part_ref[...]
        if scale is not None:
            value = (value.astype(f32) * scale).astype(bf16)
        whole_ref[pl.ds(at_row, rows), :] = value


def split_halves(core_ref, value, stage_ref, mine_ref, other_ref, index):
    half = value.shape[0] // 2
    stage_ref[...] = value
    core = core_ref[0]
    mine_ref[index] = stage_ref[pl.ds(pl.multiple_of(core * half, half), half), :]
    other_ref[index] = stage_ref[pl.ds(pl.multiple_of((1 - core) * half, half), half), :]


def place_blocks(begins_ref, block_refs, whole_ref):
    for k, block_ref in enumerate(block_refs):
        begin = pl.multiple_of(begins_ref[k], 16)
        whole_ref[pl.ds(begin, block_ref.shape[0]), :] = block_ref[...]


def attention_forward_kernel(count, place_ref, begins_ref, *refs):
    part_refs, refs = refs[:4], refs[4:]
    block_refs, refs = refs[:count], refs[count:]
    (
        gain_ref,
        head_gain_ref,
        cos_ref,
        sin_ref,
        start_ref,
        weight_ref,
        normed_ref,
        projected_ref,
        q_ref,
        k_ref,
        v_ref,
        out_ref,
        lse_ref,
    ) = refs
    place_blocks(begins_ref, block_refs, weight_ref)
    size = HEAD_DIMENSION
    heads, length, _ = q_ref.shape
    group = QUERY_GROUP
    kv = heads // group
    block = min(256, length)
    place_parts(place_ref, part_refs, normed_ref, gain_ref[...])
    for i in range(length // block):
        here = pl.ds(i * block, block)
        projected = dot(normed_ref[here, :], weight_ref[:, : projected_ref.shape[1]], 1, 0)
        projected_ref[here, :] = projected
        cos_part, sin_part = cos_ref[here, :], sin_ref[here, :]
        for t in range(projected.shape[1] // PAIR):
            raw = projected[:, t * PAIR : (t + 1) * PAIR]
            keep = is_value(t, raw)
            inverse = unless(keep, lax.rsqrt(head_means(raw * raw) + eps_norm), 1.0)
            normed = raw * inverse * head_gain_ref[:, t * PAIR : (t + 1) * PAIR]
            turned = normed * unless(keep, cos_part, 1.0) + swap_halves(normed) * unless(
                keep, sin_part, 0.0
            )
            turned = turned.astype(bf16)
            for k in range(2):
                j, g = divmod(2 * t + k, group + 2)
                piece = turned[:, k * size : (k + 1) * size]
                if g < group:
                    q_ref[j * group + g, here, :] = piece * jnp.asarray(size**-0.5, bf16)
                elif g == group:
                    k_ref[j, here, :] = piece
                else:
                    v_ref[j, here, :] = piece
    row_at = lax.broadcasted_iota(jnp.int32, (block, block), 0)
    col_at = lax.broadcasted_iota(jnp.int32, (block, block), 1)
    causal = jnp.concatenate([col_at <= row_at] * group, axis=0)
    col_all = lax.broadcasted_iota(jnp.int32, (group * block, block), 1).astype(f32)
    ones = jnp.ones((block, size), bf16)
    for j in range(kv):
        for i in range(length // block):
            here = pl.ds(i * block, block)
            queries = jnp.concatenate(
                [q_ref[j * group + g, here, :] for g in range(group)], axis=0
            )
            start = jnp.concatenate([as_column(start_ref[:, here])] * group, axis=0)
            total = jnp.zeros((group * block, 2 * size), f32)
            for b in range(i + 1):
                there = pl.ds(b * block, block)
                scores = dot(queries, k_ref[j, there, :], 1, 1)
                allowed = col_all >= start - b * block
                if b == i:
                    allowed = allowed & causal
                weights = jnp.where(allowed, jnp.exp(scores), 0.0).astype(bf16)
                values = jnp.concatenate([v_ref[j, there, :], ones], axis=1)
                total = total + dot(weights, values, 1, 0)
            row_sum = total[:, size : size + 1]
            output = (total[:, :size] / row_sum).astype(bf16)
            log_sum = jnp.log(row_sum)
            for g in range(group):
                h = j * group + g
                part = slice(g * block, (g + 1) * block)
                out_ref[here, h * size : (h + 1) * size] = output[part]
                lse_ref[h, :, here] = as_row(log_sum[part])


def attention_branch_kernel(core_ref, attended_ref, weight_ref, mine_ref, other_ref, stage_ref):
    shard, columns = attended_ref.shape[0] // 4, attended_ref.shape[1]
    for i in range(4):
        value = dot(
            attended_ref[i * shard : (i + 1) * shard, :], weight_ref[:, -columns:], 1, 1
        )
        split_halves(core_ref, value.astype(bf16), stage_ref, mine_ref, other_ref, i)


def attention_forward(place, parts, blocks, begins, gain_attn, head_gains, tables, start):
    rows, width = parts[0].shape
    length = 4 * rows
    size = HEAD_DIMENSION
    columns = blocks[0].shape[1]
    kv = columns // ((2 * QUERY_GROUP + 2) * size)
    heads = kv * QUERY_GROUP
    operands = (*parts, *blocks, gain_attn, head_gains, *tables, start)
    results = (
        jax.ShapeDtypeStruct((width, columns), bf16),
        jax.ShapeDtypeStruct((length, width), bf16),
        jax.ShapeDtypeStruct((length, (heads + 2 * kv) * size), f32),
        jax.ShapeDtypeStruct((heads, length, size), bf16),
        jax.ShapeDtypeStruct((kv, length, size), bf16),
        jax.ShapeDtypeStruct((kv, length, size), bf16),
        jax.ShapeDtypeStruct((length, heads * size), bf16),
        jax.ShapeDtypeStruct((heads, 1, length), f32),
    )
    return pl.pallas_call(
        functools.partial(attention_forward_kernel, len(blocks)),
        grid=(1,),
        in_specs=scalars(2) + [whole(value) for value in operands],
        out_specs=tuple(whole(value) for value in results),
        out_shape=results,
        compiler_params=pltpu.CompilerParams(vmem_limit_bytes=VMEM_LIMIT),
        cost_estimate=SMALL,
    )(place, begins, *operands)


def attention_branch(core, attended, weight):
    length = attended.shape[0]
    width = weight.shape[0]
    half = jax.ShapeDtypeStruct((4, length // 8, width), bf16)
    return pl.pallas_call(
        attention_branch_kernel,
        grid=(1,),
        in_specs=scalars(1) + [whole(attended), whole(weight)],
        out_specs=(whole(half), whole(half)),
        out_shape=(half, half),
        scratch_shapes=[pltpu.VMEM((length // 4, width), bf16)],
        compiler_params=pltpu.CompilerParams(vmem_limit_bytes=VMEM_LIMIT),
        cost_estimate=SMALL,
    )(core, attended, weight)


def split_pieces(total_ref, pair_ref, piece_refs):
    if len(piece_refs) == 1:
        piece_refs[0][...] = total_ref[...].astype(bf16)
        return
    keep_x, send_x, keep_y, send_y = piece_refs
    rows = keep_x.shape[1]
    x, y = pair_ref[0], pair_ref[1]
    for k in range(2):
        for ref, pair, core in (
            (keep_x, 2 * k + x, 0),
            (send_x, 2 * k + 1 - x, 0),
            (keep_y, 2 * y + k, 1),
            (send_y, 2 * (1 - y) + k, 1),
        ):
            begin = pl.multiple_of((2 * pair + core) * rows, 16)
            ref[k] = total_ref[pl.ds(begin, rows), :].astype(bf16)


def pieces_shapes(width, columns):
    if lax.axis_size("dp") != 8:
        return (jax.ShapeDtypeStruct((width, columns), bf16),)
    return (jax.ShapeDtypeStruct((2, width // 8, columns), bf16),) * 4


def heads_gradient_kernel(pair_ref, left_ref, right_ref, *refs):
    refs[-1][...] = dot(left_ref[...], right_ref[...], 0, 0)
    split_pieces(refs[-1], pair_ref, refs[:-1])


def heads_gradient(pair, left, right):
    width, columns = left.shape[1], right.shape[1]
    results = pieces_shapes(width, columns)
    return pl.pallas_call(
        heads_gradient_kernel,
        grid=(1,),
        in_specs=scalars(1) + [whole(left), whole(right)],
        out_specs=tuple(whole(value) for value in results),
        out_shape=results,
        scratch_shapes=[pltpu.VMEM((width, columns), f32)],
        compiler_params=pltpu.CompilerParams(vmem_limit_bytes=VMEM_LIMIT),
        cost_estimate=SMALL,
    )(pair, left, right)


def add_refs(left, right):
    return (left.astype(f32) + right.astype(f32)).astype(bf16)


def pieces_middle_kernel(
    pair_ref, keep_x, got_x, keep_y, got_y, keep_one, send_one, keep_two, send_two
):
    x, y = pair_ref[0], pair_ref[1]
    keep_one[...] = add_refs(keep_x[y], got_x[y])
    send_one[...] = add_refs(keep_x[1 - y], got_x[1 - y])
    keep_two[...] = add_refs(keep_y[x], got_y[x])
    send_two[...] = add_refs(keep_y[1 - x], got_y[1 - x])


def pieces_end_kernel(core_ref, keep_one, got_one, keep_two, got_two, kept, given):
    @pl.when(core_ref[0] == 0)
    def _():
        kept[...] = add_refs(keep_one[...], got_one[...])
        given[...] = add_refs(keep_two[...], got_two[...])

    @pl.when(core_ref[0] != 0)
    def _():
        given[...] = add_refs(keep_one[...], got_one[...])
        kept[...] = add_refs(keep_two[...], got_two[...])


def pieces_call(kernel, scalar, values, count):
    result = jax.ShapeDtypeStruct(values[0].shape[-2:], bf16)
    vmem = pl.BlockSpec(memory_space=pltpu.VMEM)
    return pl.pallas_call(
        kernel,
        in_specs=scalars(1) + [vmem] * len(values),
        out_specs=(vmem,) * count,
        out_shape=(result,) * count,
        compiler_params=pltpu.CompilerParams(vmem_limit_bytes=VMEM_LIMIT),
        cost_estimate=SMALL,
    )(scalar, *values)


def attention_turn_kernel(place_ref, pair_ref, *refs):
    part_refs, (weight_ref, out_ref, grads_ref, dot_ref) = refs[:4], refs[4:8]
    piece_refs, (whole_ref, total_ref) = refs[8:-2], refs[-2:]
    size = HEAD_DIMENSION
    place_parts(place_ref, part_refs, whole_ref, None)
    heads, length, _ = grads_ref.shape
    block = min(256, length)
    shape = (dot_ref.shape[0], heads * size)
    of_head = (
        lax.broadcasted_iota(jnp.int32, shape, 0)
        == lax.broadcasted_iota(jnp.int32, shape, 1) // size
    ).astype(bf16)
    for i in range(length // block):
        here = pl.ds(i * block, block)
        grads = dot(whole_ref[here, :], weight_ref[:, -heads * size :], 1, 0).astype(bf16)
        high, low = two_parts(grads.astype(f32) * out_ref[here, :].astype(f32))
        dot_ref[:, here] = dot(of_head, high, 1, 1) + dot(of_head, low, 1, 1)
        for h in range(heads):
            grads_ref[h, here, :] = grads[:, h * size : (h + 1) * size]
    total_ref[...] = dot(whole_ref[...], out_ref[...], 0, 0)
    split_pieces(total_ref, pair_ref, piece_refs)


def attention_turn(place, pair, parts, weight, attended):
    rows, width = parts[0].shape
    length, columns = attended.shape
    heads = columns // HEAD_DIMENSION
    operands = (*parts, weight, attended)
    results = (
        jax.ShapeDtypeStruct((heads, length, HEAD_DIMENSION), bf16),
        jax.ShapeDtypeStruct((-(-heads // 8) * 8, length), f32),
        *pieces_shapes(width, columns),
    )
    return pl.pallas_call(
        attention_turn_kernel,
        grid=(1,),
        in_specs=scalars(2) + [whole(value) for value in operands],
        out_specs=tuple(whole(value) for value in results),
        out_shape=results,
        scratch_shapes=[pltpu.VMEM((length, width), bf16), pltpu.VMEM((width, columns), f32)],
        compiler_params=pltpu.CompilerParams(vmem_limit_bytes=VMEM_LIMIT),
        cost_estimate=SMALL,
    )(place, pair, *operands)


def attention_backward_kernel(
    core_ref,
    q_ref,
    k_ref,
    v_ref,
    g_ref,
    lse_ref,
    dot_ref,
    start_ref,
    projected_ref,
    head_gain_ref,
    cos_ref,
    sin_ref,
    weight_ref,
    normed_ref,
    gain_ref,
    back_ref,
    mine_ref,
    other_ref,
    head_sum_ref,
    gain_sum_ref,
    grad_ref,
    dk_ref,
    dv_ref,
    stage_ref,
):
    size = HEAD_DIMENSION
    heads, length, _ = q_ref.shape
    group = QUERY_GROUP
    kv = heads // group
    block = min(256, length)
    lanes = group * block
    key_at = lax.broadcasted_iota(jnp.int32, (block, block), 0)
    row_at = lax.broadcasted_iota(jnp.int32, (block, block), 1)
    causal = jnp.concatenate([key_at <= row_at] * group, axis=1)
    key_all = lax.broadcasted_iota(jnp.int32, (block, lanes), 0).astype(f32)
    dk_ref[...] = jnp.zeros_like(dk_ref)
    dv_ref[...] = jnp.zeros_like(dv_ref)
    head_sum_ref[...] = jnp.zeros_like(head_sum_ref)
    gain_sum_ref[...] = jnp.zeros_like(gain_sum_ref)
    for j in range(kv):
        for i in range(length // block):
            here = pl.ds(i * block, block)
            head = [j * group + g for g in range(group)]
            queries = jnp.concatenate([q_ref[h, here, :] for h in head], axis=0)
            grads = jnp.concatenate([g_ref[h, here, :] for h in head], axis=0)
            lse = jnp.concatenate([lse_ref[h, :, here] for h in head], axis=1)
            row_dot = jnp.concatenate([dot_ref[h : h + 1, here] for h in head], axis=1)
            start = jnp.concatenate([start_ref[:, here]] * group, axis=1)
            dq = jnp.zeros((size, lanes), f32)
            for b in range(i + 1):
                there = pl.ds(b * block, block)
                keys = k_ref[j, there, :]
                scores = dot(keys, queries, 1, 1)
                allowed = key_all >= start - b * block
                if b == i:
                    allowed = allowed & causal
                probs = jnp.where(allowed, jnp.exp(scores - lse), 0.0)
                grad_probs = dot(v_ref[j, there, :], grads, 1, 1)
                grad_scores = (probs * (grad_probs - row_dot)).astype(bf16)
                dv_ref[j, there, :] += dot(probs.astype(bf16), grads, 1, 0)
                dk_ref[j, there, :] += dot(grad_scores, queries, 1, 0)
                dq = dq + dot(keys, grad_scores, 0, 0)
            for g in range(group):
                column = (j * (group + 2) + g) * size
                grad_ref[here, column : column + size] = (
                    dq[:, g * block : (g + 1) * block].T * size**-0.5
                )
        key_column = (j * (group + 2) + group) * size
        grad_ref[:, key_column : key_column + size] = dk_ref[j]
        grad_ref[:, key_column + size : key_column + 2 * size] = dv_ref[j]
    shard = length // 4
    for i in range(4):
        here = pl.ds(i * shard, shard)
        cos_part, sin_part = cos_ref[here, :], sin_ref[here, :]
        for t in range(back_ref.shape[1] // PAIR):
            columns = slice(t * PAIR, (t + 1) * PAIR)
            given = grad_ref[here, columns]
            keep = is_value(t, given)
            grad = given * unless(keep, cos_part, 1.0) + swap_halves(
                given * unless(keep, sin_part, 0.0)
            )
            raw = projected_ref[here, columns]
            inverse = lax.rsqrt(head_means(raw * raw) + eps_norm)
            scaled = raw * inverse
            head_sum_ref[:, columns] += jnp.sum(grad * scaled, axis=0, keepdims=True)
            weighted = grad * head_gain_ref[:, columns]
            back = inverse * (weighted - scaled * head_means(weighted * scaled))
            back_ref[here, columns] = unless(keep, back, given).astype(bf16)
        term = dot(back_ref[here, :], weight_ref[:, : back_ref.shape[1]], 1, 1)
        gain_sum_ref[...] += jnp.sum(
            term * normed_ref[here, :].astype(f32), axis=0, keepdims=True
        )
        split_halves(core_ref, term.astype(bf16), stage_ref, mine_ref, other_ref, i)
    gain_sum_ref[...] = gain_sum_ref[...] / gain_ref[...]


def attention_backward(core, queries, keys, values, grads, lse, row_dot, start, projected, *rest):
    heads, length, size = queries.shape
    kv = keys.shape[0]
    normed = rest[-2]
    width = normed.shape[1]
    half = jax.ShapeDtypeStruct((4, length // 8, width), bf16)
    operands = (queries, keys, values, grads, lse, row_dot, start, projected) + rest
    results = (
        jax.ShapeDtypeStruct(projected.shape, bf16),
        half,
        half,
        jax.ShapeDtypeStruct((1, projected.shape[1]), f32),
        jax.ShapeDtypeStruct((1, width), f32),
    )
    return pl.pallas_call(
        attention_backward_kernel,
        grid=(1,),
        in_specs=scalars(1) + [whole(value) for value in operands],
        out_specs=tuple(whole(value) for value in results),
        out_shape=results,
        scratch_shapes=[
            pltpu.VMEM(projected.shape, f32),
            pltpu.VMEM((kv, length, size), f32),
            pltpu.VMEM((kv, length, size), f32),
            pltpu.VMEM((length // 4, width), bf16),
        ],
        compiler_params=pltpu.CompilerParams(vmem_limit_bytes=VMEM_LIMIT),
        cost_estimate=SMALL,
    )(core, *operands)


def input_gradient_kernel(core_ref, kept_ref, given_ref, rows_ref, gain_ref, middle_ref, out_ref):
    half = kept_ref.shape[0]
    core = core_ref[0]
    for index, ref in ((core, kept_ref), (1 - core, given_ref)):
        part = pl.ds(pl.multiple_of(index * half, half), half)
        rows = rows_ref[part, :]
        inverse = lax.rsqrt(jnp.mean(rows * rows, axis=1, keepdims=True) + eps_norm)
        scaled = rows * inverse
        weighted = ref[...].astype(f32) * gain_ref[...]
        out_ref[part, :] = middle_ref[part, :] + inverse * (
            weighted - scaled * jnp.mean(weighted * scaled, axis=1, keepdims=True)
        )


def input_gradient(core, kept, given, rows, gain, middle):
    vmem = pl.BlockSpec(memory_space=pltpu.VMEM)
    return pl.pallas_call(
        input_gradient_kernel,
        in_specs=scalars(1) + [vmem] * 5,
        out_specs=vmem,
        out_shape=jax.ShapeDtypeStruct(rows.shape, f32),
        compiler_params=pltpu.CompilerParams(vmem_limit_bytes=VMEM_LIMIT),
        cost_estimate=SMALL,
    )(core, kept, given, rows, gain, middle)


TILE = 256


def pack_units_kernel(both_ref, down_ref, out_ref):
    columns = both_ref.shape[2]
    rows = both_ref.shape[1]
    for i in range(out_ref.shape[1] // (3 * TILE)):
        first, last = i * TILE, min(columns, (i + 1) * TILE)
        parts = (both_ref[0, :, first:last], both_ref[1, :, first:last], down_ref[:, first:last])
        for k, part in enumerate(parts):
            if last - first < TILE:
                part = jnp.concatenate(
                    [part, jnp.zeros((rows, TILE - (last - first)), f32)], axis=1
                )
            at_column = (3 * i + k) * TILE
            out_ref[:, at_column : at_column + TILE] = part.astype(bf16)


def pack_units(gate_up, down):
    rows, columns = gate_up.shape[1:]
    steps = -(-columns // TILE)
    vmem = pl.BlockSpec(memory_space=pltpu.VMEM)
    return pl.pallas_call(
        pack_units_kernel,
        in_specs=[vmem, vmem],
        out_specs=vmem,
        out_shape=jax.ShapeDtypeStruct((rows, steps * 3 * TILE), bf16),
        compiler_params=pltpu.CompilerParams(vmem_limit_bytes=VMEM_LIMIT),
        cost_estimate=SMALL,
    )(gate_up, down)


def adam_kernel(weight_ref, first_ref, second_ref, sum_ref, *out_refs):
    parts = weight_ref.shape[0]
    groups = sum_ref.shape[1] // (parts * TILE)
    for p in range(parts):
        for k in range(groups):
            columns = slice(k * TILE, (k + 1) * TILE)
            at_sum = (k * parts + p) * TILE
            new = adam_step(
                weight_ref[p, :, columns],
                first_ref[p, :, columns],
                second_ref[p, :, columns],
                sum_ref[:, at_sum : at_sum + TILE].astype(f32),
                rate_matrix,
                decay_matrix,
            )
            for ref, value in zip(out_refs, new):
                ref[p, :, columns] = value


def adam_units(weight, first, second, summed, begin):
    parts, rows, columns = weight.shape
    groups = 2
    state = pl.BlockSpec((parts, rows, groups * TILE), lambda i: (0, 0, i))
    wide = parts * groups * TILE
    return pl.pallas_call(
        adam_kernel,
        grid=(-(-columns // (groups * TILE)),),
        in_specs=[state] * 3 + [pl.BlockSpec((rows, wide), lambda i: (0, begin // wide + i))],
        out_specs=(state,) * 3,
        out_shape=(jax.ShapeDtypeStruct(weight.shape, f32),) * 3,
        compiler_params=pltpu.CompilerParams(vmem_limit_bytes=VMEM_LIMIT),
        cost_estimate=SMALL,
    )(weight, first, second, summed)


def units_forward_kernel(count, pick, pick_ref, *refs):
    row_refs, grad_refs, units_ref = refs[:count], refs[count : 2 * count], refs[2 * count]
    rows_out, grads_out, hidden_ref, both_ref = refs[-4:]

    @pl.when(pl.program_id(0) == 0)
    def _():
        for k in range(count):
            if pick:

                @pl.when(pick_ref[0] == k)
                def _():
                    rows_out[...] = row_refs[k][...]
                    grads_out[...] = grad_refs[k][...]

            else:
                part = pl.ds(k * row_refs[k].shape[0], row_refs[k].shape[0])
                rows_out[part, :] = row_refs[k][...]
                grads_out[part, :] = grad_refs[k][...]

    rows = rows_out[...]
    gate_out = dot(rows, units_ref[:, :TILE], 1, 0)
    up_out = dot(rows, units_ref[:, TILE : 2 * TILE], 1, 0)
    grad_hidden = dot(grads_out[...], units_ref[:, 2 * TILE :], 1, 0)
    gate_sig = jax.nn.sigmoid(gate_out)
    gate_act = gate_out * gate_sig
    hidden_ref[...] = (gate_act * up_out).astype(bf16)
    both_ref[:, :TILE] = (
        grad_hidden * up_out * (gate_sig + gate_act * (1.0 - gate_sig))
    ).astype(bf16)
    both_ref[:, TILE:] = (grad_hidden * gate_act).astype(bf16)


def units_forward(rows, grads, units, buffers, index, pick=None):
    count, (length, width) = len(rows), rows[0].shape
    blocks = count if pick is None else 1
    steps = units.shape[1] // (3 * TILE)
    full = pl.BlockSpec((length, width), lambda i: (0, 0))
    kept = pl.BlockSpec((blocks * length, width), lambda i: (index, 0))
    held = () if buffers is None else buffers
    return pl.pallas_call(
        functools.partial(units_forward_kernel, count, pick is not None),
        grid=(steps,),
        in_specs=scalars(1)
        + [full] * (2 * count)
        + [pl.BlockSpec((width, 3 * TILE), lambda i: (0, i))]
        + [pl.BlockSpec(memory_space=pl.ANY)] * len(held),
        out_specs=(
            kept,
            kept,
            pl.BlockSpec((blocks * length, TILE), lambda i: (index, i)),
            pl.BlockSpec((blocks * length, 2 * TILE), lambda i: (index, i)),
        ),
        out_shape=(
            jax.ShapeDtypeStruct((4 * length, width), bf16),
            jax.ShapeDtypeStruct((4 * length, width), bf16),
            jax.ShapeDtypeStruct((4 * length, steps * TILE), bf16),
            jax.ShapeDtypeStruct((4 * length, steps * 2 * TILE), bf16),
        ),
        input_output_aliases={2 * count + 2 + k: k for k in range(len(held))},
        compiler_params=pltpu.CompilerParams(vmem_limit_bytes=VMEM_LIMIT),
        cost_estimate=SMALL,
    )(jnp.zeros((1,), jnp.int32) if pick is None else pick, *rows, *grads, units, *held)


def write_blocks(total, out_refs):
    rows = out_refs[0].shape[0]
    for k, ref in enumerate(out_refs):
        ref[...] = total[k * rows : (k + 1) * rows].astype(bf16)


def units_back_kernel(both_ref, units_ref, *out_refs):
    total = None
    for i in range(both_ref.shape[1] // (2 * TILE)):
        term = dot(
            both_ref[:, i * 2 * TILE : (i + 1) * 2 * TILE],
            units_ref[:, i * 3 * TILE : (i * 3 + 2) * TILE],
            1,
            1,
        )
        total = term if total is None else total + term
    write_blocks(total, out_refs)


def units_down_kernel(hidden_ref, units_ref, *out_refs):
    total = None
    for i in range(hidden_ref.shape[1] // TILE):
        term = dot(
            hidden_ref[:, i * TILE : (i + 1) * TILE],
            units_ref[:, (i * 3 + 2) * TILE : (i * 3 + 3) * TILE],
            1,
            1,
        )
        total = term if total is None else total + term
    write_blocks(total, out_refs)


def units_to_width(kernel, values, units, first, count):
    width = units.shape[0]
    block, columns = values.shape[0] // 4, values.shape[1]
    length = block * count
    return pl.pallas_call(
        kernel,
        grid=(width // TILE,),
        in_specs=[
            pl.BlockSpec((length, columns), lambda i: (first // count, 0)),
            pl.BlockSpec((TILE, units.shape[1]), lambda i: (i, 0)),
        ],
        out_specs=(pl.BlockSpec((block, TILE), lambda i: (0, i)),) * count,
        out_shape=(jax.ShapeDtypeStruct((block, width), bf16),) * count,
        compiler_params=pltpu.CompilerParams(vmem_limit_bytes=VMEM_LIMIT),
        cost_estimate=SMALL,
    )(values, units)


def units_add_kernel(*refs):
    out_ref = refs[-1]
    begin = 0
    for kept_ref, other_ref in zip(refs[0:-1:2], refs[1:-1:2]):
        columns = kept_ref.shape[2]
        out_ref[0, :, begin : begin + columns] = (
            kept_ref[0].astype(f32) + other_ref[0].astype(f32)
        ).astype(bf16)
        begin += columns


def units_add(*values):
    pairs, rows, _ = values[0].shape
    columns = sum(value.shape[2] for value in values[::2])
    return pl.pallas_call(
        units_add_kernel,
        grid=(pairs,),
        in_specs=[
            pl.BlockSpec((1, rows, value.shape[2]), lambda i: (i, 0, 0)) for value in values
        ],
        out_specs=pl.BlockSpec((1, rows, columns), lambda i: (i, 0, 0)),
        out_shape=jax.ShapeDtypeStruct((pairs, rows, columns), bf16),
        compiler_params=pltpu.CompilerParams(vmem_limit_bytes=VMEM_LIMIT),
        cost_estimate=SMALL,
    )(*values)


def units_gradient_kernel(core_ref, left_ref, right_ref, kept_ref, given_ref, total_ref):
    total_ref[...] = dot(left_ref[...], right_ref[...], 0, 0)
    core = core_ref[0]
    pairs, rows, _ = kept_ref.shape
    for p in range(pairs):
        for c, ref in ((core, kept_ref), (1 - core, given_ref)):
            at_row = pl.multiple_of((2 * p + c) * rows, 16)
            ref[p] = total_ref[pl.ds(at_row, rows), :].astype(bf16)


def units_gradient_parts(left, right, core):
    length, width = left.shape
    columns = right.shape[1]
    count = lax.axis_size("dp")
    rows = width // count
    tile = 2 * TILE if columns % (2 * TILE) == 0 else TILE
    out = pl.BlockSpec((count // 2, rows, tile), lambda i, c: (0, 0, i))
    shape = jax.ShapeDtypeStruct((count // 2, rows, columns), bf16)
    return pl.pallas_call(
        units_gradient_kernel,
        grid_spec=pltpu.PrefetchScalarGridSpec(
            num_scalar_prefetch=1,
            grid=(columns // tile,),
            in_specs=[
                pl.BlockSpec((length, width), lambda i, c: (0, 0)),
                pl.BlockSpec((length, tile), lambda i, c: (0, i)),
            ],
            out_specs=(out, out),
            scratch_shapes=[pltpu.VMEM((width, tile), f32)],
        ),
        out_shape=(shape, shape),
        compiler_params=pltpu.CompilerParams(vmem_limit_bytes=VMEM_LIMIT),
        cost_estimate=SMALL,
    )(core[None], left, right)


def swap_core(value):
    count = lax.axis_size("dp")
    return lax.ppermute(value, "dp", [(i, i ^ 1) for i in range(count)])


def swap_near(value):
    return lax.ppermute(value, "tensor", [(0, 1), (1, 0), (2, 3), (3, 2)])


def swap_far(value):
    return lax.ppermute(value, "tensor", [(0, 2), (2, 0), (1, 3), (3, 1)])


def swap_middle(value):
    return lax.ppermute(value, "tensor", [(1, 2), (2, 1)])


def swap_opposite(value):
    return lax.ppermute(value, "tensor", [(i, 3 - i) for i in range(4)])


def to_ends(value):
    return lax.ppermute(value, "tensor", [(1, 0), (2, 3)])


def from_ends(value):
    return lax.ppermute(value, "tensor", [(0, 1), (3, 2)])


def device_of(pair, core, z):
    return (2 * pair + core) * 4 + z


def owner_swap(value):
    perm = []
    for p in range(lax.axis_size("dp") // 2):
        for z in range(4):
            own = z // 2
            perm.append((device_of(p, own, z), device_of(p, own, z ^ 1)))
            perm.append((device_of(p, 1 - own, z), device_of(p, own, z ^ 2)))
    return lax.ppermute(value, AXES, perm)


def guest_swap(value):
    perm = []
    for p in range(lax.axis_size("dp") // 2):
        for z in range(4):
            guest = 1 - z // 2
            perm.append((device_of(p, guest, z), device_of(p, guest, z ^ 1)))
    return lax.ppermute(value, AXES, perm)


def heads_scatter_near(mine, other, z):
    def term(index):
        return at(mine, index, 0).astype(f32) + at(other, index, 0).astype(f32)

    away = swap_near(term(z ^ 3).astype(bf16))
    return term(z), term(z ^ 2), swap_near(term(z ^ 1).astype(bf16)), away


def heads_scatter_end(home, far, own, core):
    kept = jnp.where(own, home, far.astype(f32))
    return kept, swap_core(jnp.where(own, far, home.astype(bf16)))


def both_halves(kept, given, core):
    given = given.astype(f32)
    return jnp.concatenate(
        [jnp.where(core == 0, kept, given), jnp.where(core == 0, given, kept)], axis=0
    )


def gather_dp(value):
    bit = 1
    while bit < lax.axis_size("dp"):
        other = swap_dp(value, bit)
        upper = (lax.axis_index("dp") & bit) != 0
        value = jnp.concatenate(
            [jnp.where(upper, other, value), jnp.where(upper, value, other)], axis=0
        )
        bit *= 2
    return value


def gather_tensor(value, bit):
    other = lax.ppermute(value, "tensor", [(i, i ^ bit) for i in range(4)])
    upper = (lax.axis_index("tensor") & bit) != 0
    return jnp.concatenate(
        [jnp.where(upper, other, value), jnp.where(upper, value, other)], axis=1
    )


def sum_dp(value, first, last):
    bit = first
    while bit < last:
        value = value + swap_dp(value, bit)
        bit *= 2
    return value


def pair_groups():
    count = lax.axis_size("dp")
    return [list(range(c, count, 2)) for c in range(2)]


def swap_dp(value, mask):
    count = lax.axis_size("dp")
    return lax.ppermute(value, "dp", [(i, i ^ mask) for i in range(count)])


def gather_pairs_begin(value):
    if lax.axis_size("dp") != 8:
        return (lax.all_gather(value, "dp", axis=0, tiled=True, axis_index_groups=pair_groups()),)
    return value, swap_dp(value, 2), swap_dp(value, 4)


def gather_pairs_end(parts):
    if len(parts) == 1:
        return parts, jnp.zeros((1,), jnp.int32)
    value, by_two, by_four = parts
    pair = lax.axis_index("dp") >> 1
    rows = value.shape[0]
    half = rows // 2
    low, high = swap_dp(by_four[:half], 2), swap_dp(by_two[half:], 4)
    begins = jnp.stack([pair, pair ^ 1, pair ^ 2, pair ^ 3, pair ^ 3]) * rows
    begins = begins + jnp.array([0, 0, 0, 0, half], jnp.int32)
    return (value, by_two, by_four, low, high), begins


def at(value, index, axis):
    return lax.dynamic_index_in_dim(value, index, axis, keepdims=False)


def add_low(left, right):
    return (left.astype(f32) + right.astype(f32)).astype(bf16)


def scatter_pairs_begin(pieces):
    if len(pieces) == 1:
        return (
            lax.psum_scatter(
                pieces[0], "dp", scatter_dimension=0, tiled=True, axis_index_groups=pair_groups()
            ),
        )
    keep_x, send_x, keep_y, send_y = pieces
    return keep_x, swap_dp(send_x, 2), keep_y, swap_dp(send_y, 4)


def scatter_pairs_middle(pair, parts):
    if len(parts) == 1:
        return parts
    return pieces_call(pieces_middle_kernel, pair, parts, 4)


def scatter_pairs_send(parts):
    if len(parts) == 1:
        return parts
    keep_one, send_one, keep_two, send_two = parts
    return keep_one, swap_dp(send_one, 4), keep_two, swap_dp(send_two, 2)


def scatter_pairs_end(core, parts):
    if len(parts) == 1:
        rows = parts[0].shape[0] // 2
        return at(parts[0].reshape(2, rows, -1), core, 0), at(
            parts[0].reshape(2, rows, -1), core ^ 1, 0
        )
    return pieces_call(pieces_end_kernel, core[None], parts, 2)


def heads_pair(shard, far, own, core):
    kept = jnp.where(own, shard, far)
    other = swap_core(jnp.where(own, far, shard))
    return jnp.concatenate(
        [jnp.where(core == 0, kept, other), jnp.where(core == 0, other, kept)], axis=0
    )


def units_gradient(summed):
    return lax.psum_scatter(
        summed.reshape(-1, summed.shape[-1]),
        "dp",
        scatter_dimension=0,
        tiled=True,
        axis_index_groups=pair_groups(),
    )


def together(*values):
    return lax.optimization_barrier(values)


def after(value, earlier):
    return lax.optimization_barrier((value, earlier))[0]


def shards(
    block_in,
    out_grad,
    positions,
    qkv_weight,
    qkv_first,
    qkv_second,
    out_weight,
    out_first,
    out_second,
    gate_up,
    gate_up_first,
    gate_up_second,
    down_weight,
    down_first,
    down_second,
    norm_gains,
    norm_gains_first,
    norm_gains_second,
):
    model_width = block_in.shape[1]
    z = lax.axis_index("tensor")
    core = lax.axis_index("dp") & 1
    own = core == z // 2
    place = jnp.where(own, z, z ^ 2)[None]
    pair = (lax.axis_index("dp") >> 1)[None]
    pair = jnp.concatenate([pair & 1, pair >> 1])

    units_columns = gate_up.shape[2]
    heads_own = jnp.concatenate([qkv_weight.astype(bf16), out_weight.astype(bf16).T], axis=1)
    heads_own, gains_own, positions = together(heads_own, norm_gains[None], positions)
    heads_far = swap_far(heads_own)
    gains_dp = gather_dp(gains_own)[:, None]
    gains_all = gather_tensor(gather_tensor(gains_dp, 1), 2).reshape(1, -1)
    inverse_in = lax.rsqrt(jnp.mean(block_in * block_in, axis=-1, keepdims=True) + eps_norm)
    scaled_in = block_in * inverse_in
    head_positions = jnp.where(own, positions, swap_core(positions))
    scaled_b, heads_own, heads_far, head_positions, units_shard, grad_own, gains_all = together(
        scaled_in.astype(bf16),
        heads_own,
        heads_far,
        head_positions,
        pack_units(after(gate_up, gains_dp), down_weight.T),
        after(out_grad, gains_dp).astype(bf16),
        gains_all,
    )

    scaled_first = owner_swap(scaled_b)
    heads_parts = gather_pairs_begin(heads_pair(heads_own, heads_far, own, core))
    tables = rope_tables(head_positions, HEAD_DIMENSION)
    length = head_positions.shape[0]
    start = jnp.maximum(jnp.arange(length, dtype=jnp.int32) - head_positions, 0)
    start = start.astype(f32)[None]
    gain_attn = gains_all[:, :model_width]
    gain_q = gains_all[0, model_width : model_width + HEAD_DIMENSION]
    gain_k = gains_all[0, model_width + HEAD_DIMENSION : model_width + 2 * HEAD_DIMENSION]
    kv_local = qkv_weight.shape[1] // ((QUERY_GROUP + 2) * HEAD_DIMENSION)
    head_gains = jnp.concatenate(
        ([gain_q] * QUERY_GROUP + [gain_k, jnp.ones_like(gain_k)]) * kv_local
    )[None]
    gain_ffn = gains_all[:, model_width + 2 * HEAD_DIMENSION :]
    (
        scaled_first,
        heads_parts,
        gain_attn,
        head_gains,
        gain_ffn,
        units_shard,
        tables,
        start,
        grad_own,
    ) = together(
        scaled_first,
        heads_parts,
        gain_attn,
        head_gains,
        gain_ffn,
        units_shard,
        tables,
        start,
        grad_own,
    )

    scaled_second = guest_swap(scaled_first)
    scaled_mine = jnp.where(own, scaled_b, scaled_first)
    scaled_other = swap_core(scaled_mine)
    heads_blocks, heads_begins = gather_pairs_end(heads_parts)
    half, quarter = grad_own.shape[0] // 2, grad_own.shape[0] // 4
    grad_far = swap_far(grad_own[:quarter])
    (
        heads_blocks,
        scaled_second,
        scaled_mine,
        scaled_other,
        units_shard,
        grad_own,
        grad_far,
    ) = together(
        heads_blocks,
        scaled_second,
        scaled_mine,
        scaled_other,
        units_shard,
        grad_own,
        grad_far,
    )

    units = lax.all_gather(units_shard, "dp", axis=0, tiled=True)
    grad_far_rest = swap_far(grad_own[quarter:])
    grad_near = swap_near(grad_own)
    scaled_next = jnp.where(own, scaled_first, scaled_second)
    scaled_parts = (scaled_mine, scaled_next, scaled_other, swap_core(scaled_next))
    w_heads, normed_all, projected, queries_b, keys_b, values_b, attended, lse = attention_forward(
        place, scaled_parts, heads_blocks, heads_begins, gain_attn, head_gains, tables, start
    )
    branch_mine, branch_other = attention_branch(core[None], attended, w_heads)
    branch_mine, branch_other, grad_far, grad_far_rest, grad_near, grad_own = together(
        branch_mine, branch_other, grad_far, grad_far_rest, grad_near, grad_own
    )
    grad_far = jnp.concatenate([grad_far, grad_far_rest], axis=0)
    branch_other = swap_core(branch_other)
    grad_middle_part = swap_middle(grad_own)
    branch_mine, branch_other, grad_far = together(branch_mine, branch_other, grad_far)
    home, term_far, near, away = heads_scatter_near(branch_mine, branch_other, z)
    away, term_far, grad_middle_part = together(away, term_far, grad_middle_part)
    far = swap_far((term_far + away.astype(f32)).astype(bf16))
    far, home, near = together(far, home, near)
    middle = block_in + both_halves(
        *heads_scatter_end(home + near.astype(f32), far, own, core), core
    )

    inverse_mid = lax.rsqrt(jnp.mean(middle * middle, axis=-1, keepdims=True) + eps_norm)
    scaled_mid = middle * inverse_mid
    rows_own = (scaled_mid * gain_ffn).astype(bf16)
    rows_far = swap_far(rows_own)
    rows_near = swap_near(rows_own)
    inner = (z == 1) | (z == 2)
    buffers = units_forward((rows_own,), (grad_own,), units, None, 2)
    rows_far, rows_near, rows_own, buffers = together(rows_far, rows_near, rows_own, buffers)
    grad_ends = to_ends(grad_far)
    rows_ends = to_ends(rows_far)
    rows_middle = swap_middle(rows_own)
    buffers = units_forward((rows_near, rows_far), (grad_near, grad_far), units, buffers, 0)
    rows_all, grad_all, hidden_b, dboth = buffers
    back_near, back_far = units_to_width(units_back_kernel, dboth, units, 0, 2)
    rows_ends, rows_middle, grad_ends, back_near, back_far, buffers = together(
        rows_ends, rows_middle, grad_ends, back_near, back_far, buffers
    )
    from_far = swap_far(back_far)
    from_near = swap_near(back_near)
    rows_all, grad_all, hidden_b, dboth = units_forward(
        (rows_ends, rows_middle),
        (grad_ends, grad_middle_part),
        units,
        buffers,
        3,
        inner.astype(jnp.int32)[None],
    )
    back_own, back_last = units_to_width(units_back_kernel, dboth, units, 2, 2)
    from_near, from_far, back_last, back_own, rows_all, grad_all, hidden_b, dboth = together(
        from_near, from_far, back_last, back_own, rows_all, grad_all, hidden_b, dboth
    )
    from_last = swap_opposite(back_last)
    down_kept, down_given = units_gradient_parts(grad_all, hidden_b, core)
    (down_last,) = units_to_width(units_down_kernel, hidden_b, units, 3, 1)
    branch_ends = [from_ends(down_last[:half]), from_ends(down_last[half:])]
    both_kept, both_given = units_gradient_parts(rows_all, dboth, core)
    from_last, branch_ends, down_kept, down_given, both_kept, both_given, down_last = together(
        from_last, branch_ends, down_kept, down_given, both_kept, both_given, down_last
    )
    grad_normed_two = (
        back_own.astype(f32)
        + from_near.astype(f32)
        + from_far.astype(f32)
        + from_last.astype(f32)
    )

    grad_gain_ffn = jnp.sum(grad_normed_two * scaled_mid, axis=0)
    weighted = grad_normed_two * gain_ffn
    grad_middle = out_grad + inverse_mid * (
        weighted - scaled_mid * jnp.mean(weighted * scaled_mid, axis=-1, keepdims=True)
    )
    grad_mid_b, grad_gain_ffn, hidden_b, down_kept, down_given, both_kept, both_given = together(
        grad_middle.astype(bf16),
        grad_gain_ffn,
        hidden_b,
        down_kept,
        down_given,
        both_kept,
        both_given,
    )
    grad_mid_first = owner_swap(grad_mid_b)
    units_sum = units_add(both_kept, swap_core(both_given), down_kept, swap_core(down_given))
    down_near, down_far, down_own = units_to_width(units_down_kernel, hidden_b, units, 0, 3)
    down_far = add_low(down_far, jnp.concatenate(branch_ends, axis=0))
    grad_mid_first, units_sum, down_near, down_far, down_own = together(
        grad_mid_first, units_sum, down_near, down_far, down_own
    )
    units_sum = units_gradient(units_sum)
    grad_mid_second = guest_swap(grad_mid_first)
    branch_far = swap_far(down_far[:half])
    grad_mid_mine = jnp.where(own, grad_mid_b, grad_mid_first)
    grad_mid_other = swap_core(grad_mid_mine)
    grad_mid_second, grad_mid_mine, grad_mid_other, branch_far, down_far = together(
        grad_mid_second, grad_mid_mine, grad_mid_other, branch_far, down_far
    )
    grad_mid_next = jnp.where(own, grad_mid_first, grad_mid_second)
    grad_mid_parts = (grad_mid_mine, grad_mid_next, grad_mid_other, swap_core(grad_mid_next))

    branch_far_rest = swap_far(down_far[half:])
    branch_near = swap_near(down_near)
    branch_middle = swap_middle(down_last)
    grad_attended, row_dot, *out_pieces = attention_turn(
        place, pair, grad_mid_parts, w_heads, attended
    )
    out_parts = scatter_pairs_begin(tuple(out_pieces))
    grad_projected, part_mine, part_other, head_sums, gain_sums = attention_backward(
        core[None],
        queries_b,
        keys_b,
        values_b,
        grad_attended,
        lse,
        row_dot,
        start,
        projected,
        head_gains,
        *tables,
        w_heads,
        normed_all,
        gain_attn,
    )
    (
        grad_projected,
        part_mine,
        part_other,
        branch_far,
        branch_far_rest,
        branch_near,
        branch_middle,
        out_parts,
    ) = together(
        grad_projected,
        part_mine,
        part_other,
        branch_far,
        branch_far_rest,
        branch_near,
        branch_middle,
        out_parts,
    )

    part_other = swap_core(part_other)
    qkv_pieces = heads_gradient(pair, normed_all, grad_projected)
    part_mine, part_other, qkv_pieces, out_parts, branch_far = together(
        part_mine, part_other, qkv_pieces, out_parts, branch_far
    )
    home, term_far, near, away = heads_scatter_near(part_mine, part_other, z)
    qkv_parts = scatter_pairs_begin(qkv_pieces)
    out_parts = scatter_pairs_middle(pair, out_parts)
    gain_sums, head_sums = after((gain_sums, head_sums), qkv_pieces)
    head_sums = head_sums.reshape(-1, QUERY_GROUP + 2, HEAD_DIMENSION)
    gain_total = jnp.concatenate(
        [
            gain_sums[0],
            jnp.sum(head_sums[:, :QUERY_GROUP], axis=(0, 1)),
            jnp.sum(head_sums[:, QUERY_GROUP], axis=0),
            grad_gain_ffn,
        ]
    )
    gain_total = sum_dp(gain_total, 1, lax.axis_size("dp") // 2)
    block_out = (
        middle
        + down_own.astype(f32)
        + branch_near.astype(f32)
        + branch_middle.astype(f32)
        + jnp.concatenate([branch_far, branch_far_rest], axis=0).astype(f32)
    )
    far_term = (term_far + away.astype(f32)).astype(bf16)
    far = swap_far(far_term)
    qkv_parts = scatter_pairs_middle(pair, after(qkv_parts, (far_term, gain_total, block_out)))
    out_parts = scatter_pairs_send(after(out_parts, qkv_parts))
    qkv_parts = scatter_pairs_send(qkv_parts)
    down_new = adam_units(
        down_weight.T[None],
        down_first.T[None],
        down_second.T[None],
        after(units_sum, (near, out_parts[0])),
        2 * units_sum.shape[1] // 3,
    )
    gain_total = after(gain_total, down_new)
    gain_last = swap_dp(gain_total, lax.axis_size("dp") // 2)
    qkv_kept, qkv_given = scatter_pairs_end(core, after(qkv_parts, (down_new, far)))
    gain_total = gain_total + after(gain_last, qkv_kept)
    gain_last = swap_near(gain_total)
    out_kept, out_given = scatter_pairs_end(core, after(out_parts, (down_new, far)))
    qkv_other, out_other = swap_core(qkv_given), swap_core(out_given)
    gain_total = gain_total + after(gain_last, out_kept)
    heads_away = jnp.concatenate(
        [jnp.where(own, qkv_other, qkv_kept), jnp.where(own, out_other, out_kept)], axis=1
    )
    kept, given = heads_scatter_end(home + near.astype(f32), far, own, core)
    units_sum = after(units_sum, heads_away)
    gain_last = swap_far(gain_total)
    heads_away = swap_far(heads_away)
    gain_total = gain_total + gain_last
    in_grad = input_gradient(core[None], kept, given, block_in, gain_attn, grad_middle)
    gate_up_new = adam_units(gate_up, gate_up_first, gate_up_second, units_sum, 0)
    heads_away, in_grad, gate_up_new = together(heads_away, in_grad, gate_up_new)
    down_new = tuple(value[0].T for value in down_new)
    qkv_columns = qkv_weight.shape[1]
    sum_qkv = jnp.where(own, qkv_kept, qkv_other).astype(f32) + heads_away[
        :, :qkv_columns
    ].astype(f32)
    sum_out = jnp.where(own, out_kept, out_other).astype(f32) + heads_away[
        :, qkv_columns:
    ].astype(f32)
    sum_out = sum_out.T
    gain_count = norm_gains.shape[0]
    gain_at = (lax.axis_index("dp") * 4 + z) * gain_count
    gain_grads = lax.dynamic_slice_in_dim(gain_total, gain_at, gain_count)

    qkv_new = adam_step(qkv_weight, qkv_first, qkv_second, sum_qkv, rate_matrix, decay_matrix)
    out_new = adam_step(out_weight, out_first, out_second, sum_out, rate_output, decay_matrix)
    gains_new = adam_step(
        norm_gains, norm_gains_first, norm_gains_second, gain_grads, rate_gains, 0.0
    )
    return (block_out, in_grad, *qkv_new, *out_new, *gate_up_new, *down_new, *gains_new)


def solution(mesh):
    tokens = P(("dp", "tensor"), None)
    by_rows = (P("dp", "tensor"),) * 3
    by_columns = (P("tensor", "dp"),) * 3
    stacked = (P(None, "dp", "tensor"),) * 3
    gains = (P(("dp", "tensor")),) * 3
    states = by_rows + by_columns + stacked + by_columns + gains
    return jax.shard_map(
        shards,
        mesh=mesh,
        in_specs=(tokens, tokens, P("dp")) + states,
        out_specs=(tokens, tokens) + states,
        check_vma=False,
    )
```

```python
import functools

import jax
import jax.numpy as jnp
from jax import lax
from jax.experimental import pallas as pl
from jax.experimental.pallas import tpu as pltpu
from jax.sharding import PartitionSpec as P

HEAD_DIMENSION = 64
STEP = 10
QUERY_GROUP = 3
AXES = ("dp", "tensor")

eps_norm = 1e-05
rope_base = 1000000.0
beta_one = 0.9
beta_two = 0.999
adam_eps = 1e-08
decay_matrix = 0.1
rate_matrix = 0.03
rate_output = 0.15
rate_gains = 0.8
bf16 = jnp.bfloat16
f32 = jnp.float32
VMEM_LIMIT = 58 * 1024 * 1024
SMALL = pl.CostEstimate(flops=1000, bytes_accessed=1000, transcendentals=0)


def whole(value):
    zeros = (0,) * len(value.shape)
    return pl.BlockSpec(value.shape, lambda i: zeros, pipeline_mode=pl.Buffered(1))


def scalars(count):
    return [pl.BlockSpec(memory_space=pltpu.SMEM)] * count


def dot(left, right, left_dim, right_dim):
    return lax.dot_general(
        left, right, (((left_dim,), (right_dim,)), ((), ())), preferred_element_type=f32
    )


def norm_rows(row_block, gain_vec):
    inverse = lax.rsqrt(jnp.mean(row_block * row_block, axis=-1, keepdims=True) + eps_norm)
    return row_block * inverse * gain_vec


def rope_tables(positions, head_size):
    inverse_freq = rope_base ** (-(jnp.arange(head_size // 2, dtype=f32) * 2.0) / head_size)
    angles = positions.astype(f32)[:, None] * inverse_freq[None, :]
    cos_part, sin_part = jnp.cos(angles), jnp.sin(angles)
    return (
        jnp.concatenate([cos_part] * 4, axis=1),
        jnp.concatenate([-sin_part, sin_part] * 2, axis=1),
    )


def adam_step(weight, first_old, second_old, gradient, step_rate, decay_rate):
    first_new = beta_one * first_old + (1.0 - beta_one) * gradient
    second_new = beta_two * second_old + (1.0 - beta_two) * gradient * gradient
    fix_one = 1.0 - beta_one**STEP
    fix_two = 1.0 - beta_two**STEP
    update = first_new / fix_one / (jnp.sqrt(second_new / fix_two) + adam_eps)
    return (weight - step_rate * (update + decay_rate * weight), first_new, second_new)


PAIR = 2 * HEAD_DIMENSION


def lanes_of(value):
    return lax.broadcasted_iota(jnp.int32, value.shape, 1)


def swap_halves(value):
    half = HEAD_DIMENSION // 2
    low = lanes_of(value) % HEAD_DIMENSION < half
    return jnp.where(low, pltpu.roll(value, PAIR - half, 1), pltpu.roll(value, half, 1))


def two_parts(value):
    high = value.astype(bf16)
    return high, (value - high.astype(f32)).astype(bf16)


def head_means(value):
    shape = (PAIR, PAIR)
    one, two = (lax.broadcasted_iota(jnp.int32, shape, d) // HEAD_DIMENSION for d in (0, 1))
    weights = jnp.where(one == two, 1.0 / HEAD_DIMENSION, 0.0).astype(bf16)
    high, low = two_parts(value)
    return dot(high, weights, 1, 0) + dot(low, weights, 1, 0)


def is_value(index, value):
    at_head = [(2 * index + k) % (QUERY_GROUP + 2) == QUERY_GROUP + 1 for k in range(2)]
    if not any(at_head):
        return None
    return (lanes_of(value) < HEAD_DIMENSION) == at_head[0]


def unless(mask, value, other):
    return value if mask is None else jnp.where(mask, other, value)


def as_row(column):
    return jnp.broadcast_to(column, (column.shape[0], 128)).T[:1, :]


def as_column(row):
    return jnp.broadcast_to(row, (128, row.shape[1])).T[:, :1]


def place_parts(place_ref, part_refs, whole_ref, scale):
    rows = part_refs[0].shape[0]
    for j, part_ref in enumerate(part_refs):
        at_row = pl.multiple_of((j ^ place_ref[0]) * rows, rows)
        value = part_ref[...]
        if scale is not None:
            value = (value.astype(f32) * scale).astype(bf16)
        whole_ref[pl.ds(at_row, rows), :] = value


def split_halves(core_ref, value, stage_ref, mine_ref, other_ref, index):
    half = value.shape[0] // 2
    stage_ref[...] = value
    core = core_ref[0]
    mine_ref[index] = stage_ref[pl.ds(pl.multiple_of(core * half, half), half), :]
    other_ref[index] = stage_ref[pl.ds(pl.multiple_of((1 - core) * half, half), half), :]


def place_blocks(begins_ref, block_refs, whole_ref):
    for k, block_ref in enumerate(block_refs):
        begin = pl.multiple_of(begins_ref[k], 16)
        whole_ref[pl.ds(begin, block_ref.shape[0]), :] = block_ref[...]


def attention_forward_kernel(count, place_ref, begins_ref, *refs):
    part_refs, refs = refs[:4], refs[4:]
    block_refs, refs = refs[:count], refs[count:]
    (
        gain_ref,
        head_gain_ref,
        cos_ref,
        sin_ref,
        start_ref,
        weight_ref,
        normed_ref,
        projected_ref,
        q_ref,
        k_ref,
        v_ref,
        out_ref,
        lse_ref,
    ) = refs
    place_blocks(begins_ref, block_refs, weight_ref)
    size = HEAD_DIMENSION
    heads, length, _ = q_ref.shape
    group = QUERY_GROUP
    kv = heads // group
    block = min(256, length)
    place_parts(place_ref, part_refs, normed_ref, gain_ref[...])
    for i in range(length // block):
        here = pl.ds(i * block, block)
        projected = dot(normed_ref[here, :], weight_ref[:, : projected_ref.shape[1]], 1, 0)
        projected_ref[here, :] = projected
        cos_part, sin_part = cos_ref[here, :], sin_ref[here, :]
        for t in range(projected.shape[1] // PAIR):
            raw = projected[:, t * PAIR : (t + 1) * PAIR]
            keep = is_value(t, raw)
            inverse = unless(keep, lax.rsqrt(head_means(raw * raw) + eps_norm), 1.0)
            normed = raw * inverse * head_gain_ref[:, t * PAIR : (t + 1) * PAIR]
            turned = normed * unless(keep, cos_part, 1.0) + swap_halves(normed) * unless(
                keep, sin_part, 0.0
            )
            turned = turned.astype(bf16)
            for k in range(2):
                j, g = divmod(2 * t + k, group + 2)
                piece = turned[:, k * size : (k + 1) * size]
                if g < group:
                    q_ref[j * group + g, here, :] = piece * jnp.asarray(size**-0.5, bf16)
                elif g == group:
                    k_ref[j, here, :] = piece
                else:
                    v_ref[j, here, :] = piece
    row_at = lax.broadcasted_iota(jnp.int32, (block, block), 0)
    col_at = lax.broadcasted_iota(jnp.int32, (block, block), 1)
    causal = jnp.concatenate([col_at <= row_at] * group, axis=0)
    col_all = lax.broadcasted_iota(jnp.int32, (group * block, block), 1).astype(f32)
    ones = jnp.ones((block, size), bf16)
    for j in range(kv):
        for i in range(length // block):
            here = pl.ds(i * block, block)
            queries = jnp.concatenate(
                [q_ref[j * group + g, here, :] for g in range(group)], axis=0
            )
            start = jnp.concatenate([as_column(start_ref[:, here])] * group, axis=0)
            total = jnp.zeros((group * block, 2 * size), f32)
            for b in range(i + 1):
                there = pl.ds(b * block, block)
                scores = dot(queries, k_ref[j, there, :], 1, 1)
                allowed = col_all >= start - b * block
                if b == i:
                    allowed = allowed & causal
                weights = jnp.where(allowed, jnp.exp(scores), 0.0).astype(bf16)
                values = jnp.concatenate([v_ref[j, there, :], ones], axis=1)
                total = total + dot(weights, values, 1, 0)
            row_sum = total[:, size : size + 1]
            output = (total[:, :size] / row_sum).astype(bf16)
            log_sum = jnp.log(row_sum)
            for g in range(group):
                h = j * group + g
                part = slice(g * block, (g + 1) * block)
                out_ref[here, h * size : (h + 1) * size] = output[part]
                lse_ref[h, :, here] = as_row(log_sum[part])


def attention_branch_kernel(core_ref, attended_ref, weight_ref, mine_ref, other_ref, stage_ref):
    shard, columns = attended_ref.shape[0] // 4, attended_ref.shape[1]
    for i in range(4):
        value = dot(
            attended_ref[i * shard : (i + 1) * shard, :], weight_ref[:, -columns:], 1, 1
        )
        split_halves(core_ref, value.astype(bf16), stage_ref, mine_ref, other_ref, i)


def attention_forward(place, parts, blocks, begins, gain_attn, head_gains, tables, start):
    rows, width = parts[0].shape
    length = 4 * rows
    size = HEAD_DIMENSION
    columns = blocks[0].shape[1]
    kv = columns // ((2 * QUERY_GROUP + 2) * size)
    heads = kv * QUERY_GROUP
    operands = (*parts, *blocks, gain_attn, head_gains, *tables, start)
    results = (
        jax.ShapeDtypeStruct((width, columns), bf16),
        jax.ShapeDtypeStruct((length, width), bf16),
        jax.ShapeDtypeStruct((length, (heads + 2 * kv) * size), f32),
        jax.ShapeDtypeStruct((heads, length, size), bf16),
        jax.ShapeDtypeStruct((kv, length, size), bf16),
        jax.ShapeDtypeStruct((kv, length, size), bf16),
        jax.ShapeDtypeStruct((length, heads * size), bf16),
        jax.ShapeDtypeStruct((heads, 1, length), f32),
    )
    return pl.pallas_call(
        functools.partial(attention_forward_kernel, len(blocks)),
        grid=(1,),
        in_specs=scalars(2) + [whole(value) for value in operands],
        out_specs=tuple(whole(value) for value in results),
        out_shape=results,
        compiler_params=pltpu.CompilerParams(vmem_limit_bytes=VMEM_LIMIT),
        cost_estimate=SMALL,
    )(place, begins, *operands)


def attention_branch(core, attended, weight):
    length = attended.shape[0]
    width = weight.shape[0]
    half = jax.ShapeDtypeStruct((4, length // 8, width), bf16)
    return pl.pallas_call(
        attention_branch_kernel,
        grid=(1,),
        in_specs=scalars(1) + [whole(attended), whole(weight)],
        out_specs=(whole(half), whole(half)),
        out_shape=(half, half),
        scratch_shapes=[pltpu.VMEM((length // 4, width), bf16)],
        compiler_params=pltpu.CompilerParams(vmem_limit_bytes=VMEM_LIMIT),
        cost_estimate=SMALL,
    )(core, attended, weight)


def split_pieces(total_ref, pair_ref, piece_refs):
    if len(piece_refs) == 1:
        piece_refs[0][...] = total_ref[...].astype(bf16)
        return
    keep_x, send_x, keep_y, send_y = piece_refs
    rows = keep_x.shape[1]
    x, y = pair_ref[0], pair_ref[1]
    for k in range(2):
        for ref, pair, core in (
            (keep_x, 2 * k + x, 0),
            (send_x, 2 * k + 1 - x, 0),
            (keep_y, 2 * y + k, 1),
            (send_y, 2 * (1 - y) + k, 1),
        ):
            begin = pl.multiple_of((2 * pair + core) * rows, 16)
            ref[k] = total_ref[pl.ds(begin, rows), :].astype(bf16)


def pieces_shapes(width, columns):
    if lax.axis_size("dp") != 8:
        return (jax.ShapeDtypeStruct((width, columns), bf16),)
    return (jax.ShapeDtypeStruct((2, width // 8, columns), bf16),) * 4


def heads_gradient_kernel(pair_ref, left_ref, right_ref, *refs):
    refs[-1][...] = dot(left_ref[...], right_ref[...], 0, 0)
    split_pieces(refs[-1], pair_ref, refs[:-1])


def heads_gradient(pair, left, right):
    width, columns = left.shape[1], right.shape[1]
    results = pieces_shapes(width, columns)
    return pl.pallas_call(
        heads_gradient_kernel,
        grid=(1,),
        in_specs=scalars(1) + [whole(left), whole(right)],
        out_specs=tuple(whole(value) for value in results),
        out_shape=results,
        scratch_shapes=[pltpu.VMEM((width, columns), f32)],
        compiler_params=pltpu.CompilerParams(vmem_limit_bytes=VMEM_LIMIT),
        cost_estimate=SMALL,
    )(pair, left, right)


def add_refs(left, right):
    return (left.astype(f32) + right.astype(f32)).astype(bf16)


def pieces_middle_kernel(
    pair_ref, keep_x, got_x, keep_y, got_y, keep_one, send_one, keep_two, send_two
):
    x, y = pair_ref[0], pair_ref[1]
    keep_one[...] = add_refs(keep_x[y], got_x[y])
    send_one[...] = add_refs(keep_x[1 - y], got_x[1 - y])
    keep_two[...] = add_refs(keep_y[x], got_y[x])
    send_two[...] = add_refs(keep_y[1 - x], got_y[1 - x])


def pieces_end_kernel(core_ref, keep_one, got_one, keep_two, got_two, kept, given):
    @pl.when(core_ref[0] == 0)
    def _():
        kept[...] = add_refs(keep_one[...], got_one[...])
        given[...] = add_refs(keep_two[...], got_two[...])

    @pl.when(core_ref[0] != 0)
    def _():
        given[...] = add_refs(keep_one[...], got_one[...])
        kept[...] = add_refs(keep_two[...], got_two[...])


def pieces_call(kernel, scalar, values, count):
    result = jax.ShapeDtypeStruct(values[0].shape[-2:], bf16)
    vmem = pl.BlockSpec(memory_space=pltpu.VMEM)
    return pl.pallas_call(
        kernel,
        in_specs=scalars(1) + [vmem] * len(values),
        out_specs=(vmem,) * count,
        out_shape=(result,) * count,
        compiler_params=pltpu.CompilerParams(vmem_limit_bytes=VMEM_LIMIT),
        cost_estimate=SMALL,
    )(scalar, *values)


def attention_turn_kernel(place_ref, pair_ref, *refs):
    part_refs, (weight_ref, out_ref, grads_ref, dot_ref) = refs[:4], refs[4:8]
    piece_refs, (whole_ref, total_ref) = refs[8:-2], refs[-2:]
    size = HEAD_DIMENSION
    place_parts(place_ref, part_refs, whole_ref, None)
    heads, length, _ = grads_ref.shape
    block = min(256, length)
    shape = (dot_ref.shape[0], heads * size)
    of_head = (
        lax.broadcasted_iota(jnp.int32, shape, 0)
        == lax.broadcasted_iota(jnp.int32, shape, 1) // size
    ).astype(bf16)
    for i in range(length // block):
        here = pl.ds(i * block, block)
        grads = dot(whole_ref[here, :], weight_ref[:, -heads * size :], 1, 0).astype(bf16)
        high, low = two_parts(grads.astype(f32) * out_ref[here, :].astype(f32))
        dot_ref[:, here] = dot(of_head, high, 1, 1) + dot(of_head, low, 1, 1)
        for h in range(heads):
            grads_ref[h, here, :] = grads[:, h * size : (h + 1) * size]
    total_ref[...] = dot(whole_ref[...], out_ref[...], 0, 0)
    split_pieces(total_ref, pair_ref, piece_refs)


def attention_turn(place, pair, parts, weight, attended):
    rows, width = parts[0].shape
    length, columns = attended.shape
    heads = columns // HEAD_DIMENSION
    operands = (*parts, weight, attended)
    results = (
        jax.ShapeDtypeStruct((heads, length, HEAD_DIMENSION), bf16),
        jax.ShapeDtypeStruct((-(-heads // 8) * 8, length), f32),
        *pieces_shapes(width, columns),
    )
    return pl.pallas_call(
        attention_turn_kernel,
        grid=(1,),
        in_specs=scalars(2) + [whole(value) for value in operands],
        out_specs=tuple(whole(value) for value in results),
        out_shape=results,
        scratch_shapes=[pltpu.VMEM((length, width), bf16), pltpu.VMEM((width, columns), f32)],
        compiler_params=pltpu.CompilerParams(vmem_limit_bytes=VMEM_LIMIT),
        cost_estimate=SMALL,
    )(place, pair, *operands)


def attention_backward_kernel(
    core_ref,
    q_ref,
    k_ref,
    v_ref,
    g_ref,
    lse_ref,
    dot_ref,
    start_ref,
    projected_ref,
    head_gain_ref,
    cos_ref,
    sin_ref,
    weight_ref,
    normed_ref,
    gain_ref,
    back_ref,
    mine_ref,
    other_ref,
    head_sum_ref,
    gain_sum_ref,
    grad_ref,
    dk_ref,
    dv_ref,
    stage_ref,
):
    size = HEAD_DIMENSION
    heads, length, _ = q_ref.shape
    group = QUERY_GROUP
    kv = heads // group
    block = min(256, length)
    lanes = group * block
    key_at = lax.broadcasted_iota(jnp.int32, (block, block), 0)
    row_at = lax.broadcasted_iota(jnp.int32, (block, block), 1)
    causal = jnp.concatenate([key_at <= row_at] * group, axis=1)
    key_all = lax.broadcasted_iota(jnp.int32, (block, lanes), 0).astype(f32)
    dk_ref[...] = jnp.zeros_like(dk_ref)
    dv_ref[...] = jnp.zeros_like(dv_ref)
    head_sum_ref[...] = jnp.zeros_like(head_sum_ref)
    gain_sum_ref[...] = jnp.zeros_like(gain_sum_ref)
    for j in range(kv):
        for i in range(length // block):
            here = pl.ds(i * block, block)
            head = [j * group + g for g in range(group)]
            queries = jnp.concatenate([q_ref[h, here, :] for h in head], axis=0)
            grads = jnp.concatenate([g_ref[h, here, :] for h in head], axis=0)
            lse = jnp.concatenate([lse_ref[h, :, here] for h in head], axis=1)
            row_dot = jnp.concatenate([dot_ref[h : h + 1, here] for h in head], axis=1)
            start = jnp.concatenate([start_ref[:, here]] * group, axis=1)
            dq = jnp.zeros((size, lanes), f32)
            for b in range(i + 1):
                there = pl.ds(b * block, block)
                keys = k_ref[j, there, :]
                scores = dot(keys, queries, 1, 1)
                allowed = key_all >= start - b * block
                if b == i:
                    allowed = allowed & causal
                probs = jnp.where(allowed, jnp.exp(scores - lse), 0.0)
                grad_probs = dot(v_ref[j, there, :], grads, 1, 1)
                grad_scores = (probs * (grad_probs - row_dot)).astype(bf16)
                dv_ref[j, there, :] += dot(probs.astype(bf16), grads, 1, 0)
                dk_ref[j, there, :] += dot(grad_scores, queries, 1, 0)
                dq = dq + dot(keys, grad_scores, 0, 0)
            for g in range(group):
                column = (j * (group + 2) + g) * size
                grad_ref[here, column : column + size] = (
                    dq[:, g * block : (g + 1) * block].T * size**-0.5
                )
        key_column = (j * (group + 2) + group) * size
        grad_ref[:, key_column : key_column + size] = dk_ref[j]
        grad_ref[:, key_column + size : key_column + 2 * size] = dv_ref[j]
    shard = length // 4
    for i in range(4):
        here = pl.ds(i * shard, shard)
        cos_part, sin_part = cos_ref[here, :], sin_ref[here, :]
        for t in range(back_ref.shape[1] // PAIR):
            columns = slice(t * PAIR, (t + 1) * PAIR)
            given = grad_ref[here, columns]
            keep = is_value(t, given)
            grad = given * unless(keep, cos_part, 1.0) + swap_halves(
                given * unless(keep, sin_part, 0.0)
            )
            raw = projected_ref[here, columns]
            inverse = lax.rsqrt(head_means(raw * raw) + eps_norm)
            scaled = raw * inverse
            head_sum_ref[:, columns] += jnp.sum(grad * scaled, axis=0, keepdims=True)
            weighted = grad * head_gain_ref[:, columns]
            back = inverse * (weighted - scaled * head_means(weighted * scaled))
            back_ref[here, columns] = unless(keep, back, given).astype(bf16)
        term = dot(back_ref[here, :], weight_ref[:, : back_ref.shape[1]], 1, 1)
        gain_sum_ref[...] += jnp.sum(
            term * normed_ref[here, :].astype(f32), axis=0, keepdims=True
        )
        split_halves(core_ref, term.astype(bf16), stage_ref, mine_ref, other_ref, i)
    gain_sum_ref[...] = gain_sum_ref[...] / gain_ref[...]


def attention_backward(core, queries, keys, values, grads, lse, row_dot, start, projected, *rest):
    heads, length, size = queries.shape
    kv = keys.shape[0]
    normed = rest[-2]
    width = normed.shape[1]
    half = jax.ShapeDtypeStruct((4, length // 8, width), bf16)
    operands = (queries, keys, values, grads, lse, row_dot, start, projected) + rest
    results = (
        jax.ShapeDtypeStruct(projected.shape, bf16),
        half,
        half,
        jax.ShapeDtypeStruct((1, projected.shape[1]), f32),
        jax.ShapeDtypeStruct((1, width), f32),
    )
    return pl.pallas_call(
        attention_backward_kernel,
        grid=(1,),
        in_specs=scalars(1) + [whole(value) for value in operands],
        out_specs=tuple(whole(value) for value in results),
        out_shape=results,
        scratch_shapes=[
            pltpu.VMEM(projected.shape, f32),
            pltpu.VMEM((kv, length, size), f32),
            pltpu.VMEM((kv, length, size), f32),
            pltpu.VMEM((length // 4, width), bf16),
        ],
        compiler_params=pltpu.CompilerParams(vmem_limit_bytes=VMEM_LIMIT),
        cost_estimate=SMALL,
    )(core, *operands)


def input_gradient_kernel(core_ref, kept_ref, given_ref, rows_ref, gain_ref, middle_ref, out_ref):
    half = kept_ref.shape[0]
    core = core_ref[0]
    for index, ref in ((core, kept_ref), (1 - core, given_ref)):
        part = pl.ds(pl.multiple_of(index * half, half), half)
        rows = rows_ref[part, :]
        inverse = lax.rsqrt(jnp.mean(rows * rows, axis=1, keepdims=True) + eps_norm)
        scaled = rows * inverse
        weighted = ref[...].astype(f32) * gain_ref[...]
        out_ref[part, :] = middle_ref[part, :] + inverse * (
            weighted - scaled * jnp.mean(weighted * scaled, axis=1, keepdims=True)
        )


def input_gradient(core, kept, given, rows, gain, middle):
    vmem = pl.BlockSpec(memory_space=pltpu.VMEM)
    return pl.pallas_call(
        input_gradient_kernel,
        in_specs=scalars(1) + [vmem] * 5,
        out_specs=vmem,
        out_shape=jax.ShapeDtypeStruct(rows.shape, f32),
        compiler_params=pltpu.CompilerParams(vmem_limit_bytes=VMEM_LIMIT),
        cost_estimate=SMALL,
    )(core, kept, given, rows, gain, middle)


TILE = 256


def pack_units_kernel(both_ref, down_ref, out_ref):
    columns = both_ref.shape[2]
    rows = both_ref.shape[1]
    steps = out_ref.shape[1] // (3 * TILE)
    for i in range(steps):
        first, last = i * TILE, min(columns, (i + 1) * TILE)
        parts = (both_ref[0, :, first:last], both_ref[1, :, first:last], down_ref[:, first:last])
        for part, at_column in zip(parts, (2 * i * TILE, (2 * i + 1) * TILE, (2 * steps + i) * TILE)):
            if last - first < TILE:
                part = jnp.concatenate(
                    [part, jnp.zeros((rows, TILE - (last - first)), f32)], axis=1
                )
            out_ref[:, at_column : at_column + TILE] = part.astype(bf16)


def pack_units(gate_up, down):
    rows, columns = gate_up.shape[1:]
    steps = -(-columns // TILE)
    vmem = pl.BlockSpec(memory_space=pltpu.VMEM)
    return pl.pallas_call(
        pack_units_kernel,
        in_specs=[vmem, vmem],
        out_specs=vmem,
        out_shape=jax.ShapeDtypeStruct((rows, steps * 3 * TILE), bf16),
        compiler_params=pltpu.CompilerParams(vmem_limit_bytes=VMEM_LIMIT),
        cost_estimate=SMALL,
    )(gate_up, down)


def adam_kernel(weight_ref, first_ref, second_ref, sum_ref, *out_refs):
    parts = weight_ref.shape[0]
    groups = sum_ref.shape[1] // (parts * TILE)
    for p in range(parts):
        for k in range(groups):
            columns = slice(k * TILE, (k + 1) * TILE)
            at_sum = (k * parts + p) * TILE
            new = adam_step(
                weight_ref[p, :, columns],
                first_ref[p, :, columns],
                second_ref[p, :, columns],
                sum_ref[:, at_sum : at_sum + TILE].astype(f32),
                rate_matrix,
                decay_matrix,
            )
            for ref, value in zip(out_refs, new):
                ref[p, :, columns] = value


def adam_units(weight, first, second, summed, begin):
    parts, rows, columns = weight.shape
    groups = 2
    state = pl.BlockSpec((parts, rows, groups * TILE), lambda i: (0, 0, i))
    wide = parts * groups * TILE
    return pl.pallas_call(
        adam_kernel,
        grid=(-(-columns // (groups * TILE)),),
        in_specs=[state] * 3 + [pl.BlockSpec((rows, wide), lambda i: (0, begin // wide + i))],
        out_specs=(state,) * 3,
        out_shape=(jax.ShapeDtypeStruct(weight.shape, f32),) * 3,
        compiler_params=pltpu.CompilerParams(vmem_limit_bytes=VMEM_LIMIT),
        cost_estimate=SMALL,
    )(weight, first, second, summed)


def units_forward_kernel(count, pick, pick_ref, *refs):
    row_refs, grad_refs = refs[:count], refs[count : 2 * count]
    units_ref, down_ref = refs[2 * count : 2 * count + 2]
    rows_out, grads_out, hidden_ref, both_ref = refs[-4:]

    @pl.when(pl.program_id(0) == 0)
    def _():
        for k in range(count):
            if pick:

                @pl.when(pick_ref[0] == k)
                def _():
                    rows_out[...] = row_refs[k][...]
                    grads_out[...] = grad_refs[k][...]

            else:
                part = pl.ds(k * row_refs[k].shape[0], row_refs[k].shape[0])
                rows_out[part, :] = row_refs[k][...]
                grads_out[part, :] = grad_refs[k][...]

    rows = rows_out[...]
    gate_out = dot(rows, units_ref[:, :TILE], 1, 0)
    up_out = dot(rows, units_ref[:, TILE:], 1, 0)
    grad_hidden = dot(grads_out[...], down_ref[...], 1, 0)
    gate_sig = jax.nn.sigmoid(gate_out)
    gate_act = gate_out * gate_sig
    hidden_ref[...] = (gate_act * up_out).astype(bf16)
    both_ref[:, :TILE] = (
        grad_hidden * up_out * (gate_sig + gate_act * (1.0 - gate_sig))
    ).astype(bf16)
    both_ref[:, TILE:] = (grad_hidden * gate_act).astype(bf16)


def units_forward(rows, grads, units, buffers, index, pick=None):
    count, (length, width) = len(rows), rows[0].shape
    blocks = count if pick is None else 1
    steps = units.shape[1] // (3 * TILE)
    full = pl.BlockSpec((length, width), lambda i: (0, 0))
    kept = pl.BlockSpec((blocks * length, width), lambda i: (index, 0))
    held = () if buffers is None else buffers
    return pl.pallas_call(
        functools.partial(units_forward_kernel, count, pick is not None),
        grid=(steps,),
        in_specs=scalars(1)
        + [full] * (2 * count)
        + [
            pl.BlockSpec((width, 2 * TILE), lambda i: (0, i)),
            pl.BlockSpec((width, TILE), lambda i: (0, 2 * steps + i)),
        ]
        + [pl.BlockSpec(memory_space=pl.ANY)] * len(held),
        out_specs=(
            kept,
            kept,
            pl.BlockSpec((blocks * length, TILE), lambda i: (index, i)),
            pl.BlockSpec((blocks * length, 2 * TILE), lambda i: (index, i)),
        ),
        out_shape=(
            jax.ShapeDtypeStruct((4 * length, width), bf16),
            jax.ShapeDtypeStruct((4 * length, width), bf16),
            jax.ShapeDtypeStruct((4 * length, steps * TILE), bf16),
            jax.ShapeDtypeStruct((4 * length, steps * 2 * TILE), bf16),
        ),
        input_output_aliases={2 * count + 3 + k: k for k in range(len(held))},
        compiler_params=pltpu.CompilerParams(vmem_limit_bytes=VMEM_LIMIT),
        cost_estimate=SMALL,
    )(jnp.zeros((1,), jnp.int32) if pick is None else pick, *rows, *grads, units, units, *held)


def write_blocks(total, out_refs):
    rows = out_refs[0].shape[0]
    for k, ref in enumerate(out_refs):
        ref[...] = total[k * rows : (k + 1) * rows].astype(bf16)


def units_to_width_kernel(values_ref, units_ref, *out_refs):
    write_blocks(dot(values_ref[...], units_ref[...], 1, 1), out_refs)


def units_to_width(values, units, part, first, count):
    width = units.shape[0]
    block, columns = values.shape[0] // 4, values.shape[1]
    length = block * count
    return pl.pallas_call(
        units_to_width_kernel,
        grid=(width // TILE,),
        in_specs=[
            pl.BlockSpec((length, columns), lambda i: (first // count, 0)),
            pl.BlockSpec((TILE, columns), lambda i: (i, part)),
        ],
        out_specs=(pl.BlockSpec((block, TILE), lambda i: (0, i)),) * count,
        out_shape=(jax.ShapeDtypeStruct((block, width), bf16),) * count,
        compiler_params=pltpu.CompilerParams(vmem_limit_bytes=VMEM_LIMIT),
        cost_estimate=SMALL,
    )(values, units)


def units_add_kernel(*refs):
    out_ref = refs[-1]
    begin = 0
    for kept_ref, other_ref in zip(refs[0:-1:2], refs[1:-1:2]):
        columns = kept_ref.shape[2]
        out_ref[0, :, begin : begin + columns] = (
            kept_ref[0].astype(f32) + other_ref[0].astype(f32)
        ).astype(bf16)
        begin += columns


def units_add(*values):
    pairs, rows, _ = values[0].shape
    columns = sum(value.shape[2] for value in values[::2])
    return pl.pallas_call(
        units_add_kernel,
        grid=(pairs,),
        in_specs=[
            pl.BlockSpec((1, rows, value.shape[2]), lambda i: (i, 0, 0)) for value in values
        ],
        out_specs=pl.BlockSpec((1, rows, columns), lambda i: (i, 0, 0)),
        out_shape=jax.ShapeDtypeStruct((pairs, rows, columns), bf16),
        compiler_params=pltpu.CompilerParams(vmem_limit_bytes=VMEM_LIMIT),
        cost_estimate=SMALL,
    )(*values)


def units_gradient_kernel(core_ref, left_ref, right_ref, kept_ref, given_ref, total_ref):
    total_ref[...] = dot(left_ref[...], right_ref[...], 0, 0)
    core = core_ref[0]
    pairs, rows, _ = kept_ref.shape
    for p in range(pairs):
        for c, ref in ((core, kept_ref), (1 - core, given_ref)):
            at_row = pl.multiple_of((2 * p + c) * rows, 16)
            ref[p] = total_ref[pl.ds(at_row, rows), :].astype(bf16)


def units_gradient_parts(left, right, core):
    length, width = left.shape
    columns = right.shape[1]
    count = lax.axis_size("dp")
    rows = width // count
    tile = 2 * TILE if columns % (2 * TILE) == 0 else TILE
    out = pl.BlockSpec((count // 2, rows, tile), lambda i, c: (0, 0, i))
    shape = jax.ShapeDtypeStruct((count // 2, rows, columns), bf16)
    return pl.pallas_call(
        units_gradient_kernel,
        grid_spec=pltpu.PrefetchScalarGridSpec(
            num_scalar_prefetch=1,
            grid=(columns // tile,),
            in_specs=[
                pl.BlockSpec((length, width), lambda i, c: (0, 0)),
                pl.BlockSpec((length, tile), lambda i, c: (0, i)),
            ],
            out_specs=(out, out),
            scratch_shapes=[pltpu.VMEM((width, tile), f32)],
        ),
        out_shape=(shape, shape),
        compiler_params=pltpu.CompilerParams(vmem_limit_bytes=VMEM_LIMIT),
        cost_estimate=SMALL,
    )(core[None], left, right)


def swap_core(value):
    count = lax.axis_size("dp")
    return lax.ppermute(value, "dp", [(i, i ^ 1) for i in range(count)])


def swap_near(value):
    return lax.ppermute(value, "tensor", [(0, 1), (1, 0), (2, 3), (3, 2)])


def swap_far(value):
    return lax.ppermute(value, "tensor", [(0, 2), (2, 0), (1, 3), (3, 1)])


def swap_middle(value):
    return lax.ppermute(value, "tensor", [(1, 2), (2, 1)])


def swap_opposite(value):
    return lax.ppermute(value, "tensor", [(i, 3 - i) for i in range(4)])


def to_ends(value):
    return lax.ppermute(value, "tensor", [(1, 0), (2, 3)])


def from_ends(value):
    return lax.ppermute(value, "tensor", [(0, 1), (3, 2)])


def device_of(pair, core, z):
    return (2 * pair + core) * 4 + z


def owner_swap(value):
    perm = []
    for p in range(lax.axis_size("dp") // 2):
        for z in range(4):
            own = z // 2
            perm.append((device_of(p, own, z), device_of(p, own, z ^ 1)))
            perm.append((device_of(p, 1 - own, z), device_of(p, own, z ^ 2)))
    return lax.ppermute(value, AXES, perm)


def guest_swap(value):
    perm = []
    for p in range(lax.axis_size("dp") // 2):
        for z in range(4):
            guest = 1 - z // 2
            perm.append((device_of(p, guest, z), device_of(p, guest, z ^ 1)))
    return lax.ppermute(value, AXES, perm)


def heads_scatter_near(mine, other, z):
    def term(index):
        return at(mine, index, 0).astype(f32) + at(other, index, 0).astype(f32)

    away = swap_near(term(z ^ 3).astype(bf16))
    return term(z), term(z ^ 2), swap_near(term(z ^ 1).astype(bf16)), away


def heads_scatter_end(home, far, own, core):
    kept = jnp.where(own, home, far.astype(f32))
    return kept, swap_core(jnp.where(own, far, home.astype(bf16)))


def both_halves(kept, given, core):
    given = given.astype(f32)
    return jnp.concatenate(
        [jnp.where(core == 0, kept, given), jnp.where(core == 0, given, kept)], axis=0
    )


def gather_dp(value):
    bit = 1
    while bit < lax.axis_size("dp"):
        other = swap_dp(value, bit)
        upper = (lax.axis_index("dp") & bit) != 0
        value = jnp.concatenate(
            [jnp.where(upper, other, value), jnp.where(upper, value, other)], axis=0
        )
        bit *= 2
    return value


def gather_tensor(value, bit):
    other = lax.ppermute(value, "tensor", [(i, i ^ bit) for i in range(4)])
    upper = (lax.axis_index("tensor") & bit) != 0
    return jnp.concatenate(
        [jnp.where(upper, other, value), jnp.where(upper, value, other)], axis=1
    )


def sum_dp(value, first, last):
    bit = first
    while bit < last:
        value = value + swap_dp(value, bit)
        bit *= 2
    return value


def pair_groups():
    count = lax.axis_size("dp")
    return [list(range(c, count, 2)) for c in range(2)]


def swap_dp(value, mask):
    count = lax.axis_size("dp")
    return lax.ppermute(value, "dp", [(i, i ^ mask) for i in range(count)])


def gather_pairs_begin(value):
    if lax.axis_size("dp") != 8:
        return (lax.all_gather(value, "dp", axis=0, tiled=True, axis_index_groups=pair_groups()),)
    return value, swap_dp(value, 2), swap_dp(value, 4)


def gather_pairs_end(parts):
    if len(parts) == 1:
        return parts, jnp.zeros((1,), jnp.int32)
    value, by_two, by_four = parts
    pair = lax.axis_index("dp") >> 1
    rows = value.shape[0]
    half = rows // 2
    low, high = swap_dp(by_four[:half], 2), swap_dp(by_two[half:], 4)
    begins = jnp.stack([pair, pair ^ 1, pair ^ 2, pair ^ 3, pair ^ 3]) * rows
    begins = begins + jnp.array([0, 0, 0, 0, half], jnp.int32)
    return (value, by_two, by_four, low, high), begins


def at(value, index, axis):
    return lax.dynamic_index_in_dim(value, index, axis, keepdims=False)


def add_low(left, right):
    return (left.astype(f32) + right.astype(f32)).astype(bf16)


def scatter_pairs_begin(pieces):
    if len(pieces) == 1:
        return (
            lax.psum_scatter(
                pieces[0], "dp", scatter_dimension=0, tiled=True, axis_index_groups=pair_groups()
            ),
        )
    keep_x, send_x, keep_y, send_y = pieces
    return keep_x, swap_dp(send_x, 2), keep_y, swap_dp(send_y, 4)


def scatter_pairs_middle(pair, parts):
    if len(parts) == 1:
        return parts
    return pieces_call(pieces_middle_kernel, pair, parts, 4)


def scatter_pairs_send(parts):
    if len(parts) == 1:
        return parts
    keep_one, send_one, keep_two, send_two = parts
    return keep_one, swap_dp(send_one, 4), keep_two, swap_dp(send_two, 2)


def scatter_pairs_end(core, parts):
    if len(parts) == 1:
        rows = parts[0].shape[0] // 2
        return at(parts[0].reshape(2, rows, -1), core, 0), at(
            parts[0].reshape(2, rows, -1), core ^ 1, 0
        )
    return pieces_call(pieces_end_kernel, core[None], parts, 2)


def heads_pair(shard, far, own, core):
    kept = jnp.where(own, shard, far)
    other = swap_core(jnp.where(own, far, shard))
    return jnp.concatenate(
        [jnp.where(core == 0, kept, other), jnp.where(core == 0, other, kept)], axis=0
    )


def units_gradient(summed):
    return lax.psum_scatter(
        summed.reshape(-1, summed.shape[-1]),
        "dp",
        scatter_dimension=0,
        tiled=True,
        axis_index_groups=pair_groups(),
    )


def together(*values):
    return lax.optimization_barrier(values)


def after(value, earlier):
    return lax.optimization_barrier((value, earlier))[0]


def shards(
    block_in,
    out_grad,
    positions,
    qkv_weight,
    qkv_first,
    qkv_second,
    out_weight,
    out_first,
    out_second,
    gate_up,
    gate_up_first,
    gate_up_second,
    down_weight,
    down_first,
    down_second,
    norm_gains,
    norm_gains_first,
    norm_gains_second,
):
    model_width = block_in.shape[1]
    z = lax.axis_index("tensor")
    core = lax.axis_index("dp") & 1
    own = core == z // 2
    place = jnp.where(own, z, z ^ 2)[None]
    pair = (lax.axis_index("dp") >> 1)[None]
    pair = jnp.concatenate([pair & 1, pair >> 1])

    units_columns = gate_up.shape[2]
    heads_own = jnp.concatenate([qkv_weight.astype(bf16), out_weight.astype(bf16).T], axis=1)
    heads_own, gains_own, positions = together(heads_own, norm_gains[None], positions)
    heads_far = swap_far(heads_own)
    gains_dp = gather_dp(gains_own)[:, None]
    gains_all = gather_tensor(gather_tensor(gains_dp, 1), 2).reshape(1, -1)
    inverse_in = lax.rsqrt(jnp.mean(block_in * block_in, axis=-1, keepdims=True) + eps_norm)
    scaled_in = block_in * inverse_in
    head_positions = jnp.where(own, positions, swap_core(positions))
    scaled_b, heads_own, heads_far, head_positions, units_shard, grad_own, gains_all = together(
        scaled_in.astype(bf16),
        heads_own,
        heads_far,
        head_positions,
        pack_units(after(gate_up, gains_dp), down_weight.T),
        after(out_grad, gains_dp).astype(bf16),
        gains_all,
    )

    scaled_first = owner_swap(scaled_b)
    heads_parts = gather_pairs_begin(heads_pair(heads_own, heads_far, own, core))
    tables = rope_tables(head_positions, HEAD_DIMENSION)
    length = head_positions.shape[0]
    start = jnp.maximum(jnp.arange(length, dtype=jnp.int32) - head_positions, 0)
    start = start.astype(f32)[None]
    gain_attn = gains_all[:, :model_width]
    gain_q = gains_all[0, model_width : model_width + HEAD_DIMENSION]
    gain_k = gains_all[0, model_width + HEAD_DIMENSION : model_width + 2 * HEAD_DIMENSION]
    kv_local = qkv_weight.shape[1] // ((QUERY_GROUP + 2) * HEAD_DIMENSION)
    head_gains = jnp.concatenate(
        ([gain_q] * QUERY_GROUP + [gain_k, jnp.ones_like(gain_k)]) * kv_local
    )[None]
    gain_ffn = gains_all[:, model_width + 2 * HEAD_DIMENSION :]
    (
        scaled_first,
        heads_parts,
        gain_attn,
        head_gains,
        gain_ffn,
        units_shard,
        tables,
        start,
        grad_own,
    ) = together(
        scaled_first,
        heads_parts,
        gain_attn,
        head_gains,
        gain_ffn,
        units_shard,
        tables,
        start,
        grad_own,
    )

    scaled_second = guest_swap(scaled_first)
    scaled_mine = jnp.where(own, scaled_b, scaled_first)
    scaled_other = swap_core(scaled_mine)
    heads_blocks, heads_begins = gather_pairs_end(heads_parts)
    half, quarter = grad_own.shape[0] // 2, grad_own.shape[0] // 4
    grad_far = swap_far(grad_own[:quarter])
    (
        heads_blocks,
        scaled_second,
        scaled_mine,
        scaled_other,
        units_shard,
        grad_own,
        grad_far,
    ) = together(
        heads_blocks,
        scaled_second,
        scaled_mine,
        scaled_other,
        units_shard,
        grad_own,
        grad_far,
    )

    units = lax.all_gather(units_shard, "dp", axis=0, tiled=True)
    grad_far_rest = swap_far(grad_own[quarter:])
    grad_near = swap_near(grad_own)
    scaled_next = jnp.where(own, scaled_first, scaled_second)
    scaled_parts = (scaled_mine, scaled_next, scaled_other, swap_core(scaled_next))
    w_heads, normed_all, projected, queries_b, keys_b, values_b, attended, lse = attention_forward(
        place, scaled_parts, heads_blocks, heads_begins, gain_attn, head_gains, tables, start
    )
    branch_mine, branch_other = attention_branch(core[None], attended, w_heads)
    branch_mine, branch_other, grad_far, grad_far_rest, grad_near, grad_own = together(
        branch_mine, branch_other, grad_far, grad_far_rest, grad_near, grad_own
    )
    grad_far = jnp.concatenate([grad_far, grad_far_rest], axis=0)
    branch_other = swap_core(branch_other)
    grad_middle_part = swap_middle(grad_own)
    branch_mine, branch_other, grad_far = together(branch_mine, branch_other, grad_far)
    home, term_far, near, away = heads_scatter_near(branch_mine, branch_other, z)
    away, term_far, grad_middle_part = together(away, term_far, grad_middle_part)
    far = swap_far((term_far + away.astype(f32)).astype(bf16))
    far, home, near = together(far, home, near)
    middle = block_in + both_halves(
        *heads_scatter_end(home + near.astype(f32), far, own, core), core
    )

    inverse_mid = lax.rsqrt(jnp.mean(middle * middle, axis=-1, keepdims=True) + eps_norm)
    scaled_mid = middle * inverse_mid
    rows_own = (scaled_mid * gain_ffn).astype(bf16)
    rows_far = swap_far(rows_own)
    rows_near = swap_near(rows_own)
    inner = (z == 1) | (z == 2)
    buffers = units_forward((rows_own,), (grad_own,), units, None, 2)
    rows_far, rows_near, rows_own, buffers = together(rows_far, rows_near, rows_own, buffers)
    grad_ends = to_ends(grad_far)
    rows_ends = to_ends(rows_far)
    rows_middle = swap_middle(rows_own)
    buffers = units_forward((rows_near, rows_far), (grad_near, grad_far), units, buffers, 0)
    rows_all, grad_all, hidden_b, dboth = buffers
    back_near, back_far = units_to_width(dboth, units, 0, 0, 2)
    rows_ends, rows_middle, grad_ends, back_near, back_far, buffers = together(
        rows_ends, rows_middle, grad_ends, back_near, back_far, buffers
    )
    from_far = swap_far(back_far)
    from_near = swap_near(back_near)
    rows_all, grad_all, hidden_b, dboth = units_forward(
        (rows_ends, rows_middle),
        (grad_ends, grad_middle_part),
        units,
        buffers,
        3,
        inner.astype(jnp.int32)[None],
    )
    back_own, back_last = units_to_width(dboth, units, 0, 2, 2)
    down_kept, down_given = units_gradient_parts(grad_all, hidden_b, core)
    (
        from_near,
        from_far,
        back_last,
        back_own,
        rows_all,
        hidden_b,
        dboth,
        down_kept,
        down_given,
    ) = together(
        from_near,
        from_far,
        back_last,
        back_own,
        rows_all,
        hidden_b,
        dboth,
        down_kept,
        down_given,
    )
    from_last = swap_opposite(back_last)
    (down_last,) = units_to_width(hidden_b, units, 2, 3, 1)
    branch_ends = [from_ends(down_last[:half]), from_ends(down_last[half:])]
    both_kept, both_given = units_gradient_parts(rows_all, dboth, core)
    from_last, branch_ends, down_kept, down_given, both_kept, both_given, down_last = together(
        from_last, branch_ends, down_kept, down_given, both_kept, both_given, down_last
    )
    grad_normed_two = (
        back_own.astype(f32)
        + from_near.astype(f32)
        + from_far.astype(f32)
        + from_last.astype(f32)
    )

    grad_gain_ffn = jnp.sum(grad_normed_two * scaled_mid, axis=0)
    weighted = grad_normed_two * gain_ffn
    grad_middle = out_grad + inverse_mid * (
        weighted - scaled_mid * jnp.mean(weighted * scaled_mid, axis=-1, keepdims=True)
    )
    grad_mid_b, grad_gain_ffn, hidden_b, down_kept, down_given, both_kept, both_given = together(
        grad_middle.astype(bf16),
        grad_gain_ffn,
        hidden_b,
        down_kept,
        down_given,
        both_kept,
        both_given,
    )
    grad_mid_first = owner_swap(grad_mid_b)
    units_sum = units_add(both_kept, swap_core(both_given), down_kept, swap_core(down_given))
    down_near, down_far, down_own = units_to_width(hidden_b, units, 2, 0, 3)
    down_far = add_low(down_far, jnp.concatenate(branch_ends, axis=0))
    grad_mid_first, units_sum, down_near, down_far, down_own = together(
        grad_mid_first, units_sum, down_near, down_far, down_own
    )
    units_sum = units_gradient(units_sum)
    grad_mid_second = guest_swap(grad_mid_first)
    branch_far = swap_far(down_far[: 3 * half // 4])
    grad_mid_mine = jnp.where(own, grad_mid_b, grad_mid_first)
    grad_mid_other = swap_core(grad_mid_mine)
    grad_mid_second, grad_mid_mine, grad_mid_other, branch_far, down_far = together(
        grad_mid_second, grad_mid_mine, grad_mid_other, branch_far, down_far
    )
    grad_mid_next = jnp.where(own, grad_mid_first, grad_mid_second)
    grad_mid_parts = (grad_mid_mine, grad_mid_next, grad_mid_other, swap_core(grad_mid_next))

    branch_far_rest = swap_far(down_far[3 * half // 4 :])
    branch_middle = swap_middle(down_last)
    grad_attended, row_dot, *out_pieces = attention_turn(
        place, pair, grad_mid_parts, w_heads, attended
    )
    branch_near = swap_near(after(down_near, row_dot))
    out_parts = scatter_pairs_begin(tuple(out_pieces))
    grad_projected, part_mine, part_other, head_sums, gain_sums = attention_backward(
        core[None],
        queries_b,
        keys_b,
        values_b,
        grad_attended,
        lse,
        row_dot,
        start,
        projected,
        head_gains,
        *tables,
        w_heads,
        normed_all,
        gain_attn,
    )
    (
        grad_projected,
        part_mine,
        part_other,
        branch_far,
        branch_far_rest,
        branch_near,
        branch_middle,
        out_parts,
    ) = together(
        grad_projected,
        part_mine,
        part_other,
        branch_far,
        branch_far_rest,
        branch_near,
        branch_middle,
        out_parts,
    )

    part_other = swap_core(part_other)
    qkv_pieces = heads_gradient(pair, normed_all, grad_projected)
    part_mine, part_other, qkv_pieces, out_parts, branch_far = together(
        part_mine, part_other, qkv_pieces, out_parts, branch_far
    )
    home, term_far, near, away = heads_scatter_near(part_mine, part_other, z)
    qkv_parts = scatter_pairs_begin(qkv_pieces)
    out_parts = scatter_pairs_middle(pair, out_parts)
    gain_sums, head_sums = after((gain_sums, head_sums), qkv_pieces)
    head_sums = head_sums.reshape(-1, QUERY_GROUP + 2, HEAD_DIMENSION)
    gain_total = jnp.concatenate(
        [
            gain_sums[0],
            jnp.sum(head_sums[:, :QUERY_GROUP], axis=(0, 1)),
            jnp.sum(head_sums[:, QUERY_GROUP], axis=0),
            grad_gain_ffn,
        ]
    )
    gain_total = sum_dp(gain_total, 1, 2)
    block_out = (
        middle
        + down_own.astype(f32)
        + branch_near.astype(f32)
        + branch_middle.astype(f32)
        + jnp.concatenate([branch_far, branch_far_rest], axis=0).astype(f32)
    )
    far_term = (term_far + away.astype(f32)).astype(bf16)
    far = swap_far(far_term)
    qkv_parts = scatter_pairs_middle(pair, after(qkv_parts, (far_term, gain_total, block_out)))
    out_parts = scatter_pairs_send(after(out_parts, qkv_parts))
    qkv_parts = scatter_pairs_send(qkv_parts)
    down_new = adam_units(
        down_weight.T[None],
        down_first.T[None],
        down_second.T[None],
        after(units_sum, (near, out_parts[0])),
        2 * units_sum.shape[1] // 3,
    )
    gain_total = after(gain_total, down_new)
    gain_total = sum_dp(gain_total, 2, lax.axis_size("dp") // 2)
    gain_last = swap_dp(gain_total, lax.axis_size("dp") // 2)
    qkv_kept, qkv_given = scatter_pairs_end(core, after(qkv_parts, (down_new, far)))
    gain_total = gain_total + after(gain_last, qkv_kept)
    gain_last = swap_near(gain_total)
    out_kept, out_given = scatter_pairs_end(core, after(out_parts, (down_new, far)))
    qkv_other, out_other = swap_core(qkv_given), swap_core(out_given)
    gain_total = gain_total + after(gain_last, out_kept)
    heads_away = jnp.concatenate(
        [jnp.where(own, qkv_other, qkv_kept), jnp.where(own, out_other, out_kept)], axis=1
    )
    kept, given = heads_scatter_end(home + near.astype(f32), far, own, core)
    units_sum = after(units_sum, heads_away)
    gain_last = swap_far(gain_total)
    heads_away = swap_far(heads_away)
    gain_total = gain_total + gain_last
    in_grad = input_gradient(core[None], kept, given, block_in, gain_attn, grad_middle)
    gate_up_new = adam_units(gate_up, gate_up_first, gate_up_second, units_sum, 0)
    heads_away, in_grad, gate_up_new = together(heads_away, in_grad, gate_up_new)
    down_new = tuple(value[0].T for value in down_new)
    qkv_columns = qkv_weight.shape[1]
    sum_qkv = jnp.where(own, qkv_kept, qkv_other).astype(f32) + heads_away[
        :, :qkv_columns
    ].astype(f32)
    sum_out = jnp.where(own, out_kept, out_other).astype(f32) + heads_away[
        :, qkv_columns:
    ].astype(f32)
    sum_out = sum_out.T
    gain_count = norm_gains.shape[0]
    gain_at = (lax.axis_index("dp") * 4 + z) * gain_count
    gain_grads = lax.dynamic_slice_in_dim(gain_total, gain_at, gain_count)

    qkv_new = adam_step(qkv_weight, qkv_first, qkv_second, sum_qkv, rate_matrix, decay_matrix)
    out_new = adam_step(out_weight, out_first, out_second, sum_out, rate_output, decay_matrix)
    gains_new = adam_step(
        norm_gains, norm_gains_first, norm_gains_second, gain_grads, rate_gains, 0.0
    )
    return (block_out, in_grad, *qkv_new, *out_new, *gate_up_new, *down_new, *gains_new)


def solution(mesh):
    tokens = P(("dp", "tensor"), None)
    by_rows = (P("dp", "tensor"),) * 3
    by_columns = (P("tensor", "dp"),) * 3
    stacked = (P(None, "dp", "tensor"),) * 3
    gains = (P(("dp", "tensor")),) * 3
    states = by_rows + by_columns + stacked + by_columns + gains
    return jax.shard_map(
        shards,
        mesh=mesh,
        in_specs=(tokens, tokens, P("dp")) + states,
        out_specs=(tokens, tokens) + states,
        check_vma=False,
    )
```

```python
import functools

import jax
import jax.numpy as jnp
from jax import lax
from jax.experimental import pallas as pl
from jax.experimental.pallas import tpu as pltpu
from jax.sharding import PartitionSpec as P

HEAD_DIMENSION = 64
STEP = 10
QUERY_GROUP = 3
AXES = ("dp", "tensor")

eps_norm = 1e-05
rope_base = 1000000.0
beta_one = 0.9
beta_two = 0.999
adam_eps = 1e-08
decay_matrix = 0.1
rate_matrix = 0.03
rate_output = 0.15
rate_gains = 0.8
bf16 = jnp.bfloat16
f32 = jnp.float32
VMEM_LIMIT = 58 * 1024 * 1024
SMALL = pl.CostEstimate(flops=1000, bytes_accessed=1000, transcendentals=0)


def whole(value):
    zeros = (0,) * len(value.shape)
    return pl.BlockSpec(value.shape, lambda i: zeros, pipeline_mode=pl.Buffered(1))


def scalars(count):
    return [pl.BlockSpec(memory_space=pltpu.SMEM)] * count


def dot(left, right, left_dim, right_dim):
    return lax.dot_general(
        left, right, (((left_dim,), (right_dim,)), ((), ())), preferred_element_type=f32
    )


def norm_rows(row_block, gain_vec):
    inverse = lax.rsqrt(jnp.mean(row_block * row_block, axis=-1, keepdims=True) + eps_norm)
    return row_block * inverse * gain_vec


def rope_tables(positions, head_size):
    inverse_freq = rope_base ** (-(jnp.arange(head_size // 2, dtype=f32) * 2.0) / head_size)
    angles = positions.astype(f32)[:, None] * inverse_freq[None, :]
    cos_part, sin_part = jnp.cos(angles), jnp.sin(angles)
    return (
        jnp.concatenate([cos_part] * 4, axis=1),
        jnp.concatenate([-sin_part, sin_part] * 2, axis=1),
    )


def adam_step(weight, first_old, second_old, gradient, step_rate, decay_rate):
    first_new = beta_one * first_old + (1.0 - beta_one) * gradient
    second_new = beta_two * second_old + (1.0 - beta_two) * gradient * gradient
    fix_one = 1.0 - beta_one**STEP
    fix_two = 1.0 - beta_two**STEP
    update = first_new / fix_one / (jnp.sqrt(second_new / fix_two) + adam_eps)
    return (weight - step_rate * (update + decay_rate * weight), first_new, second_new)


PAIR = 2 * HEAD_DIMENSION


def lanes_of(value):
    return lax.broadcasted_iota(jnp.int32, value.shape, 1)


def swap_halves(value):
    half = HEAD_DIMENSION // 2
    low = lanes_of(value) % HEAD_DIMENSION < half
    return jnp.where(low, pltpu.roll(value, PAIR - half, 1), pltpu.roll(value, half, 1))


def two_parts(value):
    high = value.astype(bf16)
    return high, (value - high.astype(f32)).astype(bf16)


def head_means(value):
    shape = (PAIR, PAIR)
    one, two = (lax.broadcasted_iota(jnp.int32, shape, d) // HEAD_DIMENSION for d in (0, 1))
    weights = jnp.where(one == two, 1.0 / HEAD_DIMENSION, 0.0).astype(bf16)
    high, low = two_parts(value)
    return dot(high, weights, 1, 0) + dot(low, weights, 1, 0)


def is_value(index, value):
    at_head = [(2 * index + k) % (QUERY_GROUP + 2) == QUERY_GROUP + 1 for k in range(2)]
    if not any(at_head):
        return None
    return (lanes_of(value) < HEAD_DIMENSION) == at_head[0]


def unless(mask, value, other):
    return value if mask is None else jnp.where(mask, other, value)


def as_row(column):
    return jnp.broadcast_to(column, (column.shape[0], 128)).T[:1, :]


def as_column(row):
    return jnp.broadcast_to(row, (128, row.shape[1])).T[:, :1]


def place_parts(place_ref, part_refs, whole_ref, scale):
    rows = part_refs[0].shape[0]
    for j, part_ref in enumerate(part_refs):
        at_row = pl.multiple_of((j ^ place_ref[0]) * rows, rows)
        value = part_ref[...]
        if scale is not None:
            value = (value.astype(f32) * scale).astype(bf16)
        whole_ref[pl.ds(at_row, rows), :] = value


def split_halves(core_ref, value, stage_ref, mine_ref, other_ref, index):
    half = value.shape[0] // 2
    stage_ref[...] = value
    core = core_ref[0]
    mine_ref[index] = stage_ref[pl.ds(pl.multiple_of(core * half, half), half), :]
    other_ref[index] = stage_ref[pl.ds(pl.multiple_of((1 - core) * half, half), half), :]


def place_blocks(begins_ref, block_refs, whole_ref):
    for k, block_ref in enumerate(block_refs):
        begin = pl.multiple_of(begins_ref[k], 16)
        whole_ref[pl.ds(begin, block_ref.shape[0]), :] = block_ref[...]


def attention_forward_kernel(count, place_ref, begins_ref, *refs):
    part_refs, refs = refs[:4], refs[4:]
    block_refs, refs = refs[:count], refs[count:]
    (
        gain_ref,
        head_gain_ref,
        cos_ref,
        sin_ref,
        start_ref,
        weight_ref,
        normed_ref,
        projected_ref,
        q_ref,
        k_ref,
        v_ref,
        out_ref,
        lse_ref,
    ) = refs
    place_blocks(begins_ref, block_refs, weight_ref)
    size = HEAD_DIMENSION
    heads, length, _ = q_ref.shape
    group = QUERY_GROUP
    kv = heads // group
    block = min(256, length)
    place_parts(place_ref, part_refs, normed_ref, gain_ref[...])
    for i in range(length // block):
        here = pl.ds(i * block, block)
        projected = dot(normed_ref[here, :], weight_ref[:, : projected_ref.shape[1]], 1, 0)
        projected_ref[here, :] = projected
        cos_part, sin_part = cos_ref[here, :], sin_ref[here, :]
        for t in range(projected.shape[1] // PAIR):
            raw = projected[:, t * PAIR : (t + 1) * PAIR]
            keep = is_value(t, raw)
            inverse = unless(keep, lax.rsqrt(head_means(raw * raw) + eps_norm), 1.0)
            normed = raw * inverse * head_gain_ref[:, t * PAIR : (t + 1) * PAIR]
            turned = normed * unless(keep, cos_part, 1.0) + swap_halves(normed) * unless(
                keep, sin_part, 0.0
            )
            turned = turned.astype(bf16)
            for k in range(2):
                j, g = divmod(2 * t + k, group + 2)
                piece = turned[:, k * size : (k + 1) * size]
                if g < group:
                    q_ref[j * group + g, here, :] = piece * jnp.asarray(size**-0.5, bf16)
                elif g == group:
                    k_ref[j, here, :] = piece
                else:
                    v_ref[j, here, :] = piece
    row_at = lax.broadcasted_iota(jnp.int32, (block, block), 0)
    col_at = lax.broadcasted_iota(jnp.int32, (block, block), 1)
    causal = jnp.concatenate([col_at <= row_at] * group, axis=0)
    col_all = lax.broadcasted_iota(jnp.int32, (group * block, block), 1).astype(f32)
    ones = jnp.ones((block, size), bf16)
    for j in range(kv):
        for i in range(length // block):
            here = pl.ds(i * block, block)
            queries = jnp.concatenate(
                [q_ref[j * group + g, here, :] for g in range(group)], axis=0
            )
            start = jnp.concatenate([as_column(start_ref[:, here])] * group, axis=0)
            total = jnp.zeros((group * block, 2 * size), f32)
            for b in range(i + 1):
                there = pl.ds(b * block, block)
                scores = dot(queries, k_ref[j, there, :], 1, 1)
                allowed = col_all >= start - b * block
                if b == i:
                    allowed = allowed & causal
                weights = jnp.where(allowed, jnp.exp(scores), 0.0).astype(bf16)
                values = jnp.concatenate([v_ref[j, there, :], ones], axis=1)
                total = total + dot(weights, values, 1, 0)
            row_sum = total[:, size : size + 1]
            output = (total[:, :size] / row_sum).astype(bf16)
            log_sum = jnp.log(row_sum)
            for g in range(group):
                h = j * group + g
                part = slice(g * block, (g + 1) * block)
                out_ref[here, h * size : (h + 1) * size] = output[part]
                lse_ref[h, :, here] = as_row(log_sum[part])


def attention_branch_kernel(core_ref, attended_ref, weight_ref, mine_ref, other_ref, stage_ref):
    shard, columns = attended_ref.shape[0] // 4, attended_ref.shape[1]
    for i in range(4):
        value = dot(
            attended_ref[i * shard : (i + 1) * shard, :], weight_ref[:, -columns:], 1, 1
        )
        split_halves(core_ref, value.astype(bf16), stage_ref, mine_ref, other_ref, i)


def attention_forward(place, parts, blocks, begins, gain_attn, head_gains, tables, start):
    rows, width = parts[0].shape
    length = 4 * rows
    size = HEAD_DIMENSION
    columns = blocks[0].shape[1]
    kv = columns // ((2 * QUERY_GROUP + 2) * size)
    heads = kv * QUERY_GROUP
    operands = (*parts, *blocks, gain_attn, head_gains, *tables, start)
    results = (
        jax.ShapeDtypeStruct((width, columns), bf16),
        jax.ShapeDtypeStruct((length, width), bf16),
        jax.ShapeDtypeStruct((length, (heads + 2 * kv) * size), f32),
        jax.ShapeDtypeStruct((heads, length, size), bf16),
        jax.ShapeDtypeStruct((kv, length, size), bf16),
        jax.ShapeDtypeStruct((kv, length, size), bf16),
        jax.ShapeDtypeStruct((length, heads * size), bf16),
        jax.ShapeDtypeStruct((heads, 1, length), f32),
    )
    return pl.pallas_call(
        functools.partial(attention_forward_kernel, len(blocks)),
        grid=(1,),
        in_specs=scalars(2) + [whole(value) for value in operands],
        out_specs=tuple(whole(value) for value in results),
        out_shape=results,
        compiler_params=pltpu.CompilerParams(vmem_limit_bytes=VMEM_LIMIT),
        cost_estimate=SMALL,
    )(place, begins, *operands)


def attention_branch(core, attended, weight):
    length = attended.shape[0]
    width = weight.shape[0]
    half = jax.ShapeDtypeStruct((4, length // 8, width), bf16)
    return pl.pallas_call(
        attention_branch_kernel,
        grid=(1,),
        in_specs=scalars(1) + [whole(attended), whole(weight)],
        out_specs=(whole(half), whole(half)),
        out_shape=(half, half),
        scratch_shapes=[pltpu.VMEM((length // 4, width), bf16)],
        compiler_params=pltpu.CompilerParams(vmem_limit_bytes=VMEM_LIMIT),
        cost_estimate=SMALL,
    )(core, attended, weight)


def split_pieces(total_ref, pair_ref, piece_refs):
    if len(piece_refs) == 1:
        piece_refs[0][...] = total_ref[...].astype(bf16)
        return
    keep_x, send_x, keep_y, send_y = piece_refs
    rows = keep_x.shape[1]
    x, y = pair_ref[0], pair_ref[1]
    for k in range(2):
        for ref, pair, core in (
            (keep_x, 2 * k + x, 0),
            (send_x, 2 * k + 1 - x, 0),
            (keep_y, 2 * y + k, 1),
            (send_y, 2 * (1 - y) + k, 1),
        ):
            begin = pl.multiple_of((2 * pair + core) * rows, 16)
            ref[k] = total_ref[pl.ds(begin, rows), :].astype(bf16)


def pieces_shapes(width, columns):
    if lax.axis_size("dp") != 8:
        return (jax.ShapeDtypeStruct((width, columns), bf16),)
    return (jax.ShapeDtypeStruct((2, width // 8, columns), bf16),) * 4


def heads_gradient_kernel(pair_ref, left_ref, right_ref, *refs):
    refs[-1][...] = dot(left_ref[...], right_ref[...], 0, 0)
    split_pieces(refs[-1], pair_ref, refs[:-1])


def heads_gradient(pair, left, right):
    width, columns = left.shape[1], right.shape[1]
    results = pieces_shapes(width, columns)
    return pl.pallas_call(
        heads_gradient_kernel,
        grid=(1,),
        in_specs=scalars(1) + [whole(left), whole(right)],
        out_specs=tuple(whole(value) for value in results),
        out_shape=results,
        scratch_shapes=[pltpu.VMEM((width, columns), f32)],
        compiler_params=pltpu.CompilerParams(vmem_limit_bytes=VMEM_LIMIT),
        cost_estimate=SMALL,
    )(pair, left, right)


def add_refs(left, right):
    return (left.astype(f32) + right.astype(f32)).astype(bf16)


def pieces_middle_kernel(
    pair_ref, keep_x, got_x, keep_y, got_y, keep_one, send_one, keep_two, send_two
):
    x, y = pair_ref[0], pair_ref[1]
    keep_one[...] = add_refs(keep_x[y], got_x[y])
    send_one[...] = add_refs(keep_x[1 - y], got_x[1 - y])
    keep_two[...] = add_refs(keep_y[x], got_y[x])
    send_two[...] = add_refs(keep_y[1 - x], got_y[1 - x])


def pieces_end_kernel(core_ref, keep_one, got_one, keep_two, got_two, kept, given):
    @pl.when(core_ref[0] == 0)
    def _():
        kept[...] = add_refs(keep_one[...], got_one[...])
        given[...] = add_refs(keep_two[...], got_two[...])

    @pl.when(core_ref[0] != 0)
    def _():
        given[...] = add_refs(keep_one[...], got_one[...])
        kept[...] = add_refs(keep_two[...], got_two[...])


def pieces_call(kernel, scalar, values, count):
    result = jax.ShapeDtypeStruct(values[0].shape[-2:], bf16)
    vmem = pl.BlockSpec(memory_space=pltpu.VMEM)
    return pl.pallas_call(
        kernel,
        in_specs=scalars(1) + [vmem] * len(values),
        out_specs=(vmem,) * count,
        out_shape=(result,) * count,
        compiler_params=pltpu.CompilerParams(vmem_limit_bytes=VMEM_LIMIT),
        cost_estimate=SMALL,
    )(scalar, *values)


def attention_turn_kernel(place_ref, pair_ref, *refs):
    part_refs, (weight_ref, out_ref, grads_ref, dot_ref) = refs[:4], refs[4:8]
    piece_refs, (whole_ref, total_ref) = refs[8:-2], refs[-2:]
    size = HEAD_DIMENSION
    place_parts(place_ref, part_refs, whole_ref, None)
    heads, length, _ = grads_ref.shape
    block = min(256, length)
    shape = (dot_ref.shape[0], heads * size)
    of_head = (
        lax.broadcasted_iota(jnp.int32, shape, 0)
        == lax.broadcasted_iota(jnp.int32, shape, 1) // size
    ).astype(bf16)
    for i in range(length // block):
        here = pl.ds(i * block, block)
        grads = dot(whole_ref[here, :], weight_ref[:, -heads * size :], 1, 0).astype(bf16)
        high, low = two_parts(grads.astype(f32) * out_ref[here, :].astype(f32))
        dot_ref[:, here] = dot(of_head, high, 1, 1) + dot(of_head, low, 1, 1)
        for h in range(heads):
            grads_ref[h, here, :] = grads[:, h * size : (h + 1) * size]
    total_ref[...] = dot(whole_ref[...], out_ref[...], 0, 0)
    split_pieces(total_ref, pair_ref, piece_refs)


def attention_turn(place, pair, parts, weight, attended):
    rows, width = parts[0].shape
    length, columns = attended.shape
    heads = columns // HEAD_DIMENSION
    operands = (*parts, weight, attended)
    results = (
        jax.ShapeDtypeStruct((heads, length, HEAD_DIMENSION), bf16),
        jax.ShapeDtypeStruct((-(-heads // 8) * 8, length), f32),
        *pieces_shapes(width, columns),
    )
    return pl.pallas_call(
        attention_turn_kernel,
        grid=(1,),
        in_specs=scalars(2) + [whole(value) for value in operands],
        out_specs=tuple(whole(value) for value in results),
        out_shape=results,
        scratch_shapes=[pltpu.VMEM((length, width), bf16), pltpu.VMEM((width, columns), f32)],
        compiler_params=pltpu.CompilerParams(vmem_limit_bytes=VMEM_LIMIT),
        cost_estimate=SMALL,
    )(place, pair, *operands)


def attention_backward_kernel(
    core_ref,
    q_ref,
    k_ref,
    v_ref,
    g_ref,
    lse_ref,
    dot_ref,
    start_ref,
    projected_ref,
    head_gain_ref,
    cos_ref,
    sin_ref,
    weight_ref,
    normed_ref,
    gain_ref,
    back_ref,
    mine_ref,
    other_ref,
    head_sum_ref,
    gain_sum_ref,
    grad_ref,
    dk_ref,
    dv_ref,
    stage_ref,
):
    size = HEAD_DIMENSION
    heads, length, _ = q_ref.shape
    group = QUERY_GROUP
    kv = heads // group
    block = min(256, length)
    lanes = group * block
    key_at = lax.broadcasted_iota(jnp.int32, (block, block), 0)
    row_at = lax.broadcasted_iota(jnp.int32, (block, block), 1)
    causal = jnp.concatenate([key_at <= row_at] * group, axis=1)
    key_all = lax.broadcasted_iota(jnp.int32, (block, lanes), 0).astype(f32)
    dk_ref[...] = jnp.zeros_like(dk_ref)
    dv_ref[...] = jnp.zeros_like(dv_ref)
    head_sum_ref[...] = jnp.zeros_like(head_sum_ref)
    gain_sum_ref[...] = jnp.zeros_like(gain_sum_ref)
    for j in range(kv):
        for i in range(length // block):
            here = pl.ds(i * block, block)
            head = [j * group + g for g in range(group)]
            queries = jnp.concatenate([q_ref[h, here, :] for h in head], axis=0)
            grads = jnp.concatenate([g_ref[h, here, :] for h in head], axis=0)
            lse = jnp.concatenate([lse_ref[h, :, here] for h in head], axis=1)
            row_dot = jnp.concatenate([dot_ref[h : h + 1, here] for h in head], axis=1)
            start = jnp.concatenate([start_ref[:, here]] * group, axis=1)
            dq = jnp.zeros((size, lanes), f32)
            for b in range(i + 1):
                there = pl.ds(b * block, block)
                keys = k_ref[j, there, :]
                scores = dot(keys, queries, 1, 1)
                allowed = key_all >= start - b * block
                if b == i:
                    allowed = allowed & causal
                probs = jnp.where(allowed, jnp.exp(scores - lse), 0.0)
                grad_probs = dot(v_ref[j, there, :], grads, 1, 1)
                grad_scores = (probs * (grad_probs - row_dot)).astype(bf16)
                dv_ref[j, there, :] += dot(probs.astype(bf16), grads, 1, 0)
                dk_ref[j, there, :] += dot(grad_scores, queries, 1, 0)
                dq = dq + dot(keys, grad_scores, 0, 0)
            for g in range(group):
                column = (j * (group + 2) + g) * size
                grad_ref[here, column : column + size] = (
                    dq[:, g * block : (g + 1) * block].T * size**-0.5
                )
        key_column = (j * (group + 2) + group) * size
        grad_ref[:, key_column : key_column + size] = dk_ref[j]
        grad_ref[:, key_column + size : key_column + 2 * size] = dv_ref[j]
    shard = length // 4
    for i in range(4):
        here = pl.ds(i * shard, shard)
        cos_part, sin_part = cos_ref[here, :], sin_ref[here, :]
        for t in range(back_ref.shape[1] // PAIR):
            columns = slice(t * PAIR, (t + 1) * PAIR)
            given = grad_ref[here, columns]
            keep = is_value(t, given)
            grad = given * unless(keep, cos_part, 1.0) + swap_halves(
                given * unless(keep, sin_part, 0.0)
            )
            raw = projected_ref[here, columns]
            inverse = lax.rsqrt(head_means(raw * raw) + eps_norm)
            scaled = raw * inverse
            head_sum_ref[:, columns] += jnp.sum(grad * scaled, axis=0, keepdims=True)
            weighted = grad * head_gain_ref[:, columns]
            back = inverse * (weighted - scaled * head_means(weighted * scaled))
            back_ref[here, columns] = unless(keep, back, given).astype(bf16)
        term = dot(back_ref[here, :], weight_ref[:, : back_ref.shape[1]], 1, 1)
        gain_sum_ref[...] += jnp.sum(
            term * normed_ref[here, :].astype(f32), axis=0, keepdims=True
        )
        split_halves(core_ref, term.astype(bf16), stage_ref, mine_ref, other_ref, i)
    gain_sum_ref[...] = gain_sum_ref[...] / gain_ref[...]


def attention_backward(core, queries, keys, values, grads, lse, row_dot, start, projected, *rest):
    heads, length, size = queries.shape
    kv = keys.shape[0]
    normed = rest[-2]
    width = normed.shape[1]
    half = jax.ShapeDtypeStruct((4, length // 8, width), bf16)
    operands = (queries, keys, values, grads, lse, row_dot, start, projected) + rest
    results = (
        jax.ShapeDtypeStruct(projected.shape, bf16),
        half,
        half,
        jax.ShapeDtypeStruct((1, projected.shape[1]), f32),
        jax.ShapeDtypeStruct((1, width), f32),
    )
    return pl.pallas_call(
        attention_backward_kernel,
        grid=(1,),
        in_specs=scalars(1) + [whole(value) for value in operands],
        out_specs=tuple(whole(value) for value in results),
        out_shape=results,
        scratch_shapes=[
            pltpu.VMEM(projected.shape, f32),
            pltpu.VMEM((kv, length, size), f32),
            pltpu.VMEM((kv, length, size), f32),
            pltpu.VMEM((length // 4, width), bf16),
        ],
        compiler_params=pltpu.CompilerParams(vmem_limit_bytes=VMEM_LIMIT),
        cost_estimate=SMALL,
    )(core, *operands)


def input_gradient_kernel(core_ref, kept_ref, given_ref, rows_ref, gain_ref, middle_ref, out_ref):
    half = kept_ref.shape[0]
    core = core_ref[0]
    for index, ref in ((core, kept_ref), (1 - core, given_ref)):
        part = pl.ds(pl.multiple_of(index * half, half), half)
        rows = rows_ref[part, :]
        inverse = lax.rsqrt(jnp.mean(rows * rows, axis=1, keepdims=True) + eps_norm)
        scaled = rows * inverse
        weighted = ref[...].astype(f32) * gain_ref[...]
        out_ref[part, :] = middle_ref[part, :] + inverse * (
            weighted - scaled * jnp.mean(weighted * scaled, axis=1, keepdims=True)
        )


def input_gradient(core, kept, given, rows, gain, middle):
    vmem = pl.BlockSpec(memory_space=pltpu.VMEM)
    return pl.pallas_call(
        input_gradient_kernel,
        in_specs=scalars(1) + [vmem] * 5,
        out_specs=vmem,
        out_shape=jax.ShapeDtypeStruct(rows.shape, f32),
        compiler_params=pltpu.CompilerParams(vmem_limit_bytes=VMEM_LIMIT),
        cost_estimate=SMALL,
    )(core, kept, given, rows, gain, middle)


TILE = 256


def pack_units_kernel(both_ref, down_ref, out_ref):
    columns = both_ref.shape[2]
    rows = both_ref.shape[1]
    steps = out_ref.shape[1] // (3 * TILE)
    for i in range(steps):
        first, last = i * TILE, min(columns, (i + 1) * TILE)
        parts = (both_ref[0, :, first:last], both_ref[1, :, first:last], down_ref[:, first:last])
        for part, at_column in zip(parts, (2 * i * TILE, (2 * i + 1) * TILE, (2 * steps + i) * TILE)):
            if last - first < TILE:
                part = jnp.concatenate(
                    [part, jnp.zeros((rows, TILE - (last - first)), f32)], axis=1
                )
            out_ref[:, at_column : at_column + TILE] = part.astype(bf16)


def pack_units(gate_up, down):
    rows, columns = gate_up.shape[1:]
    steps = -(-columns // TILE)
    vmem = pl.BlockSpec(memory_space=pltpu.VMEM)
    return pl.pallas_call(
        pack_units_kernel,
        in_specs=[vmem, vmem],
        out_specs=vmem,
        out_shape=jax.ShapeDtypeStruct((rows, steps * 3 * TILE), bf16),
        compiler_params=pltpu.CompilerParams(vmem_limit_bytes=VMEM_LIMIT),
        cost_estimate=SMALL,
    )(gate_up, down)


def adam_kernel(weight_ref, first_ref, second_ref, sum_ref, *out_refs):
    parts = weight_ref.shape[0]
    groups = sum_ref.shape[1] // (parts * TILE)
    for p in range(parts):
        for k in range(groups):
            columns = slice(k * TILE, (k + 1) * TILE)
            at_sum = (k * parts + p) * TILE
            new = adam_step(
                weight_ref[p, :, columns],
                first_ref[p, :, columns],
                second_ref[p, :, columns],
                sum_ref[:, at_sum : at_sum + TILE].astype(f32),
                rate_matrix,
                decay_matrix,
            )
            for ref, value in zip(out_refs, new):
                ref[p, :, columns] = value


def adam_units(weight, first, second, summed, begin):
    parts, rows, columns = weight.shape
    groups = 2
    state = pl.BlockSpec((parts, rows, groups * TILE), lambda i: (0, 0, i))
    wide = parts * groups * TILE
    return pl.pallas_call(
        adam_kernel,
        grid=(-(-columns // (groups * TILE)),),
        in_specs=[state] * 3 + [pl.BlockSpec((rows, wide), lambda i: (0, begin // wide + i))],
        out_specs=(state,) * 3,
        out_shape=(jax.ShapeDtypeStruct(weight.shape, f32),) * 3,
        compiler_params=pltpu.CompilerParams(vmem_limit_bytes=VMEM_LIMIT),
        cost_estimate=SMALL,
    )(weight, first, second, summed)


def units_forward_kernel(count, pick, pick_ref, *refs):
    row_refs, grad_refs = refs[:count], refs[count : 2 * count]
    units_ref, down_ref = refs[2 * count : 2 * count + 2]
    rows_out, grads_out, hidden_ref, both_ref = refs[-4:]

    @pl.when(pl.program_id(0) == 0)
    def _():
        for k in range(count):
            if pick:

                @pl.when(pick_ref[0] == k)
                def _():
                    rows_out[...] = row_refs[k][...]
                    grads_out[...] = grad_refs[k][...]

            else:
                part = pl.ds(k * row_refs[k].shape[0], row_refs[k].shape[0])
                rows_out[part, :] = row_refs[k][...]
                grads_out[part, :] = grad_refs[k][...]

    rows = rows_out[...]
    gate_out = dot(rows, units_ref[:, :TILE], 1, 0)
    up_out = dot(rows, units_ref[:, TILE:], 1, 0)
    grad_hidden = dot(grads_out[...], down_ref[...], 1, 0)
    gate_sig = jax.nn.sigmoid(gate_out)
    gate_act = gate_out * gate_sig
    hidden_ref[...] = (gate_act * up_out).astype(bf16)
    both_ref[:, :TILE] = (
        grad_hidden * up_out * (gate_sig + gate_act * (1.0 - gate_sig))
    ).astype(bf16)
    both_ref[:, TILE:] = (grad_hidden * gate_act).astype(bf16)


def units_forward(rows, grads, units, buffers, index, pick=None):
    count, (length, width) = len(rows), rows[0].shape
    blocks = count if pick is None else 1
    steps = units.shape[1] // (3 * TILE)
    full = pl.BlockSpec((length, width), lambda i: (0, 0))
    kept = pl.BlockSpec((blocks * length, width), lambda i: (index, 0))
    held = () if buffers is None else buffers
    return pl.pallas_call(
        functools.partial(units_forward_kernel, count, pick is not None),
        grid=(steps,),
        in_specs=scalars(1)
        + [full] * (2 * count)
        + [
            pl.BlockSpec((width, 2 * TILE), lambda i: (0, i)),
            pl.BlockSpec((width, TILE), lambda i: (0, 2 * steps + i)),
        ]
        + [pl.BlockSpec(memory_space=pl.ANY)] * len(held),
        out_specs=(
            kept,
            kept,
            pl.BlockSpec((blocks * length, TILE), lambda i: (index, i)),
            pl.BlockSpec((blocks * length, 2 * TILE), lambda i: (index, i)),
        ),
        out_shape=(
            jax.ShapeDtypeStruct((4 * length, width), bf16),
            jax.ShapeDtypeStruct((4 * length, width), bf16),
            jax.ShapeDtypeStruct((4 * length, steps * TILE), bf16),
            jax.ShapeDtypeStruct((4 * length, steps * 2 * TILE), bf16),
        ),
        input_output_aliases={2 * count + 3 + k: k for k in range(len(held))},
        compiler_params=pltpu.CompilerParams(vmem_limit_bytes=VMEM_LIMIT),
        cost_estimate=SMALL,
    )(jnp.zeros((1,), jnp.int32) if pick is None else pick, *rows, *grads, units, units, *held)


def write_blocks(total, out_refs):
    rows = out_refs[0].shape[0]
    for k, ref in enumerate(out_refs):
        ref[...] = total[k * rows : (k + 1) * rows].astype(bf16)


def units_to_width_kernel(values_ref, units_ref, *out_refs):
    write_blocks(dot(values_ref[...], units_ref[...], 1, 1), out_refs)


def units_to_width(values, units, part, first, count, pieces=None):
    pieces = pieces or count
    width = units.shape[0]
    block, columns = values.shape[0] // 4, values.shape[1]
    length = block * count
    return pl.pallas_call(
        units_to_width_kernel,
        grid=(width // TILE,),
        in_specs=[
            pl.BlockSpec((length, columns), lambda i: (first // count, 0)),
            pl.BlockSpec((TILE, columns), lambda i: (i, part)),
        ],
        out_specs=(pl.BlockSpec((length // pieces, TILE), lambda i: (0, i)),) * pieces,
        out_shape=(jax.ShapeDtypeStruct((length // pieces, width), bf16),) * pieces,
        compiler_params=pltpu.CompilerParams(vmem_limit_bytes=VMEM_LIMIT),
        cost_estimate=SMALL,
    )(values, units)


def units_add_kernel(*refs):
    out_ref = refs[-1]
    begin = 0
    for kept_ref, other_ref in zip(refs[0:-1:2], refs[1:-1:2]):
        columns = kept_ref.shape[2]
        out_ref[0, :, begin : begin + columns] = (
            kept_ref[0].astype(f32) + other_ref[0].astype(f32)
        ).astype(bf16)
        begin += columns


def units_add(*values):
    pairs, rows, _ = values[0].shape
    columns = sum(value.shape[2] for value in values[::2])
    return pl.pallas_call(
        units_add_kernel,
        grid=(pairs,),
        in_specs=[
            pl.BlockSpec((1, rows, value.shape[2]), lambda i: (i, 0, 0)) for value in values
        ],
        out_specs=pl.BlockSpec((1, rows, columns), lambda i: (i, 0, 0)),
        out_shape=jax.ShapeDtypeStruct((pairs, rows, columns), bf16),
        compiler_params=pltpu.CompilerParams(vmem_limit_bytes=VMEM_LIMIT),
        cost_estimate=SMALL,
    )(*values)


def units_gradient_kernel(core_ref, left_ref, right_ref, kept_ref, given_ref, total_ref):
    total_ref[...] = dot(left_ref[...], right_ref[...], 0, 0)
    core = core_ref[0]
    pairs, rows, _ = kept_ref.shape
    for p in range(pairs):
        for c, ref in ((core, kept_ref), (1 - core, given_ref)):
            at_row = pl.multiple_of((2 * p + c) * rows, 16)
            ref[p] = total_ref[pl.ds(at_row, rows), :].astype(bf16)


def units_gradient_parts(left, right, core):
    length, width = left.shape
    columns = right.shape[1]
    count = lax.axis_size("dp")
    rows = width // count
    tile = 2 * TILE if columns % (2 * TILE) == 0 else TILE
    out = pl.BlockSpec((count // 2, rows, tile), lambda i, c: (0, 0, i))
    shape = jax.ShapeDtypeStruct((count // 2, rows, columns), bf16)
    return pl.pallas_call(
        units_gradient_kernel,
        grid_spec=pltpu.PrefetchScalarGridSpec(
            num_scalar_prefetch=1,
            grid=(columns // tile,),
            in_specs=[
                pl.BlockSpec((length, width), lambda i, c: (0, 0)),
                pl.BlockSpec((length, tile), lambda i, c: (0, i)),
            ],
            out_specs=(out, out),
            scratch_shapes=[pltpu.VMEM((width, tile), f32)],
        ),
        out_shape=(shape, shape),
        compiler_params=pltpu.CompilerParams(vmem_limit_bytes=VMEM_LIMIT),
        cost_estimate=SMALL,
    )(core[None], left, right)


def swap_core(value):
    count = lax.axis_size("dp")
    return lax.ppermute(value, "dp", [(i, i ^ 1) for i in range(count)])


def swap_near(value):
    return lax.ppermute(value, "tensor", [(0, 1), (1, 0), (2, 3), (3, 2)])


def swap_far(value):
    return lax.ppermute(value, "tensor", [(0, 2), (2, 0), (1, 3), (3, 1)])


def swap_middle(value):
    return lax.ppermute(value, "tensor", [(1, 2), (2, 1)])


def swap_opposite(value):
    return lax.ppermute(value, "tensor", [(i, 3 - i) for i in range(4)])


def to_ends(value):
    return lax.ppermute(value, "tensor", [(1, 0), (2, 3)])


def from_ends(value):
    return lax.ppermute(value, "tensor", [(0, 1), (3, 2)])


def device_of(pair, core, z):
    return (2 * pair + core) * 4 + z


def owner_swap(value):
    perm = []
    for p in range(lax.axis_size("dp") // 2):
        for z in range(4):
            own = z // 2
            perm.append((device_of(p, own, z), device_of(p, own, z ^ 1)))
            perm.append((device_of(p, 1 - own, z), device_of(p, own, z ^ 2)))
    return lax.ppermute(value, AXES, perm)


def guest_swap(value):
    perm = []
    for p in range(lax.axis_size("dp") // 2):
        for z in range(4):
            guest = 1 - z // 2
            perm.append((device_of(p, guest, z), device_of(p, guest, z ^ 1)))
    return lax.ppermute(value, AXES, perm)


def heads_scatter_near(mine, other, z):
    def term(index):
        return at(mine, index, 0).astype(f32) + at(other, index, 0).astype(f32)

    away = swap_near(term(z ^ 3).astype(bf16))
    return term(z), term(z ^ 2), swap_near(term(z ^ 1).astype(bf16)), away


def heads_scatter_end(home, far, own, core):
    kept = jnp.where(own, home, far.astype(f32))
    return kept, swap_core(jnp.where(own, far, home.astype(bf16)))


def both_halves(kept, given, core):
    given = given.astype(f32)
    return jnp.concatenate(
        [jnp.where(core == 0, kept, given), jnp.where(core == 0, given, kept)], axis=0
    )


def gather_dp(value):
    bit = 1
    while bit < lax.axis_size("dp"):
        other = swap_dp(value, bit)
        upper = (lax.axis_index("dp") & bit) != 0
        value = jnp.concatenate(
            [jnp.where(upper, other, value), jnp.where(upper, value, other)], axis=0
        )
        bit *= 2
    return value


def gather_tensor(value, bit):
    other = lax.ppermute(value, "tensor", [(i, i ^ bit) for i in range(4)])
    upper = (lax.axis_index("tensor") & bit) != 0
    return jnp.concatenate(
        [jnp.where(upper, other, value), jnp.where(upper, value, other)], axis=1
    )


def sum_dp(value, first, last):
    bit = first
    while bit < last:
        value = value + swap_dp(value, bit)
        bit *= 2
    return value


def pair_groups():
    count = lax.axis_size("dp")
    return [list(range(c, count, 2)) for c in range(2)]


def swap_dp(value, mask):
    count = lax.axis_size("dp")
    return lax.ppermute(value, "dp", [(i, i ^ mask) for i in range(count)])


def gather_pairs_begin(value):
    if lax.axis_size("dp") != 8:
        return (lax.all_gather(value, "dp", axis=0, tiled=True, axis_index_groups=pair_groups()),)
    return value, swap_dp(value, 2), swap_dp(value, 4)


def gather_pairs_end(parts):
    if len(parts) == 1:
        return parts, jnp.zeros((1,), jnp.int32)
    value, by_two, by_four = parts
    pair = lax.axis_index("dp") >> 1
    rows = value.shape[0]
    half = rows // 2
    low, high = swap_dp(by_four[:half], 2), swap_dp(by_two[half:], 4)
    begins = jnp.stack([pair, pair ^ 1, pair ^ 2, pair ^ 3, pair ^ 3]) * rows
    begins = begins + jnp.array([0, 0, 0, 0, half], jnp.int32)
    return (value, by_two, by_four, low, high), begins


def at(value, index, axis):
    return lax.dynamic_index_in_dim(value, index, axis, keepdims=False)


def add_low(left, right):
    return (left.astype(f32) + right.astype(f32)).astype(bf16)


def scatter_pairs_begin(pieces):
    if len(pieces) == 1:
        return (
            lax.psum_scatter(
                pieces[0], "dp", scatter_dimension=0, tiled=True, axis_index_groups=pair_groups()
            ),
        )
    keep_x, send_x, keep_y, send_y = pieces
    return keep_x, swap_dp(send_x, 2), keep_y, swap_dp(send_y, 4)


def scatter_pairs_middle(pair, parts):
    if len(parts) == 1:
        return parts
    return pieces_call(pieces_middle_kernel, pair, parts, 4)


def scatter_pairs_send(parts):
    if len(parts) == 1:
        return parts
    keep_one, send_one, keep_two, send_two = parts
    return keep_one, swap_dp(send_one, 4), keep_two, swap_dp(send_two, 2)


def scatter_pairs_end(core, parts):
    if len(parts) == 1:
        rows = parts[0].shape[0] // 2
        return at(parts[0].reshape(2, rows, -1), core, 0), at(
            parts[0].reshape(2, rows, -1), core ^ 1, 0
        )
    return pieces_call(pieces_end_kernel, core[None], parts, 2)


def heads_pair(shard, far, own, core):
    kept = jnp.where(own, shard, far)
    other = swap_core(jnp.where(own, far, shard))
    return jnp.concatenate(
        [jnp.where(core == 0, kept, other), jnp.where(core == 0, other, kept)], axis=0
    )


def units_gradient(summed):
    return lax.psum_scatter(
        summed.reshape(-1, summed.shape[-1]),
        "dp",
        scatter_dimension=0,
        tiled=True,
        axis_index_groups=pair_groups(),
    )


def together(*values):
    return lax.optimization_barrier(values)


def after(value, earlier):
    return lax.optimization_barrier((value, earlier))[0]


def shards(
    block_in,
    out_grad,
    positions,
    qkv_weight,
    qkv_first,
    qkv_second,
    out_weight,
    out_first,
    out_second,
    gate_up,
    gate_up_first,
    gate_up_second,
    down_weight,
    down_first,
    down_second,
    norm_gains,
    norm_gains_first,
    norm_gains_second,
):
    model_width = block_in.shape[1]
    z = lax.axis_index("tensor")
    core = lax.axis_index("dp") & 1
    own = core == z // 2
    place = jnp.where(own, z, z ^ 2)[None]
    pair = (lax.axis_index("dp") >> 1)[None]
    pair = jnp.concatenate([pair & 1, pair >> 1])

    units_columns = gate_up.shape[2]
    heads_own = jnp.concatenate([qkv_weight.astype(bf16), out_weight.astype(bf16).T], axis=1)
    heads_own, gains_own, positions = together(heads_own, norm_gains[None], positions)
    heads_far = swap_far(heads_own)
    gains_dp = gather_dp(gains_own)[:, None]
    gains_all = gather_tensor(gather_tensor(gains_dp, 1), 2).reshape(1, -1)
    inverse_in = lax.rsqrt(jnp.mean(block_in * block_in, axis=-1, keepdims=True) + eps_norm)
    scaled_in = block_in * inverse_in
    head_positions = jnp.where(own, positions, swap_core(positions))
    scaled_b, heads_own, heads_far, head_positions, units_shard, grad_own, gains_all = together(
        scaled_in.astype(bf16),
        heads_own,
        heads_far,
        head_positions,
        pack_units(after(gate_up, gains_dp), down_weight.T),
        after(out_grad, gains_dp).astype(bf16),
        gains_all,
    )

    scaled_first = owner_swap(scaled_b)
    heads_parts = gather_pairs_begin(heads_pair(heads_own, heads_far, own, core))
    tables = rope_tables(head_positions, HEAD_DIMENSION)
    length = head_positions.shape[0]
    start = jnp.maximum(jnp.arange(length, dtype=jnp.int32) - head_positions, 0)
    start = start.astype(f32)[None]
    gain_attn = gains_all[:, :model_width]
    gain_q = gains_all[0, model_width : model_width + HEAD_DIMENSION]
    gain_k = gains_all[0, model_width + HEAD_DIMENSION : model_width + 2 * HEAD_DIMENSION]
    kv_local = qkv_weight.shape[1] // ((QUERY_GROUP + 2) * HEAD_DIMENSION)
    head_gains = jnp.concatenate(
        ([gain_q] * QUERY_GROUP + [gain_k, jnp.ones_like(gain_k)]) * kv_local
    )[None]
    gain_ffn = gains_all[:, model_width + 2 * HEAD_DIMENSION :]
    (
        scaled_first,
        heads_parts,
        gain_attn,
        head_gains,
        gain_ffn,
        units_shard,
        tables,
        start,
        grad_own,
    ) = together(
        scaled_first,
        heads_parts,
        gain_attn,
        head_gains,
        gain_ffn,
        units_shard,
        tables,
        start,
        grad_own,
    )

    scaled_second = guest_swap(scaled_first)
    scaled_mine = jnp.where(own, scaled_b, scaled_first)
    scaled_other = swap_core(scaled_mine)
    heads_blocks, heads_begins = gather_pairs_end(heads_parts)
    half, quarter = grad_own.shape[0] // 2, grad_own.shape[0] // 4
    grad_far = swap_far(grad_own[:quarter])
    (
        heads_blocks,
        scaled_second,
        scaled_mine,
        scaled_other,
        units_shard,
        grad_own,
        grad_far,
    ) = together(
        heads_blocks,
        scaled_second,
        scaled_mine,
        scaled_other,
        units_shard,
        grad_own,
        grad_far,
    )

    units = lax.all_gather(units_shard, "dp", axis=0, tiled=True)
    grad_far_rest = swap_far(grad_own[quarter:])
    grad_near = swap_near(grad_own)
    scaled_next = jnp.where(own, scaled_first, scaled_second)
    scaled_parts = (scaled_mine, scaled_next, scaled_other, swap_core(scaled_next))
    w_heads, normed_all, projected, queries_b, keys_b, values_b, attended, lse = attention_forward(
        place, scaled_parts, heads_blocks, heads_begins, gain_attn, head_gains, tables, start
    )
    branch_mine, branch_other = attention_branch(core[None], attended, w_heads)
    branch_mine, branch_other, grad_far, grad_far_rest, grad_near, grad_own = together(
        branch_mine, branch_other, grad_far, grad_far_rest, grad_near, grad_own
    )
    grad_far = jnp.concatenate([grad_far, grad_far_rest], axis=0)
    branch_other = swap_core(branch_other)
    grad_middle_part = swap_middle(grad_own)
    branch_mine, branch_other, grad_far = together(branch_mine, branch_other, grad_far)
    home, term_far, near, away = heads_scatter_near(branch_mine, branch_other, z)
    away, term_far, grad_middle_part = together(away, term_far, grad_middle_part)
    far = swap_far((term_far + away.astype(f32)).astype(bf16))
    far, home, near = together(far, home, near)
    middle = block_in + both_halves(
        *heads_scatter_end(home + near.astype(f32), far, own, core), core
    )

    inverse_mid = lax.rsqrt(jnp.mean(middle * middle, axis=-1, keepdims=True) + eps_norm)
    scaled_mid = middle * inverse_mid
    rows_own = (scaled_mid * gain_ffn).astype(bf16)
    rows_far = swap_far(rows_own)
    rows_near = swap_near(rows_own)
    inner = (z == 1) | (z == 2)
    buffers = units_forward((rows_own,), (grad_own,), units, None, 2)
    rows_far, rows_near, rows_own, buffers = together(rows_far, rows_near, rows_own, buffers)
    grad_ends = to_ends(grad_far)
    rows_ends = to_ends(rows_far)
    rows_middle = swap_middle(rows_own)
    buffers = units_forward((rows_near, rows_far), (grad_near, grad_far), units, buffers, 0)
    rows_all, grad_all, hidden_b, dboth = buffers
    back_near, back_far = units_to_width(dboth, units, 0, 0, 2)
    rows_ends, rows_middle, grad_ends, back_near, back_far, buffers = together(
        rows_ends, rows_middle, grad_ends, back_near, back_far, buffers
    )
    from_far = swap_far(back_far)
    from_near = swap_near(back_near)
    rows_all, grad_all, hidden_b, dboth = units_forward(
        (rows_ends, rows_middle),
        (grad_ends, grad_middle_part),
        units,
        buffers,
        3,
        inner.astype(jnp.int32)[None],
    )
    back_own, back_last = units_to_width(dboth, units, 0, 2, 2)
    down_kept, down_given = units_gradient_parts(grad_all, hidden_b, core)
    (
        from_near,
        from_far,
        back_last,
        back_own,
        rows_all,
        hidden_b,
        dboth,
        down_kept,
        down_given,
    ) = together(
        from_near,
        from_far,
        back_last,
        back_own,
        rows_all,
        hidden_b,
        dboth,
        down_kept,
        down_given,
    )
    from_last = swap_opposite(back_last)
    down_last = units_to_width(hidden_b, units, 2, 3, 1, 2)
    branch_ends = [from_ends(part) for part in down_last]
    both_kept, both_given = units_gradient_parts(rows_all, dboth, core)
    from_last, branch_ends, down_kept, down_given, both_kept, both_given, down_last = together(
        from_last, branch_ends, down_kept, down_given, both_kept, both_given, down_last
    )
    grad_normed_two = (
        back_own.astype(f32)
        + from_near.astype(f32)
        + from_far.astype(f32)
        + from_last.astype(f32)
    )

    grad_gain_ffn = jnp.sum(grad_normed_two * scaled_mid, axis=0)
    weighted = grad_normed_two * gain_ffn
    grad_middle = out_grad + inverse_mid * (
        weighted - scaled_mid * jnp.mean(weighted * scaled_mid, axis=-1, keepdims=True)
    )
    grad_mid_b, grad_gain_ffn, hidden_b, down_kept, down_given, both_kept, both_given = together(
        grad_middle.astype(bf16),
        grad_gain_ffn,
        hidden_b,
        down_kept,
        down_given,
        both_kept,
        both_given,
    )
    grad_mid_first = owner_swap(grad_mid_b)
    units_sum = units_add(both_kept, swap_core(both_given), down_kept, swap_core(down_given))
    down_near, down_far, down_own = units_to_width(hidden_b, units, 2, 0, 3)
    down_far = add_low(down_far, jnp.concatenate(branch_ends, axis=0))
    grad_mid_first, units_sum, down_near, down_far, down_own = together(
        grad_mid_first, units_sum, down_near, down_far, down_own
    )
    units_sum = units_gradient(units_sum)
    grad_mid_second = guest_swap(grad_mid_first)
    branch_far = swap_far(down_far[: 3 * half // 4])
    grad_mid_mine = jnp.where(own, grad_mid_b, grad_mid_first)
    grad_mid_other = swap_core(grad_mid_mine)
    grad_mid_second, grad_mid_mine, grad_mid_other, branch_far, down_far = together(
        grad_mid_second, grad_mid_mine, grad_mid_other, branch_far, down_far
    )
    grad_mid_next = jnp.where(own, grad_mid_first, grad_mid_second)
    grad_mid_parts = (grad_mid_mine, grad_mid_next, grad_mid_other, swap_core(grad_mid_next))

    branch_far_rest = swap_far(down_far[3 * half // 4 :])
    branch_middle = swap_middle(jnp.concatenate(down_last, axis=0))
    grad_attended, row_dot, *out_pieces = attention_turn(
        place, pair, grad_mid_parts, w_heads, attended
    )
    branch_near = swap_near(after(down_near, row_dot))
    out_parts = scatter_pairs_begin(tuple(out_pieces))
    grad_projected, part_mine, part_other, head_sums, gain_sums = attention_backward(
        core[None],
        queries_b,
        keys_b,
        values_b,
        grad_attended,
        lse,
        row_dot,
        start,
        projected,
        head_gains,
        *tables,
        w_heads,
        normed_all,
        gain_attn,
    )
    (
        grad_projected,
        part_mine,
        part_other,
        branch_far,
        branch_far_rest,
        branch_near,
        branch_middle,
        out_parts,
    ) = together(
        grad_projected,
        part_mine,
        part_other,
        branch_far,
        branch_far_rest,
        branch_near,
        branch_middle,
        out_parts,
    )

    part_other = swap_core(part_other)
    qkv_pieces = heads_gradient(pair, normed_all, grad_projected)
    part_mine, part_other, qkv_pieces, out_parts, branch_far = together(
        part_mine, part_other, qkv_pieces, out_parts, branch_far
    )
    home, term_far, near, away = heads_scatter_near(part_mine, part_other, z)
    qkv_parts = scatter_pairs_begin(qkv_pieces)
    out_parts = scatter_pairs_middle(pair, out_parts)
    gain_sums, head_sums = after((gain_sums, head_sums), qkv_pieces)
    head_sums = head_sums.reshape(-1, QUERY_GROUP + 2, HEAD_DIMENSION)
    gain_total = jnp.concatenate(
        [
            gain_sums[0],
            jnp.sum(head_sums[:, :QUERY_GROUP], axis=(0, 1)),
            jnp.sum(head_sums[:, QUERY_GROUP], axis=0),
            grad_gain_ffn,
        ]
    )
    gain_total = sum_dp(gain_total, 1, 2)
    block_out = (
        middle
        + down_own.astype(f32)
        + branch_near.astype(f32)
        + branch_middle.astype(f32)
        + jnp.concatenate([branch_far, branch_far_rest], axis=0).astype(f32)
    )
    far_term = (term_far + away.astype(f32)).astype(bf16)
    far = swap_far(far_term)
    qkv_parts = scatter_pairs_middle(pair, after(qkv_parts, (far_term, gain_total, block_out)))
    out_parts = scatter_pairs_send(after(out_parts, qkv_parts))
    qkv_parts = scatter_pairs_send(qkv_parts)
    down_new = adam_units(
        down_weight.T[None],
        down_first.T[None],
        down_second.T[None],
        after(units_sum, (near, out_parts[0])),
        2 * units_sum.shape[1] // 3,
    )
    count = lax.axis_size("dp")
    gain_last = swap_dp(after(gain_total, down_new), 2)
    qkv_kept, qkv_given = scatter_pairs_end(core, after(qkv_parts, (down_new, far)))
    gain_total = sum_dp(gain_total + after(gain_last, qkv_kept), 4, count // 2)
    gain_last = swap_dp(gain_total, count // 2)
    out_kept, out_given = scatter_pairs_end(core, after(out_parts, qkv_kept))
    qkv_other, out_other = swap_core(qkv_given), swap_core(out_given)
    gain_total = gain_total + after(gain_last, out_kept)
    gain_last = swap_near(gain_total)
    heads_away = jnp.concatenate(
        [jnp.where(own, qkv_other, qkv_kept), jnp.where(own, out_other, out_kept)], axis=1
    )
    kept, given = heads_scatter_end(home + near.astype(f32), far, own, core)
    units_sum = after(units_sum, heads_away)
    gain_total = gain_total + after(gain_last, heads_away)
    gain_last = swap_far(gain_total)
    heads_away = swap_far(heads_away)
    in_grad = input_gradient(core[None], kept, given, block_in, gain_attn, grad_middle)
    gate_up_new = adam_units(gate_up, gate_up_first, gate_up_second, units_sum, 0)
    gain_total = gain_total + after(gain_last, gate_up_new)
    heads_away, in_grad, gate_up_new = together(heads_away, in_grad, gate_up_new)
    down_new = tuple(value[0].T for value in down_new)
    qkv_columns = qkv_weight.shape[1]
    sum_qkv = jnp.where(own, qkv_kept, qkv_other).astype(f32) + heads_away[
        :, :qkv_columns
    ].astype(f32)
    sum_out = jnp.where(own, out_kept, out_other).astype(f32) + heads_away[
        :, qkv_columns:
    ].astype(f32)
    sum_out = sum_out.T
    gain_count = norm_gains.shape[0]
    gain_at = (lax.axis_index("dp") * 4 + z) * gain_count
    gain_grads = lax.dynamic_slice_in_dim(gain_total, gain_at, gain_count)

    qkv_new = adam_step(qkv_weight, qkv_first, qkv_second, sum_qkv, rate_matrix, decay_matrix)
    out_new = adam_step(out_weight, out_first, out_second, sum_out, rate_output, decay_matrix)
    gains_new = adam_step(
        norm_gains, norm_gains_first, norm_gains_second, gain_grads, rate_gains, 0.0
    )
    return (block_out, in_grad, *qkv_new, *out_new, *gate_up_new, *down_new, *gains_new)


def solution(mesh):
    tokens = P(("dp", "tensor"), None)
    by_rows = (P("dp", "tensor"),) * 3
    by_columns = (P("tensor", "dp"),) * 3
    stacked = (P(None, "dp", "tensor"),) * 3
    gains = (P(("dp", "tensor")),) * 3
    states = by_rows + by_columns + stacked + by_columns + gains
    return jax.shard_map(
        shards,
        mesh=mesh,
        in_specs=(tokens, tokens, P("dp")) + states,
        out_specs=(tokens, tokens) + states,
        check_vma=False,
    )
```
